128 devices in a mesh: dp: 4 (over y), ctx: 32 (over x, z, core).
Axes of the slice: x: 4, y: 4, z: 4, core: 2. Of those that a mesh axis runs over, the one named last changes fastest.
Arguments:
- tokens: bfloat16 [16384, 576], P(('dp', 'ctx')), may hold values from -6 to 6
- out_grad: bfloat16 [16384, 576], P(('dp', 'ctx')), may hold values from -6 to 6
- w_query: bfloat16 [2, 576, 576], P(None, 'dp'), may hold values from -0.25 to 0.25
- w_key: bfloat16 [2, 576, 192], P(None, 'dp'), may hold values from -0.25 to 0.25
- w_value: bfloat16 [2, 576, 192], P(None, 'dp'), may hold values from -0.25 to 0.25
- w_out: bfloat16 [2, 576, 576], P(None, 'dp'), may hold values from -2 to 2
- w_gate: bfloat16 [2, 576, 1536], P(None, 'dp'), may hold values from -0.25 to 0.25
- w_up: bfloat16 [2, 576, 1536], P(None, 'dp'), may hold values from -0.25 to 0.25
- w_down: bfloat16 [2, 1536, 576], P(None, 'dp'), may hold values from -0.15625 to 0.15625
- attn_gain: bfloat16 [2, 576], P(None, 'dp'), may hold values from 0.5 to 1.5
- ffn_gain: bfloat16 [2, 576], P(None, 'dp'), may hold values from 0.5 to 1.5
- block_pairs: int32 [32], replicated, may hold values from 0 to 31, each once
Outputs:
- out: bfloat16 [16384, 576], P(('dp', 'ctx'))
- tokens_grad: float32 [16384, 576], P(('dp', 'ctx'))
- grad_query: float32 [2, 576, 576], P(None, 'dp')
- grad_key: float32 [2, 576, 192], P(None, 'dp')
- grad_value: float32 [2, 576, 192], P(None, 'dp')
- grad_out: float32 [2, 576, 576], P(None, 'dp')
- grad_gate: float32 [2, 576, 1536], P(None, 'dp')
- grad_up: float32 [2, 576, 1536], P(None, 'dp')
- grad_down: float32 [2, 1536, 576], P(None, 'dp')
- grad_attn_gain: float32 [2, 576], P(None, 'dp')
- grad_ffn_gain: float32 [2, 576], P(None, 'dp')
The draws below stay inside these ranges and needn't reach their ends.
Inputs may be any that keep to these rules, and one draw needn't show every extreme that they name: A permutation of the ctx indices; ctx index c holds blocks block_pairs[c] and 63 - block_pairs[c] of each of its sequences.
All inputs are finite; a program needn't handle non-finite values.
Results may differ from the reference program's by a relative error of at most 0.03.
Values may be sent and summed in bfloat16 or wider, within the bound.
A program may use at most 128 MiB of HBM per device.

```python
import jax
import jax.numpy as jnp
from jax import lax

D = 576
HEADS = 9
KV_HEADS = 3
HEAD_DIM = 64
FF = 1536
LAYERS = 2
TOK_DEV = 128
SEQ = 4096
TOKENS = 16384
N_DP = 4
N_CTX = 32


def shard_levels(rng, extent, pieces, least, high):
    def one(dim, shards_of):
        steps = jax.random.uniform(jax.random.fold_in(jax.random.fold_in(rng, 6), dim), (shards_of,), jnp.float32, least / len(pieces), high / len(pieces))
        return jnp.repeat(jnp.exp(steps), extent[dim] // shards_of).reshape((-1,) + (1,) * (len(extent) - dim - 1))

    gain = one(*pieces[0])
    for cut in pieces[1:]:
        gain = gain * one(*cut)
    return gain


def gaussian(rng, extent, scale, limit, split=(), held_as=jnp.bfloat16):
    loudness = shard_levels(rng, extent, split, -0.22, 0.18) if split else 1.0
    values = jax.random.normal(rng, extent, jnp.float32) * scale * loudness
    return jnp.minimum(jnp.maximum(values, -limit), limit).astype(held_as)


def setup_inputs(seed: int = 0) -> dict:
    streams_of = jax.random.split(jax.random.key(seed), 13)
    return {
        "tokens": gaussian(streams_of[0], (TOKENS, D), 1.0, 6.0, ((0, 128),)),
        "out_grad": gaussian(streams_of[1], (TOKENS, D), 1.0, 6.0, ((0, 128),)),
        "w_query": gaussian(streams_of[2], (LAYERS, D, D), D ** -0.5, 0.25, ((1, 4),)),
        "w_key": gaussian(streams_of[3], (LAYERS, D, KV_HEADS * HEAD_DIM), D ** -0.5, 0.25, ((1, 4),)),
        "w_value": gaussian(streams_of[4], (LAYERS, D, KV_HEADS * HEAD_DIM), D ** -0.5, 0.25, ((1, 4),)),
        "w_out": gaussian(streams_of[5], (LAYERS, D, D), (D // 64) ** -0.5, 2.0, ((1, 4),)),
        "w_gate": gaussian(streams_of[6], (LAYERS, D, FF), D ** -0.5, 0.25, ((1, 4),)),
        "w_up": gaussian(streams_of[7], (LAYERS, D, FF), D ** -0.5, 0.25, ((1, 4),)),
        "w_down": gaussian(streams_of[8], (LAYERS, FF, D), FF ** -0.5, 0.15625, ((1, 4),)),
        "attn_gain": jnp.clip(1.0 + 0.1 * jax.random.normal(streams_of[9], (LAYERS, D), jnp.float32), 0.5, 1.5).astype(jnp.bfloat16),
        "ffn_gain": jnp.clip(1.0 + 0.1 * jax.random.normal(streams_of[10], (LAYERS, D), jnp.float32), 0.5, 1.5).astype(jnp.bfloat16),
        "block_pairs": jax.random.permutation(streams_of[11], N_CTX).astype(jnp.int32),
    }


NORM_EPS = 1e-05
ROPE_BASE = 100000.0
NEG_BIG = -1e+30
HIGH_PREC = lax.Precision.HIGHEST

@jax.custom_vjp
def low(v):
    return lax.optimization_barrier(v.astype(jnp.bfloat16)).astype(jnp.float32)

@jax.custom_vjp
def low_back(v):
    return v

def low_keep(v):
    return (low(v), None)

def low_pass(kept, grad):
    return (grad,)

def back_keep(v):
    return (v, None)

def back_low(kept, grad):
    return (low(grad),)
low.defvjp(low_keep, low_pass)
low_back.defvjp(back_keep, back_low)

def matmul(left, right):
    return jnp.dot(left, right, precision=HIGH_PREC, preferred_element_type=jnp.float32)

def rms_norm(hidden, gain_vec):
    inv_rms = lax.rsqrt(lax.optimization_barrier(jnp.mean(hidden * hidden, axis=-1, keepdims=True)) + NORM_EPS)
    return hidden * inv_rms * gain_vec

def rope_tables(positions, head_width):
    half_width = head_width // 2
    frequency = ROPE_BASE ** (-2.0 * jnp.arange(half_width, dtype=jnp.float32) / head_width)
    angles = positions.astype(jnp.float32)[:, None] * frequency[None, :]
    angles = jnp.concatenate([angles, angles], axis=1)
    return (jnp.cos(angles), jnp.sin(angles))

def rotate(heads_in, cosine_table, sine_table):
    half_width = heads_in.shape[-1] // 2
    turned = jnp.concatenate([-heads_in[..., half_width:], heads_in[..., :half_width]], axis=-1)
    return heads_in * cosine_table[:, None, :] + turned * sine_table[:, None, :]

def attend(queries, key_rows, value_rows):
    seq_len = queries.shape[0]
    q_block_len = min(512, seq_len)
    q_blocks = seq_len // q_block_len
    key_pos = jnp.arange(seq_len, dtype=jnp.int32)

    def one_block(inputs):
        q_block, start = inputs
        scores = low_back(jnp.einsum('tkgd,skd->kgts', q_block, key_rows, precision=HIGH_PREC))
        query_pos = start + jnp.arange(q_block_len, dtype=jnp.int32)
        visible = key_pos[None, None, None, :] <= query_pos[None, None, :, None]
        scores = jnp.where(visible, scores, NEG_BIG)
        attn_probs = low(jax.nn.softmax(scores, axis=-1))
        return jnp.einsum('kgts,skd->tkgd', attn_probs, value_rows, precision=HIGH_PREC)
    shaped = queries.reshape((q_blocks, q_block_len) + queries.shape[1:])
    starts = jnp.arange(q_blocks, dtype=jnp.int32) * q_block_len
    result = lax.map(jax.checkpoint(one_block), (shaped, starts))
    return result.reshape(seq_len, HEADS * HEAD_DIM)

def one_layer(hidden, params, cosine_table, sine_table):
    query_w, key_w, value_w, out_w, gate_w, up_w, down_w, gain_attn, gain_ffn = params
    seq_len = hidden.shape[0]
    group_size = HEADS // KV_HEADS
    normed = low(rms_norm(hidden, gain_attn))
    q_raw = low_back(matmul(normed, query_w)).reshape(seq_len, HEADS, HEAD_DIM)
    k_raw = low_back(matmul(normed, key_w)).reshape(seq_len, KV_HEADS, HEAD_DIM)
    value_rows = low_back(low(matmul(normed, value_w))).reshape(seq_len, KV_HEADS, HEAD_DIM)
    queries = low(rotate(q_raw, cosine_table, sine_table) * 0.125).reshape(seq_len, KV_HEADS, group_size, HEAD_DIM)
    key_rows = low(rotate(k_raw, cosine_table, sine_table))
    attn = low_back(low(attend(queries, key_rows, value_rows)))
    mid_hidden = hidden + low_back(matmul(attn, out_w))
    normed_ffn = low(rms_norm(mid_hidden, gain_ffn))
    gate = low_back(matmul(normed_ffn, gate_w))
    up_proj = low_back(matmul(normed_ffn, up_w))
    inner = low(jax.nn.silu(gate) * up_proj)
    return mid_hidden + low_back(matmul(inner, down_w))

def forward(hidden, params, cosine_table, sine_table):
    for layer_idx in range(LAYERS):
        layer_params = tuple((item[layer_idx] for item in params))
        hidden = one_layer(hidden, layer_params, cosine_table, sine_table)
    return hidden

def reference(tokens, out_grad, w_query, w_key, w_value, w_out, w_gate, w_up, w_down, attn_gain, ffn_gain, block_pairs):
    half_rows = TOK_DEV // 2
    slot_block = jnp.stack([block_pairs, 2 * N_CTX - 1 - block_pairs], axis=1).reshape(-1).astype(jnp.int32)
    params = (w_query.astype(jnp.float32), w_key.astype(jnp.float32), w_value.astype(jnp.float32), w_out.astype(jnp.float32), w_gate.astype(jnp.float32), w_up.astype(jnp.float32), w_down.astype(jnp.float32), attn_gain.astype(jnp.float32), ffn_gain.astype(jnp.float32))
    positions = jnp.arange(SEQ, dtype=jnp.int32)
    cosine_table, sine_table = rope_tables(positions, HEAD_DIM)

    def to_natural(rows_in):
        slots = rows_in.reshape(2 * N_CTX, half_rows, D)
        return jnp.zeros_like(slots).at[slot_block].set(slots).reshape(SEQ, D)

    def to_slots(rows_in):
        return rows_in.reshape(2 * N_CTX, half_rows, D)[slot_block].reshape(SEQ, D)

    def one_sequence(grad_total, inputs):
        seq_tokens, seq_grad = inputs
        result, pull_back = jax.vjp(lambda tok_in, par_in: forward(tok_in, par_in, cosine_table, sine_table), to_natural(seq_tokens), params)
        d_tokens, d_params = pull_back(to_natural(seq_grad))
        grad_total = jax.tree.map(jnp.add, grad_total, d_params)
        return (grad_total, (to_slots(result), to_slots(d_tokens)))
    zero_grads = jax.tree.map(jnp.zeros_like, params)
    grads, (outputs, d_tokens) = lax.scan(one_sequence, zero_grads, (tokens.astype(jnp.float32).reshape(N_DP, SEQ, D), out_grad.astype(jnp.float32).reshape(N_DP, SEQ, D)))
    return (outputs.reshape(TOKENS, D).astype(jnp.bfloat16), d_tokens.reshape(TOKENS, D), grads[0], grads[1], grads[2], grads[3], grads[4], grads[5], grads[6], grads[7], grads[8])
```

```python
import functools

import jax
import jax.numpy as jnp
from jax import lax
from jax.experimental import pallas as pl
from jax.experimental.pallas import tpu as pltpu
from jax.sharding import PartitionSpec as P

HEADS = 9
KV = 3
HD = 64
LAYERS = 2
D = 576
FF = 1536
NX = 4
NZ = 4
NY = 4
NORM_EPS = 1e-05
ROPE_BASE = 100000.0
NEG = -1e30
BIG = 1e30
MESH = pl.DeviceIdType.MESH
ALL = slice(None)
F32 = jnp.float32
BF = jnp.bfloat16
VMEM_LIMIT = 60 * 1024 * 1024


def place():
    ctx = lax.axis_index("ctx")
    return lax.div(ctx, 8), lax.rem(lax.div(ctx, 2), 4), lax.rem(ctx, 2)


def ctx_of(x, z, c):
    return (x * NZ + z) * 2 + c


def turn(i, d):
    return lax.rem(i + (d + 4), 4)


def neighbour(axis, d):
    x, z, c = place()
    return ctx_of(turn(x, d), z, c) if axis == 0 else ctx_of(x, turn(z, d), c)


def other_core():
    x, z, c = place()
    return ctx_of(x, z, 1 - c)


def greet(dp_too):
    barrier = pltpu.get_barrier_semaphore()
    ids = [neighbour(0, 1), neighbour(0, -1), neighbour(1, 1), neighbour(1, -1), other_core()]
    for i in ids:
        pl.semaphore_signal(barrier, inc=1, device_id={"ctx": i}, device_id_type=MESH)
    count = len(ids)
    if dp_too:
        y = lax.axis_index("dp")
        for k in (1, 2, 3):
            pl.semaphore_signal(barrier, inc=1, device_id={"dp": turn(y, k)}, device_id_type=MESH)
        count += 3
    pl.semaphore_wait(barrier, count)


class Wire:
    def __init__(self, send, recv):
        self.send, self.recv, self.open = send, recv, []

    def desc(self, src, dst, k, dev):
        return pltpu.make_async_remote_copy(
            src_ref=src,
            dst_ref=dst,
            send_sem=self.send.at[k],
            recv_sem=self.recv.at[k],
            device_id=dev,
            device_id_type=MESH,
        )

    def go(self, src, dst, k, dev):
        copy = self.desc(src, dst, k, dev)
        copy.start()
        self.open.append(copy)

    def got(self, dst, k, dev):
        self.desc(dst, dst, k, dev).wait_recv()

    def close(self):
        for copy in self.open:
            copy.wait_send()
        self.open = []


def run_all(gens):
    gens = list(gens)
    while gens:
        left = []
        for g in gens:
            try:
                next(g)
                left.append(g)
            except StopIteration:
                pass
        gens = left


def gather_half(wire, base, h, view, core_too):
    x, z, c = place()
    axes = (0, 1) if h == 0 else (1, 0)
    pos = (x, z) if h == 0 else (z, x)
    oth = {"ctx": other_core()}
    for stage in (0, 1):
        axis, me = axes[stage], pos[stage]
        right, left = {"ctx": neighbour(axis, 1)}, {"ctx": neighbour(axis, -1)}
        b = base + 4 * stage

        def at(i, part):
            return view(i, pos[1], part, c) if stage == 0 else view(ALL, i, part, c)

        def share(i, k):
            if stage == 1 and core_too:
                wire.go(at(i, None), at(i, None), base + 8 + k, oth)

        wire.go(at(me, None), at(me, None), b, right)
        wire.go(at(me, None), at(me, None), b + 1, left)
        share(me, 0)
        yield
        wire.got(at(turn(me, -1), None), b, left)
        wire.go(at(turn(me, -1), 0), at(turn(me, -1), 0), b + 2, right)
        share(turn(me, -1), 1)
        yield
        wire.got(at(turn(me, 1), None), b + 1, right)
        wire.go(at(turn(me, 1), 1), at(turn(me, 1), 1), b + 3, left)
        share(turn(me, 1), 2)
        yield
        wire.got(at(turn(me, 2), 0), b + 2, left)
        wire.got(at(turn(me, 2), 1), b + 3, right)
        share(turn(me, 2), 3)
        yield
    if core_too:
        me = pos[1]
        for k, d in enumerate((0, -1, 1, 2)):
            wire.got(view(ALL, turn(me, d), None, 1 - c), base + 8 + k, oth)


def add_into(dst, *srcs):
    if len(dst.shape) > 2:

        def step(i, carry):
            add_into(dst.at[i], *[s.at[i] for s in srcs])
            return carry

        if len(dst.shape) == 3:
            for i in range(dst.shape[0]):
                step(i, 0)
        else:
            lax.fori_loop(0, dst.shape[0], step, 0)
        return
    total = dst[...].astype(F32)
    for s in srcs:
        total = total + s[...].astype(F32)
    dst[...] = total.astype(dst.dtype)


def scatter_half(wire, base, h, view, core_src, core_dst, slots):
    x, z, c = place()
    axes = (1, 0) if h == 0 else (0, 1)
    pos = (z, x) if h == 0 else (x, z)
    oth = {"ctx": other_core()}
    order = (2, 1, -1, 0)
    if core_src is not None:
        for k, d in enumerate(order):
            f = turn(pos[0], d)
            wire.go(core_src(f), core_dst(f), base + k, oth)
        yield

    def core_sum(k):
        f = turn(pos[0], order[k])
        wire.got(core_dst(f), base + k, oth)
        add_into(view(f, ALL, None), core_dst(f))

    for stage in (0, 1):
        axis, me = axes[stage], pos[stage]
        right, left = {"ctx": neighbour(axis, 1)}, {"ctx": neighbour(axis, -1)}
        b = base + 4 + 4 * stage
        one_a, one_b, two_a, two_b = slots[stage]

        def at(i, part):
            return view(i, ALL, part) if stage == 0 else view(pos[0], i, part)

        if stage == 0:
            core_sum(0)
        wire.go(at(turn(me, 2), 0), one_a, b, right)
        wire.go(at(turn(me, 2), 1), one_b, b + 1, left)
        yield
        if stage == 0:
            core_sum(1)
            core_sum(2)
        wire.got(one_a, b, left)
        add_into(at(turn(me, 1), 0), one_a)
        wire.go(at(turn(me, 1), None), two_a, b + 2, right)
        yield
        wire.got(one_b, b + 1, right)
        add_into(at(turn(me, -1), 1), one_b)
        wire.go(at(turn(me, -1), None), two_b, b + 3, left)
        yield
        if stage == 0:
            core_sum(3)
        wire.got(two_a, b + 2, left)
        wire.got(two_b, b + 3, right)
        add_into(at(me, None), two_a, two_b)
        yield


def lanes(shape):
    return lax.broadcasted_iota(jnp.int32, shape, len(shape) - 1)


def mm(a, b):
    return lax.dot_general(a, b, (((1,), (0,)), ((), ())), preferred_element_type=F32)


def mm_t(a, b):
    return lax.dot_general(a, b, (((1,), (1,)), ((), ())), preferred_element_type=F32)


def tmm(a, b):
    return lax.dot_general(a, b, (((0,), (0,)), ((), ())), preferred_element_type=F32)


def inv_rms(v):
    return lax.rsqrt(jnp.mean(v * v, axis=-1, keepdims=True) + NORM_EPS)


def norm_back(v, g, d):
    r = inv_rms(v)
    dv = r * g * d - v * (r * r * r * jnp.mean(g * d * v, axis=-1, keepdims=True))
    return dv, jnp.sum(d * v * r, axis=0, keepdims=True)


def rope(t, cos, ssin):
    first = lax.rem(lanes(t.shape), HD) < HD // 2
    turned = jnp.where(first, pltpu.roll(t, 96, 1), pltpu.roll(t, 32, 1))
    return t * cos + turned * ssin


def pair(t, half):
    lo, hi = t[:64], t[64:]
    first = lanes((64, 128)) < HD
    if half == 0:
        return jnp.where(first, lo, pltpu.roll(hi, HD, 1))
    return jnp.where(first, pltpu.roll(lo, HD, 1), hi)


def unpair(a, b):
    first = lanes((64, 128)) < HD
    lo = jnp.where(first, a, pltpu.roll(b, HD, 1))
    hi = jnp.where(first, pltpu.roll(a, HD, 1), b)
    return jnp.concatenate([lo, hi], axis=0)


def tile(v, i):
    return v[:, 128 * i : 128 * i + 128]


def doubled(p):
    first = lanes((192, 128)) < HD
    one = jnp.where(first, pltpu.roll(p, HD, 1), 0.0)
    zero = jnp.zeros((192, 128), F32)
    return jnp.concatenate(
        [jnp.concatenate([one, zero], axis=1), jnp.concatenate([zero, p], axis=1)], axis=0
    ).astype(BF)


def slot_row(scal, c, row_a, row_b):
    pick = jnp.full((1, 384), scal[2, c], F32) > 0.5
    own = jnp.full((1, 384), scal[3, c], F32)
    extra = jnp.where(lanes((1, 384)) >= 192, own, 0.0)
    return jnp.where(pick, row_a, row_b), extra


def w_mat(wv, kind, i):
    return wv[kind, i].reshape(D, 384)


def w_down(wv, i):
    return wv[3, :, i].reshape(D, 384)


def load_weights(w_any, layer, wv, sems):
    return [
        pltpu.make_async_copy(w_any.at[layer, k], wv.at[k], sems.at[k]) for k in range(4)
    ]


def chunk_of(buf, ci, i):
    return buf[ci // 2, pl.ds(2 * (ci % 2), 2), :, i].reshape(256, 128)


def diag_keys(k):
    first = lanes((64, 128)) < HD
    zero = jnp.zeros((64, 128), k.dtype)
    both = jnp.concatenate([jnp.where(first, k, zero), jnp.where(first, zero, k)], axis=0)
    return both


def diag_bias():
    shape = (128, 384)
    key = lax.rem(lax.broadcasted_iota(jnp.int32, shape, 0), 64)
    q = lanes(shape)
    visible = (q >= 192) & (key <= lax.rem(q, 64))
    return jnp.where(visible, 0.0, NEG)


def weights_kernel(win, gin, w_out, g_out, send, recv, loc):
    x, z, c = place()
    y = lax.axis_index("dp")
    greet(True)
    wire = Wire(send, recv)
    own = pltpu.make_async_copy(win.at[c, x, z], w_out.at[c, x, z, y], loc.at[0])
    own.start()
    gown = pltpu.make_async_copy(gin, g_out.at[y], loc.at[1])
    gown.start()
    for k in (1, 2, 3):
        dev = {"dp": turn(y, k)}
        wire.go(win.at[c, x, z], w_out.at[c, x, z, y], 24 + k, dev)
        wire.go(gin, g_out.at[y], 28 + k, dev)
    own.wait()
    gown.wait()
    for k in (1, 2, 3):
        dev = {"dp": turn(y, k)}
        wire.got(w_out.at[c, x, z, turn(y, -k)], 24 + k, dev)
        wire.got(g_out.at[turn(y, -k)], 28 + k, dev)

    rows = {None: pl.ds(0, 144), 0: pl.ds(0, 64), 1: pl.ds(64, 80)}

    def view_of(h):
        def view(first, second, part, core):
            xi, zi = (first, second) if h == 0 else (second, first)
            return w_out.at[core, xi, zi, pl.ds(2 * h, 2), rows[part]]

        return view

    run_all([gather_half(wire, 12 * h, h, view_of(h), True) for h in (0, 1)])
    wire.close()


def gather_weights(win, gin):
    any_spec = pl.BlockSpec(memory_space=pl.ANY)
    return pl.pallas_call(
        weights_kernel,
        out_shape=(
            jax.ShapeDtypeStruct((LAYERS, NX, NZ, NY, 144, 384), BF),
            jax.ShapeDtypeStruct((NY, 16, 256), BF),
        ),
        in_specs=[any_spec, any_spec],
        out_specs=(any_spec, any_spec),
        scratch_shapes=[
            pltpu.SemaphoreType.DMA((32,)),
            pltpu.SemaphoreType.DMA((32,)),
            pltpu.SemaphoreType.DMA((2,)),
        ],
        compiler_params=pltpu.CompilerParams(
            collective_id=0, has_side_effects=True, vmem_limit_bytes=VMEM_LIMIT
        ),
        name="gather_weights",
    )(win, gin)


def forward_kernel(
    layer, h_ref, w_any, gains, cos_ref, sin_ref, mask_ref, ind_ref, scal,
    next_ref, mid_ref, attn_ref, qt_ref, kv, lse_ref, op_ref,
    wv, s_scr, sd_scr, acc_scr, wide, send, recv, loc,
):
    x, z, c = place()
    loads = load_weights(w_any, layer, wv, loc)
    for k in (2, 0, 1, 3):
        loads[k].start()
    greet(False)
    h = h_ref[...]
    n1 = (h * inv_rms(h) * gains[0:1]).astype(BF)
    loads[2].wait()
    qkv = [mm(n1, w_mat(wv, 2, i)) for i in range(3)]
    tiles = [tile(qkv[i // 3], i % 3) for i in range(8)]
    cos, ssin = cos_ref[...], sin_ref[...]
    tiles[:6] = [rope(t, cos, ssin) for t in tiles[:6]]
    k_pairs = [pair(tiles[4], 1), pair(tiles[5], 0), pair(tiles[5], 1)]
    v_pairs = [pair(tiles[6], 0), pair(tiles[6], 1), pair(tiles[7], 0)]
    for i, p in enumerate(k_pairs + v_pairs):
        kv[x, z, c, i] = p.astype(BF)

    wire = Wire(send, recv)
    rows = {None: pl.ds(0, 64), 0: pl.ds(0, 32), 1: pl.ds(32, 32)}

    def view_of(hf):
        def view(first, second, part, core):
            xi, zi = (first, second) if hf == 0 else (second, first)
            return kv.at[xi, zi, core, pl.ds(3 * hf, 3), rows[part]]

        return view

    gens = [gather_half(wire, 12 * hf, hf, view_of(hf), True) for hf in (0, 1)]
    for g in gens:
        next(g)
    for k in range(KV):
        qp = jnp.concatenate(
            [pair(tiles[(3 * k + g) // 2], (3 * k + g) % 2) for g in range(3)], axis=0
        )
        qt_ref[k] = doubled(qp * 0.125)
    run_all(gens)
    wire.close()

    lane = lanes((1, 384))
    in_one = lane < 192
    bias = diag_bias()
    zero128 = jnp.zeros((128, 128), BF)
    own = [kv[x, z, c, i] for i in range(6)]
    runs = []
    for k in range(KV):
        sd = mm_t(jnp.concatenate([zero128, diag_keys(own[k])], axis=1), qt_ref[k]) + bias
        sd_scr[k] = sd
        lo = jnp.max(sd[:64].reshape(8, 8, 384), axis=0)
        hi = jnp.max(sd[64:].reshape(8, 8, 384), axis=0)
        runs += [jnp.full((8, 384), NEG, F32), lo, hi]

    def scores(ci, carry):
        carry = list(carry)
        m = mask_ref[ci]
        for k in range(KV):
            keys = chunk_of(kv, ci, k)
            s = mm_t(jnp.concatenate([keys, keys * m], axis=1), qt_ref[k])
            s_scr[k, ci] = s
            for i in range(4):
                top = jnp.max(s[64 * i : 64 * i + 64].reshape(8, 8, 384), axis=0)
                slot = 4 * ci + i
                carry[3 * k] = jnp.maximum(carry[3 * k], top)
                carry[3 * k + 1] = jnp.maximum(carry[3 * k + 1], top + scal[0, slot])
                carry[3 * k + 2] = jnp.maximum(carry[3 * k + 2], top + scal[1, slot])
        return tuple(carry)

    runs = lax.fori_loop(0, 8, scores, tuple(runs))
    row_a, row_b = [], []
    for k in range(KV):
        one, lo, hi = [jnp.max(r, axis=0, keepdims=True) for r in runs[3 * k : 3 * k + 3]]
        top = jnp.where(in_one, one, hi)
        top = jnp.maximum(top, pltpu.roll(top, 192, 1))
        row_a.append(jnp.where(in_one, top, lo))
        row_b.append(top)

    dlane = lanes((128, 128))
    drow = lax.broadcasted_iota(jnp.int32, (128, 128), 0)
    dind = jnp.where(
        ((dlane == 65) & (drow < 64)) | ((dlane == 66) & (drow >= 64)), 1.0, 0.0
    ).astype(BF)
    for k in range(KV):
        sd = sd_scr[k]
        p = jnp.concatenate([jnp.exp(sd[:64] - row_a[k]), jnp.exp(sd[64:] - row_b[k])], axis=0)
        vals = jnp.concatenate([dind, diag_keys(own[3 + k])], axis=1)
        acc_scr[k] = tmm(vals, p.astype(BF))

    def values(ci, carry):
        m, ind = mask_ref[ci], ind_ref[ci]
        first = lanes((256, 128)) < HD
        for k in range(KV):
            s = s_scr[k, ci]
            parts = []
            for i in range(4):
                base, extra = slot_row(scal, 4 * ci + i, row_a[k], row_b[k])
                parts.append(jnp.exp(s[64 * i : 64 * i + 64] - (base + extra)))
            p = jnp.concatenate(parts, axis=0).astype(BF)
            v = chunk_of(kv, ci, 3 + k)
            vals = jnp.concatenate([jnp.where(first, v, ind), v * m], axis=1)
            acc_scr[k] += tmm(vals, p)
        return carry

    lax.fori_loop(0, 8, values, 0)

    pairs = []
    for k in range(KV):
        acc = acc_scr[k]
        rolled = pltpu.roll(acc, 192, 1)
        hi = acc[0:64] + rolled[192:256]
        lo = rolled[128:192]
        tot_hi = acc[64:65] + rolled[66:67]
        tot_lo = rolled[65:66]
        lse_hi = row_b[k] + jnp.log(jnp.where(in_one, tot_hi, 1.0))
        lse_hi = jnp.where(in_one, lse_hi, pltpu.roll(lse_hi, 192, 1))
        lse_lo = pltpu.roll(row_a[k], 192, 1) + jnp.log(jnp.where(in_one, tot_lo, 1.0))
        lse_ref[k, 0:1] = jnp.where(in_one, lse_hi, pltpu.roll(lse_lo, 192, 1))
        lse_ref[k, 1:2] = lse_hi
        lse_ref[k, 2:8] = jnp.zeros((6, 384), F32)
        out_t = jnp.concatenate(
            [lo / jnp.where(in_one, tot_lo, 1.0), hi / jnp.where(in_one, tot_hi, 1.0)], axis=0
        )
        p = jnp.transpose(out_t)[:192]
        op_ref[k] = p
        pairs += [p[64 * g : 64 * g + 64] for g in range(3)]
    pairs.append(jnp.zeros((64, 128), F32))
    attn = jnp.concatenate(
        [unpair(pairs[2 * t], pairs[2 * t + 1]) for t in range(5)], axis=1
    ).astype(BF)
    attn_ref[...] = attn
    a = attn[:, :D]
    proj = jnp.concatenate([mm(a, w_mat(wv, 2, 2)), mm(a, w_mat(wv, 2, 3))], axis=1)
    mid = h + pltpu.roll(proj, D, 1)[:, :D]
    mid_ref[...] = mid
    n2 = (mid * inv_rms(mid) * gains[1:2]).astype(BF)
    for k in (0, 1, 3):
        loads[k].wait()
    for i in range(4):
        gate = mm(n2, w_mat(wv, 0, i))
        up = mm(n2, w_mat(wv, 1, i))
        inner = (gate * jax.nn.sigmoid(gate) * up).astype(BF)
        mid = mid + mm_t(inner, w_down(wv, i))
    next_ref[...] = mid


def forward_layer(layer, h, w, gains, cos, ssin, mask, ind, scal):
    vm = pl.BlockSpec(memory_space=pltpu.VMEM)
    return pl.pallas_call(
        functools.partial(forward_kernel, layer),
        out_shape=(
            jax.ShapeDtypeStruct((128, D), F32),
            jax.ShapeDtypeStruct((128, D), F32),
            jax.ShapeDtypeStruct((128, 640), BF),
            jax.ShapeDtypeStruct((KV, 384, 256), BF),
            jax.ShapeDtypeStruct((NX, NZ, 2, 6, 64, 128), BF),
            jax.ShapeDtypeStruct((KV, 8, 384), F32),
            jax.ShapeDtypeStruct((KV, 192, 128), F32),
        ),
        in_specs=[vm, pl.BlockSpec(memory_space=pl.ANY), vm, vm, vm, vm, vm,
                  pl.BlockSpec(memory_space=pltpu.SMEM)],
        out_specs=(vm,) * 7,
        scratch_shapes=[
            pltpu.VMEM((4, 4, 4, 144, 384), BF),
            pltpu.VMEM((KV, 8, 256, 384), F32),
            pltpu.VMEM((KV, 128, 384), F32),
            pltpu.VMEM((KV, 256, 384), F32),
            pltpu.VMEM((128, 640), F32),
            pltpu.SemaphoreType.DMA((24,)),
            pltpu.SemaphoreType.DMA((24,)),
            pltpu.SemaphoreType.DMA((4,)),
        ],
        compiler_params=pltpu.CompilerParams(
            collective_id=1 + layer, has_side_effects=True, vmem_limit_bytes=VMEM_LIMIT
        ),
        name="forward_layer",
    )(h, w, gains, cos, ssin, mask, ind, scal)


def transposed(v, wide):
    wide[:, :D] = v.astype(F32)
    return jnp.transpose(wide[...])[:D].astype(BF)


def backward_kernel(
    layer, g_ref, h_ref, mid_ref, attn_ref, qt_ref, kv, lse_ref, op_ref, w_any, gains,
    cos_ref, sin_ref, mask_ref, scal,
    dh_ref, gw, gg_ref,
    wv, dot_scr, dq_scr, pbuf, rcore, one_a1, one_b1, two_a1, two_b1, one_a2, one_b2, two_a2,
    two_b2, wide, send, recv, loc,
):
    x, z, c = place()
    loads = load_weights(w_any, layer, wv, loc)
    for k in (0, 1, 3, 2):
        loads[k].start()
    greet(False)
    wide[...] = jnp.zeros((128, 640), F32)
    g = g_ref[...]
    mid = mid_ref[...]
    gain2 = gains[1:2]
    n2 = (mid * inv_rms(mid) * gain2).astype(BF)
    n2_t = transposed(n2, wide)
    branch = g.astype(BF)
    branch_t = transposed(branch, wide)
    d_n2 = jnp.zeros((128, D), F32)
    for k in (0, 1, 3):
        loads[k].wait()
    for i in range(4):
        gate_w, up_w, down_w = w_mat(wv, 0, i), w_mat(wv, 1, i), w_down(wv, i)
        gate = mm(n2, gate_w)
        up = mm(n2, up_w)
        sig = jax.nn.sigmoid(gate)
        act = gate * sig
        inner = (act * up).astype(BF)
        d_inner = mm(branch, down_w)
        d_gate = (d_inner * up * (sig + act * (1.0 - sig))).astype(BF)
        d_up = (d_inner * act).astype(BF)
        gw[0, i] = mm(n2_t, d_gate).astype(BF).reshape(4, 144, 384)
        gw[1, i] = mm(n2_t, d_up).astype(BF).reshape(4, 144, 384)
        gw[3, :, i] = mm(branch_t, inner).astype(BF).reshape(4, 144, 384)
        d_n2 = d_n2 + mm_t(d_gate, gate_w) + mm_t(d_up, up_w)
    d_hn, gg2 = norm_back(mid, gain2, d_n2)
    d_mid = g + d_hn
    gg_ref[1:2] = gg2
    gg_ref[2:8] = jnp.zeros((6, D), F32)
    loads[2].wait()
    wide[:, :D] = d_mid
    dm = jnp.concatenate([wide[...], jnp.zeros((128, 128), F32)], axis=1)
    dm = pltpu.roll(dm, 192, 1).astype(BF)
    d_attn = mm_t(dm[:, :384], w_mat(wv, 2, 2)) + mm_t(dm[:, 384:], w_mat(wv, 2, 3))
    wide[:, :D] = d_attn
    attn_t = jnp.transpose(attn_ref[...].astype(F32))[:D].astype(BF)
    g_out = mm(attn_t, dm)
    gw[2, 3] = g_out[:, 384:].astype(BF).reshape(4, 144, 384)
    gw[2, 2] = g_out[:, :384].astype(BF).reshape(4, 144, 384)
    da = wide[...].astype(BF).astype(F32)
    da_tiles = [tile(da, i) for i in range(5)]

    in_one = lanes((1, 384)) < 192
    pick_lo = jnp.where(
        lanes((16, 128)) < HD,
        jnp.where(lax.broadcasted_iota(jnp.int32, (16, 128), 0) == 0, 1.0, 0.0),
        jnp.where(lax.broadcasted_iota(jnp.int32, (16, 128), 0) == 1, 1.0, 0.0),
    ).astype(BF)
    delta_a, delta_b = [], []
    for k in range(KV):
        dp = jnp.concatenate(
            [pair(da_tiles[(3 * k + q) // 2], (3 * k + q) % 2) for q in range(3)], axis=0
        )
        dot_scr[k] = doubled(dp)
        prod = dp * op_ref[k]
        prod = jnp.concatenate([prod, prod], axis=0)
        coarse = prod.astype(BF)
        fine = (prod - coarse.astype(F32)).astype(BF)
        rows = mm_t(pick_lo, coarse) + mm_t(pick_lo, fine)
        lo, hi = rows[0:1], rows[1:2]
        delta_a.append(jnp.where(in_one, hi, lo))
        delta_b.append(hi)

    def back(k, keys2, vals2, subs, deltas, bias):
        s = mm_t(keys2, qt_ref[k])
        if bias is not None:
            s = s + bias
        dp = mm_t(vals2, dot_scr[k])
        probs, d_s = [], []
        for i, (sub, delta) in enumerate(zip(subs, deltas)):
            p = jnp.exp(s[64 * i : 64 * i + 64] - sub)
            probs.append(p.astype(BF))
            d_s.append((p * (dp[64 * i : 64 * i + 64] - delta)).astype(BF))
        probs = jnp.concatenate(probs, axis=0)
        d_s = jnp.concatenate(d_s, axis=0)
        return mm(d_s, qt_ref[k]), mm(probs, dot_scr[k]), tmm(keys2, d_s)

    def chunk(ci, carry):
        m = mask_ref[ci]
        mf = m.astype(F32)
        for k in range(KV):
            keys, vals = chunk_of(kv, ci, k), chunk_of(kv, ci, KV + k)
            subs, deltas = [], []
            for i in range(4):
                base, extra = slot_row(scal, 4 * ci + i, lse_ref[k, 0:1], lse_ref[k, 1:2])
                subs.append(base + extra)
                deltas.append(slot_row(scal, 4 * ci + i, delta_a[k], delta_b[k])[0])
            dk, dv, dq = back(
                k,
                jnp.concatenate([keys, keys * m], axis=1),
                jnp.concatenate([vals, vals * m], axis=1),
                subs,
                deltas,
                None,
            )
            first = lanes((256, 128)) < HD
            for j, d in ((k, dk), (KV + k, dv)):
                both = jnp.where(first, d[:, :128], 0.0) + mf * d[:, 128:]
                pbuf[ci // 2, pl.ds(2 * (ci % 2), 2), :, j] = both.astype(BF).reshape(2, 2, 64, 128)
            dq_scr[k] += dq
        return carry

    bias = diag_bias()
    zero128 = jnp.zeros((128, 128), BF)
    own_grads = []
    first = lanes((64, 128)) < HD
    for k in range(KV):
        dk, dv, dq = back(
            k,
            jnp.concatenate([zero128, diag_keys(kv[x, z, c, k])], axis=1),
            jnp.concatenate([zero128, diag_keys(kv[x, z, c, KV + k])], axis=1),
            [lse_ref[k, 0:1], lse_ref[k, 1:2]],
            [delta_a[k], delta_b[k]],
            bias,
        )
        own_grads.append([jnp.where(first, d[:64, 128:], d[64:, 128:]) for d in (dk, dv)])
        dq_scr[k] = dq
    lax.fori_loop(0, 8, chunk, 0)
    for k in range(KV):
        for j in (0, 1):
            part = pbuf.at[x, z, c, KV * j + k]
            part[...] = (part[...].astype(F32) + own_grads[k][j]).astype(BF)

    wire = Wire(send, recv)
    rws = {None: pl.ds(0, 64), 0: pl.ds(0, 32), 1: pl.ds(32, 32)}

    def half_of(hf):
        def xz(f, s):
            return (s, f) if hf == 0 else (f, s)

        heads = pl.ds(3 * hf, 3)

        def view(f, s, part):
            xi, zi = xz(f, s)
            return pbuf.at[xi, zi, c, heads, rws[part]]

        def core_src(f):
            xi, zi = xz(f, ALL)
            return pbuf.at[xi, zi, 1 - c, heads]

        def core_dst(f):
            xi, zi = xz(f, ALL)
            return rcore.at[xi, zi, heads]

        slots = (
            (one_a1.at[hf], one_b1.at[hf], two_a1.at[hf], two_b1.at[hf]),
            (one_a2.at[hf], one_b2.at[hf], two_a2.at[hf], two_b2.at[hf]),
        )
        return scatter_half(wire, 12 * hf, hf, view, core_src, core_dst, slots)

    gens = [half_of(hf) for hf in (0, 1)]
    for gen in gens:
        next(gen)

    h = h_ref[...]
    gain1 = gains[0:1]
    n1 = (h * inv_rms(h) * gain1).astype(BF)
    n1_t = transposed(n1, wide)
    cos, ssin = cos_ref[...], -sin_ref[...]
    pairs = []
    for k in range(KV):
        dq = dq_scr[k]
        rolled = pltpu.roll(dq, 192, 1)
        out_t = jnp.concatenate([rolled[128:192], dq[0:64] + rolled[192:256]], axis=0)
        p = jnp.transpose(out_t)[:192]
        pairs += [p[64 * q : 64 * q + 64] for q in range(3)]
    run_all(gens)
    wire.close()
    done = [pbuf[x, z, c, i].astype(F32) for i in range(6)]
    pairs += done
    pairs.append(jnp.zeros((64, 128), F32))
    first = lanes((128, 128)) < HD
    tiles = []
    for t in range(8):
        v = unpair(pairs[2 * t], pairs[2 * t + 1])
        if t < 6:
            v = rope(v, cos, ssin)
            if t < 4:
                v = v * 0.125
            elif t == 4:
                v = jnp.where(first, v * 0.125, v)
        tiles.append(v.astype(BF))
    tiles.append(jnp.zeros((128, 128), BF))
    d_n1 = jnp.zeros((128, D), F32)
    for i in range(3):
        d = jnp.concatenate(tiles[3 * i : 3 * i + 3], axis=1)
        gr = mm(n1_t, d)
        if i == 2:
            gr = gr + gw[2, 2].reshape(D, 384).astype(F32)
        gw[2, i] = gr.astype(BF).reshape(4, 144, 384)
        d_n1 = d_n1 + mm_t(d, w_mat(wv, 2, i))
    d_h, gg1 = norm_back(h, gain1, d_n1)
    gg_ref[0:1] = gg1
    dh_ref[...] = d_mid + d_h


def backward_layer(layer, g, saved, w, gains, cos, ssin, mask, scal):
    vm = pl.BlockSpec(memory_space=pltpu.VMEM)
    return pl.pallas_call(
        functools.partial(backward_kernel, layer),
        out_shape=(
            jax.ShapeDtypeStruct((128, D), F32),
            jax.ShapeDtypeStruct((4, 4, 4, 144, 384), BF),
            jax.ShapeDtypeStruct((8, D), F32),
        ),
        in_specs=[vm] * 8 + [pl.BlockSpec(memory_space=pl.ANY)] + [vm] * 4
        + [pl.BlockSpec(memory_space=pltpu.SMEM)],
        out_specs=(vm,) * 3,
        scratch_shapes=[
            pltpu.VMEM((4, 4, 4, 144, 384), BF),
            pltpu.VMEM((KV, 384, 256), BF),
            pltpu.VMEM((KV, 256, 384), F32),
            pltpu.VMEM((NX, NZ, 2, 6, 64, 128), BF),
            pltpu.VMEM((NX, NZ, 6, 64, 128), BF),
            pltpu.VMEM((2, 4, 3, 32, 128), BF),
            pltpu.VMEM((2, 4, 3, 32, 128), BF),
            pltpu.VMEM((2, 4, 3, 64, 128), BF),
            pltpu.VMEM((2, 4, 3, 64, 128), BF),
            pltpu.VMEM((2, 3, 32, 128), BF),
            pltpu.VMEM((2, 3, 32, 128), BF),
            pltpu.VMEM((2, 3, 64, 128), BF),
            pltpu.VMEM((2, 3, 64, 128), BF),
            pltpu.VMEM((128, 640), F32),
            pltpu.SemaphoreType.DMA((24,)),
            pltpu.SemaphoreType.DMA((24,)),
            pltpu.SemaphoreType.DMA((4,)),
        ],
        compiler_params=pltpu.CompilerParams(
            collective_id=3 + layer, has_side_effects=True, vmem_limit_bytes=VMEM_LIMIT
        ),
        name="backward_layer",
    )(g, *saved, w, gains, cos, ssin, mask, scal)


def reduce_kernel(
    g0, g1, out, part_sum, rcore, one_a1, one_b1, two_a1, two_b1, one_a2, one_b2, two_a2, two_b2,
    from_y, send, recv, loc,
):
    x, z, c = place()
    y = lax.axis_index("dp")
    greet(True)
    wire = Wire(send, recv)
    a_rows, b_rows = pl.ds(0, 64), pl.ds(64, 80)
    rws = {None: pl.ds(0, 144), 0: a_rows, 1: b_rows}
    load = pltpu.make_async_copy(g0, part_sum, loc.at[0])
    for core, keep in ((0, g0), (1, g1)):

        @pl.when(c == core)
        def _():
            pltpu.make_async_copy(keep, part_sum, loc.at[0]).start()

    load.wait()

    def half_of(hf):
        def xz(f, s):
            return (s, f) if hf == 0 else (f, s)

        ys = pl.ds(2 * hf, 2)

        def view(f, s, part):
            xi, zi = xz(f, s)
            return part_sum.at[xi, zi, ys, rws[part]]

        def core_dst(f):
            xi, zi = xz(f, ALL)
            return rcore.at[xi, zi, ys]

        slots = (
            (one_a1.at[hf], one_b1.at[hf], two_a1.at[hf], two_b1.at[hf]),
            (one_a2.at[hf], one_b2.at[hf], two_a2.at[hf], two_b2.at[hf]),
        )

        def start_core(src):
            f0 = z if hf == 0 else x
            for k, d in enumerate((2, 1, -1, 0)):
                f = turn(f0, d)
                xi, zi = xz(f, ALL)
                wire.desc(
                    src.at[xi, zi, ys], core_dst(f), 12 * hf + k, {"ctx": other_core()}
                ).start()

        return view, core_dst, slots, start_core

    halves = [half_of(hf) for hf in (0, 1)]
    for core, give in ((0, g1), (1, g0)):

        @pl.when(c == core)
        def _():
            for item in halves:
                item[3](give)

    gens = []
    for hf, (view, core_dst, slots, start_core) in enumerate(halves):
        gens.append(scatter_half(wire, 12 * hf, hf, view, None, core_dst, slots))
    run_all(gens)
    mine = part_sum.at[x, z]
    for k in (1, 2, 3):
        wire.go(mine.at[turn(y, k)], from_y.at[k - 1], 23 + k, {"dp": turn(y, k)})
    for k in (1, 2, 3):
        wire.got(from_y.at[k - 1], 23 + k, {"dp": turn(y, -k)})
    total = part_sum[x, z, y].astype(F32)
    for k in range(3):
        total = total + from_y[k].astype(F32)
    out[c, x, z] = total.astype(BF)
    parts = (
        {None: pl.ds(0, 64), 0: pl.ds(0, 32), 1: pl.ds(32, 32)},
        {None: pl.ds(64, 80), 0: pl.ds(64, 32), 1: pl.ds(96, 48)},
    )

    def view_of(h):
        def view(first, second, part, core):
            xi, zi = (first, second) if h == 0 else (second, first)
            return out.at[core, xi, zi, parts[h][part]]

        return view

    run_all([gather_half(wire, 27 + 12 * h, h, view_of(h), True) for h in (0, 1)])
    wire.close()
    for hf in (0, 1):
        for k in range(4):
            f = turn(z if hf == 0 else x, (2, 1, -1, 0)[k])
            dst = halves[hf][1](f)
            wire.desc(dst, dst, 12 * hf + k, {"ctx": other_core()}).wait_send()


def reduce_grads(g0, g1):
    any_spec = pl.BlockSpec(memory_space=pl.ANY)
    return pl.pallas_call(
        reduce_kernel,
        out_shape=jax.ShapeDtypeStruct((LAYERS, NX, NZ, 144, 384), BF),
        in_specs=[any_spec, any_spec],
        out_specs=pl.BlockSpec(memory_space=pltpu.VMEM),
        scratch_shapes=[
            pltpu.VMEM((NX, NZ, NY, 144, 384), BF),
            pltpu.VMEM((NX, NZ, NY, 144, 384), BF),
            pltpu.VMEM((2, 4, 2, 64, 384), BF),
            pltpu.VMEM((2, 4, 2, 80, 384), BF),
            pltpu.VMEM((2, 4, 2, 144, 384), BF),
            pltpu.VMEM((2, 4, 2, 144, 384), BF),
            pltpu.VMEM((2, 2, 64, 384), BF),
            pltpu.VMEM((2, 2, 80, 384), BF),
            pltpu.VMEM((2, 2, 144, 384), BF),
            pltpu.VMEM((2, 2, 144, 384), BF),
            pltpu.VMEM((3, 144, 384), BF),
            pltpu.SemaphoreType.DMA((51,)),
            pltpu.SemaphoreType.DMA((51,)),
            pltpu.SemaphoreType.DMA((1,)),
        ],
        compiler_params=pltpu.CompilerParams(
            collective_id=5, has_side_effects=True, vmem_limit_bytes=VMEM_LIMIT
        ),
        name="reduce_grads",
    )(g0, g1)


def pack_weights(wq, wk, wv, wo, wg, wu, wd):
    def blocks(w):
        return w.reshape(LAYERS, 144, 4, 384).transpose(0, 2, 1, 3)

    attn = jnp.concatenate([wq, wk, wv, wo], axis=2)
    down = wd.transpose(0, 2, 1).reshape(LAYERS, 4, 144, 384)
    return jnp.stack([blocks(wg), blocks(wu), blocks(attn), down], axis=1)


def unpack_grads(r):
    r = r.astype(F32)

    def cols(v):
        return v.transpose(0, 2, 1, 3).reshape(LAYERS, 144, 1536)

    attn = cols(r[:, 2])
    down = r[:, 3].reshape(LAYERS, D, 384).transpose(0, 2, 1)
    return (
        attn[:, :, :576], attn[:, :, 576:768], attn[:, :, 768:960], attn[:, :, 960:],
        cols(r[:, 0]), cols(r[:, 1]), down,
    )


def body(
    tokens, out_grad, w_query, w_key, w_value, w_out, w_gate, w_up, w_down_, attn_gain, ffn_gain,
    block_pairs,
):
    me = lax.axis_index("ctx")
    y = lax.axis_index("dp")
    mine = block_pairs[me]
    offs = jnp.arange(64, dtype=jnp.int32)
    pos = jnp.concatenate([mine * 64 + offs, (63 - mine) * 64 + offs])
    freq = ROPE_BASE ** (-2.0 * jnp.arange(HD // 2, dtype=F32) / HD)
    ang = pos.astype(F32)[:, None] * freq[None, :]
    cos = jnp.cos(ang)
    sin = jnp.sin(ang)
    cos = jnp.concatenate([cos] * 4, axis=1)
    ssin = jnp.concatenate([-sin, sin, -sin, sin], axis=1)
    is_lo = block_pairs < mine
    is_hi = block_pairs > mine
    scal = jnp.stack([
        jnp.where(is_lo, 0.0, NEG), jnp.where(is_hi, 0.0, NEG),
        jnp.where(is_lo, 1.0, 0.0), jnp.where(is_lo | is_hi, 0.0, BIG),
    ]).astype(F32)
    lane = jnp.arange(128)[None, :]
    lo_col = jnp.repeat(is_lo, 64)[:, None]
    hi_col = jnp.repeat(is_hi, 64)[:, None]
    mask = jnp.where(lane < 64, lo_col, hi_col).astype(BF).reshape(8, 256, 128)
    ind = ((lane == 64) | ((lane == 65) & lo_col) | ((lane == 66) & hi_col)).astype(BF)
    ind = ind.reshape(8, 256, 128)

    win = pack_weights(w_query, w_key, w_value, w_out, w_gate, w_up, w_down_)
    gin = jnp.zeros((16, 256), BF)
    gin = gin.at[0:2, :144].set(attn_gain).at[2:4, :144].set(ffn_gain)
    w, gall = gather_weights(win, gin)
    gall = gall[:, :4, :144].transpose(1, 0, 2).reshape(4, D).astype(F32)
    gains = [jnp.stack([gall[l], gall[2 + l]] + [gall[l]] * 6) for l in range(LAYERS)]

    h = tokens.astype(F32)
    states = []
    for l in range(LAYERS):
        nxt, mid, attn, qt, kv, lse, op = forward_layer(
            l, h, w, gains[l], cos, ssin, mask, ind, scal
        )
        states.append((h, mid, attn, qt, kv, lse, op))
        h = nxt
    result = h.astype(BF)
    g = out_grad.astype(F32)
    gws, ggs = [None] * 2, [None] * 2
    for l in (1, 0):
        g, gws[l], gg = backward_layer(l, g, states[l], w, gains[l], cos, ssin, mask, scal)
        ggs[l] = lax.psum(gg[:2], ("dp", "ctx"))
    grads = unpack_grads(reduce_grads(gws[0], gws[1]))
    gg = jnp.stack(ggs, axis=1)
    gg = lax.dynamic_slice(gg, (0, 0, y * 144), (2, LAYERS, 144))
    return (result, g) + grads + (gg[0], gg[1])


def solution(mesh):
    row = P(("dp", "ctx"), None)
    mat = P(None, "dp", None)
    vec = P(None, "dp")
    return jax.shard_map(
        body,
        mesh=mesh,
        in_specs=(row, row) + (mat,) * 7 + (vec, vec, P()),
        out_specs=(row, row) + (mat,) * 7 + (vec, vec),
        check_vma=False,
    )
```

```python
import functools

import jax
import jax.numpy as jnp
from jax import lax
from jax.experimental import pallas as pl
from jax.experimental.pallas import tpu as pltpu
from jax.sharding import PartitionSpec as P

HEADS = 9
KV = 3
HD = 64
LAYERS = 2
D = 576
FF = 1536
NX = 4
NZ = 4
NY = 4
NORM_EPS = 1e-05
ROPE_BASE = 100000.0
NEG = -1e30
BIG = 1e30
MESH = pl.DeviceIdType.MESH
ALL = slice(None)
F32 = jnp.float32
BF = jnp.bfloat16
VMEM_LIMIT = 60 * 1024 * 1024
DIRS = (2, 1, -1)
SEMS = 256


def place():
    ctx = lax.axis_index("ctx")
    return lax.div(ctx, 8), lax.rem(lax.div(ctx, 2), 4), lax.rem(ctx, 2)


def ctx_of(x, z, c):
    return (x * NZ + z) * 2 + c


def turn(i, d):
    return lax.rem(i + (d + 4), 4)


def neighbour(axis, d):
    x, z, c = place()
    return ctx_of(turn(x, d), z, c) if axis == 0 else ctx_of(x, turn(z, d), c)


def other_core():
    x, z, c = place()
    return ctx_of(x, z, 1 - c)


def greet(dp_too=False, far_too=False):
    barrier = pltpu.get_barrier_semaphore()
    x, z, c = place()
    ids = [neighbour(0, 1), neighbour(0, -1), neighbour(1, 1), neighbour(1, -1), other_core()]
    if far_too:
        ids += [neighbour(0, 2), neighbour(1, 2)]
    for i in ids:
        pl.semaphore_signal(barrier, inc=1, device_id={"ctx": i}, device_id_type=MESH)
    count = len(ids)
    if dp_too:
        y = lax.axis_index("dp")
        for k in (1, 2, 3):
            pl.semaphore_signal(barrier, inc=1, device_id={"dp": turn(y, k)}, device_id_type=MESH)
        count += 3
    pl.semaphore_wait(barrier, count)


class Wire:
    def __init__(self, send, recv):
        self.send, self.recv, self.open, self.used = send, recv, [], 0

    def take(self, n):
        self.used += n
        assert self.used <= SEMS
        return self.used - n

    def desc(self, src, dst, k, dev):
        return pltpu.make_async_remote_copy(
            src_ref=src,
            dst_ref=dst,
            send_sem=self.send.at[k],
            recv_sem=self.recv.at[k],
            device_id=dev,
            device_id_type=MESH,
        )

    def go(self, src, dst, k, dev):
        copy = self.desc(src, dst, k, dev)
        copy.start()
        self.open.append(copy)

    def got(self, dst, k, dev):
        self.desc(dst, dst, k, dev).wait_recv()

    def close(self):
        for copy in self.open:
            copy.wait_send()
        self.open = []


def lockstep(gens):
    gens = list(gens)
    while gens:
        left = []
        for g in gens:
            try:
                next(g)
                left.append(g)
            except StopIteration:
                pass
        gens = left
        yield


def run_all(gens):
    for _ in lockstep(gens):
        pass


def tick(gen):
    try:
        next(gen)
    except StopIteration:
        pass


def halves(h):
    x, z, _ = place()
    return ((0, 1), (x, z)) if h == 0 else ((1, 0), (z, x))


def xz(h, first, second):
    return (first, second) if h == 0 else (second, first)


def on_plane(axis, d):
    return {"ctx": neighbour(axis, d)}


def on_y(d):
    return {"dp": turn(lax.axis_index("dp"), d)}


def gather_half(wire, h, view, share_view):
    c = place()[2]
    axes, (me1, me2) = halves(h)
    oth = {"ctx": other_core()}
    near, far, core = wire.take(3), wire.take(12), wire.take(4)
    firsts = [me1] + [turn(me1, -d) for d in DIRS]

    def along(n):
        block = view(firsts[n], me2)
        for j, d in enumerate(DIRS):
            wire.go(block, block, far + 3 * n + j, on_plane(axes[1], d))

    own = view(me1, me2)
    for j, d in enumerate(DIRS):
        wire.go(own, own, near + j, on_plane(axes[0], d))
    along(0)
    yield
    for j in (1, 2, 0):
        wire.got(view(firsts[j + 1], me2), near + j, oth)
        along(j + 1)
    mine = share_view(ALL, me2, c)
    wire.go(mine, mine, core + 3, oth)
    yield
    for j in (1, 2, 0):
        second = turn(me2, -DIRS[j])
        for n in range(4):
            wire.got(view(firsts[n], second), far + 3 * n + j, oth)
        part = share_view(ALL, second, c)
        wire.go(part, part, core + j, oth)
    yield
    for j in range(4):
        second = turn(me2, -DIRS[j]) if j < 3 else me2
        wire.got(share_view(ALL, second, 1 - c), core + j, oth)


def add_into(dst, *srcs):
    if len(dst.shape) > 2:

        def step(i, carry):
            add_into(dst.at[i], *[s.at[i] for s in srcs])
            return carry

        if len(dst.shape) == 3:
            for i in range(dst.shape[0]):
                step(i, 0)
        else:
            lax.fori_loop(0, dst.shape[0], step, 0)
        return
    total = dst[...].astype(F32)
    for s in srcs:
        total = total + s[...].astype(F32)
    dst[...] = total.astype(dst.dtype)


def core_swap(wire, me, src, dst):
    base = wire.take(4)
    order = DIRS + (0,)
    oth = {"ctx": other_core()}
    for k, d in enumerate(order):
        wire.go(src(turn(me, d)), dst(turn(me, d)), base + k, oth)

    def ready_of(view):
        def ready(d):
            f = turn(me, d)
            wire.got(dst(f), base + order.index(d), oth)
            add_into(view(f), dst(f))

        return ready

    return ready_of


def ring_reduce(wire, me, dev, at, buf, ready):
    base = wire.take(3)
    for j, d in enumerate(DIRS):
        ready(d)
        wire.go(at(turn(me, d)), buf.at[j], base + j, dev(d))
    ready(0)
    yield
    for j, d in enumerate(DIRS):
        wire.got(buf.at[j], base + j, dev(d))
    add_into(at(me), buf.at[0], buf.at[1], buf.at[2])


def scatter_half(wire, h, view, bufs, ready):
    axes, pos = halves(h)
    yield from ring_reduce(
        wire, pos[0], lambda d: on_plane(axes[0], d), lambda i: view(i, ALL), bufs[0], ready
    )
    yield from ring_reduce(
        wire, pos[1], lambda d: on_plane(axes[1], d), lambda i: view(pos[0], i), bufs[1],
        lambda d: None,
    )


def lanes(shape):
    return lax.broadcasted_iota(jnp.int32, shape, len(shape) - 1)


def mm(a, b):
    return lax.dot_general(a, b, (((1,), (0,)), ((), ())), preferred_element_type=F32)


def mm_t(a, b):
    return lax.dot_general(a, b, (((1,), (1,)), ((), ())), preferred_element_type=F32)


def tmm(a, b):
    return lax.dot_general(a, b, (((0,), (0,)), ((), ())), preferred_element_type=F32)


def inv_rms(v):
    return lax.rsqrt(jnp.mean(v * v, axis=-1, keepdims=True) + NORM_EPS)


def norm_back(v, g, d):
    r = inv_rms(v)
    dv = r * g * d - v * (r * r * r * jnp.mean(g * d * v, axis=-1, keepdims=True))
    return dv, jnp.sum(d * v * r, axis=0, keepdims=True)


def rope(t, cos, ssin):
    first = lax.rem(lanes(t.shape), HD) < HD // 2
    turned = jnp.where(first, pltpu.roll(t, 96, 1), pltpu.roll(t, 32, 1))
    return t * cos + turned * ssin


def pair(t, half):
    lo, hi = t[:64], t[64:]
    first = lanes((64, 128)) < HD
    if half == 0:
        return jnp.where(first, lo, pltpu.roll(hi, HD, 1))
    return jnp.where(first, pltpu.roll(lo, HD, 1), hi)


def unpair(a, b):
    first = lanes((64, 128)) < HD
    lo = jnp.where(first, a, pltpu.roll(b, HD, 1))
    hi = jnp.where(first, pltpu.roll(a, HD, 1), b)
    return jnp.concatenate([lo, hi], axis=0)


def tile(v, i):
    return v[:, 128 * i : 128 * i + 128]


def doubled(p):
    first = lanes((192, 128)) < HD
    one = jnp.where(first, pltpu.roll(p, HD, 1), 0.0)
    zero = jnp.zeros((192, 128), F32)
    return jnp.concatenate(
        [jnp.concatenate([one, zero], axis=1), jnp.concatenate([zero, p], axis=1)], axis=0
    ).astype(BF)


def slot_row(scal, c, row_a, row_b):
    pick = jnp.full((1, 384), scal[2, c], F32) > 0.5
    own = jnp.full((1, 384), scal[3, c], F32)
    extra = jnp.where(lanes((1, 384)) >= 192, own, 0.0)
    return jnp.where(pick, row_a, row_b), extra


def rel(i):
    return turn(i - lax.axis_index("dp"), 4)


def w_mat(wv, kind, i):
    return jnp.concatenate([wv[kind, i, rel(j)] for j in range(NY)], axis=0)


def w_attn(wa, i):
    return jnp.concatenate([wa[i, rel(j)] for j in range(NY)], axis=0)


def w_down(wv, i):
    return wv[3, :, rel(i)].reshape(D, 384)


def load_weights(w_attn_any, w_mlp_any, wa, wm, sems):
    return [
        pltpu.make_async_copy(w_mlp_any.at[0], wm.at[0], sems.at[0]),
        pltpu.make_async_copy(w_mlp_any.at[1], wm.at[1], sems.at[1]),
        pltpu.make_async_copy(w_attn_any, wa, sems.at[2]),
        pltpu.make_async_copy(w_mlp_any.at[3], wm.at[3], sems.at[3]),
    ]


def multiple(v, n):
    return pl.multiple_of(v, n)


def kv_gather(wire, kv, k):
    c = place()[2]

    def gen(h):
        def view(first, second):
            xi, zi = xz(h, first, second)
            return kv.at[xi, zi, c, k, h]

        def share(first, second, core):
            xi, zi = xz(h, first, second)
            return kv.at[xi, zi, core, k, h]

        return gather_half(wire, h, view, share)

    return lockstep([gen(h) for h in (0, 1)])


def chunk_of(buf, ci, k, j):
    return buf[ci // 2, pl.ds(2 * (ci % 2), 2), :, k, j].reshape(256, 128)


def diag_keys(k):
    first = lanes((64, 128)) < HD
    zero = jnp.zeros((64, 128), k.dtype)
    both = jnp.concatenate([jnp.where(first, k, zero), jnp.where(first, zero, k)], axis=0)
    return both


def diag_bias():
    shape = (128, 384)
    key = lax.rem(lax.broadcasted_iota(jnp.int32, shape, 0), 64)
    q = lanes(shape)
    visible = (q >= 192) & (key <= lax.rem(q, 64))
    return jnp.where(visible, 0.0, NEG)


def row_split():
    c = place()[2]
    mine = pl.ds(multiple(64 * c, 16), 80)
    return mine, lambda core: pl.ds(multiple(80 * core, 16), 64)


def over_y(wire, src, view):
    mine, handed = row_split()
    c = place()[2]
    oth = {"ctx": other_core()}
    near, core = wire.take(3), wire.take(3)
    for j, d in enumerate(DIRS):
        wire.go(src(mine), view((4 - d) % 4, mine), near + j, on_y(d))
    yield
    for j in (1, 2, 0):
        k = (4 - DIRS[j]) % 4
        wire.got(view(k, mine), near + j, oth)
        part = view(k, handed(c))
        wire.go(part, part, core + j, oth)
    yield
    for j in range(3):
        wire.got(view((4 - DIRS[j]) % 4, handed(1 - c)), core + j, oth)


def attn_weights_gen(wire, win, wa, first, count):
    blocks = pl.ds(first, count)
    return over_y(
        wire, lambda rows: win.at[blocks, rows], lambda k, rows: wa.at[blocks, k, rows]
    )


def weights_gen(wire, win, w, own):
    x, z, _ = place()
    mine, handed = row_split()
    hi, lo = pl.ds(256, 128), pl.ds(0, 256)
    own.start()
    around = over_y(
        wire, lambda rows: win.at[:, :, rows, hi], lambda k, rows: w.at[:, :, k, rows, hi]
    )

    def over():
        near = wire.take(3)
        for j, d in enumerate(DIRS):
            wire.go(
                win.at[x, z, mine, lo], w.at[x, z, (4 - d) % 4, mine, lo], near + j, on_y(d)
            )
        yield
        for j, d in enumerate(DIRS):
            wire.got(w.at[x, z, (4 - d) % 4, mine, lo], near + j, on_y(d))

        def half(h):
            cols = pl.ds(128 * h, 128)

            def view(first, second):
                xi, zi = xz(h, first, second)
                return w.at[xi, zi, pl.ds(1, 3), mine, cols]

            def share(first, second, core):
                xi, zi = xz(h, first, second)
                return w.at[xi, zi, pl.ds(1, 3), handed(core), cols]

            return gather_half(wire, h, view, share)

        yield from lockstep([half(0), half(1)])

    yield from lockstep([over(), around])
    own.wait()


def gains_exchange(wire, gin, landing):
    base = wire.take(3)
    for j, d in enumerate(DIRS):
        wire.go(gin, landing.at[(4 - d) % 4], base + j, on_y(d))
    yield
    for j, d in enumerate(DIRS):
        wire.got(landing.at[(4 - d) % 4], base + j, on_y(d))


def gains_rows(gin, landing):
    total = jnp.zeros((16, 640), F32)
    landing[0] = gin[...]
    for j in range(NY):
        part = landing[rel(j)].astype(F32)
        part = jnp.concatenate([part, jnp.zeros((16, 384), F32)], axis=1)
        total = total + (pltpu.roll(part, 144 * j, 1) if j else part)
    return total


def first_forward_kernel(
    h_ref, win_a, win_b, gin, cos_ref, sin_ref, mask_ref, ind_ref, scal,
    next_ref, mid_ref, attn_ref, qt_ref, kv, lse_ref, op_ref, a_out, b_out, gains,
    wa, wm, s_scr, sd_scr, acc_scr, landing, send, recv, loc,
):
    greet(True, True)
    wire = Wire(send, recv)
    own_a = pltpu.make_async_copy(win_a, wa.at[:, 0], loc.at[0])
    own_b = pltpu.make_async_copy(win_b, wm.at[:, :, 0], loc.at[1])
    own_a.start()
    early = attn_weights_gen(wire, win_a, wa, 0, 3)
    tick(early)
    last = attn_weights_gen(wire, win_a, wa, 3, 1)
    run_all([early, gains_exchange(wire, gin, landing), last])
    own_a.wait()
    keep_a = pltpu.make_async_copy(wa, a_out, loc.at[2])
    keep_a.start()
    gains[...] = gains_rows(gin, landing)
    later = weights_gen(wire, win_b, wm, own_b)
    tick(later)

    def need(kind):
        if kind == 0:
            run_all([later])

    forward_core(
        0, wire, later, need, h_ref, gains, cos_ref, sin_ref, mask_ref, ind_ref, scal,
        next_ref, mid_ref, attn_ref, qt_ref, kv, lse_ref, op_ref, wa, wm, s_scr, sd_scr, acc_scr,
    )
    keep_b = pltpu.make_async_copy(wm, b_out, loc.at[3])
    keep_b.start()
    keep_a.wait()
    keep_b.wait()
    wire.close()


def second_forward_kernel(
    h_ref, b_any, win_m, gains, cos_ref, sin_ref, mask_ref, ind_ref, scal,
    next_ref, mid_ref, attn_ref, qt_ref, kv, lse_ref, op_ref, m_out,
    wa, wm, s_scr, sd_scr, acc_scr, send, recv, loc,
):
    load = pltpu.make_async_copy(b_any.at[2], wa, loc.at[0])
    load.start()
    greet(True, True)
    wire = Wire(send, recv)
    later = weights_gen(wire, win_m, wm, pltpu.make_async_copy(win_m, wm.at[:, :, 0], loc.at[1]))
    tick(later)

    def need(kind):
        if kind == 2:
            load.wait()
        if kind == 0:
            run_all([later])

    forward_core(
        1, wire, later, need, h_ref, gains, cos_ref, sin_ref, mask_ref, ind_ref, scal,
        next_ref, mid_ref, attn_ref, qt_ref, kv, lse_ref, op_ref, wa, wm, s_scr, sd_scr, acc_scr,
    )
    keep = pltpu.make_async_copy(wm, m_out, loc.at[2])
    keep.start()
    keep.wait()
    wire.close()


def forward_core(
    layer, wire, later, need, h_ref, gains, cos_ref, sin_ref, mask_ref, ind_ref, scal,
    next_ref, mid_ref, attn_ref, qt_ref, kv, lse_ref, op_ref, wa, wm, s_scr, sd_scr, acc_scr,
):
    x, z, c = place()
    h = h_ref[...]
    n1 = (h * inv_rms(h) * gains[layer : layer + 1, :D]).astype(BF)
    need(2)
    cos, ssin = cos_ref[...], sin_ref[...]
    low = lanes((128, 128)) < HD
    kv_part = mm(n1, w_attn(wa, 0))
    t0, t1, t2 = [tile(kv_part, i) for i in range(3)]
    t0 = rope(t0, cos, ssin)
    t1 = jnp.where(low, rope(t1, cos, ssin), t1)
    k_pairs = [pair(t0, 0), pair(t0, 1), pair(t1, 0)]
    v_pairs = [pair(t1, 1), pair(t2, 0), pair(t2, 1)]
    spread = []
    for k in range(KV):
        kv[x, z, c, k, 0] = k_pairs[k].astype(BF)
        kv[x, z, c, k, 1] = v_pairs[k].astype(BF)
        spread.append(kv_gather(wire, kv, k))
        tick(spread[k])
    q_part = [mm(n1, w_attn(wa, i)) for i in (1, 2)]
    tiles = [rope(tile(q_part[i // 3], i % 3), cos, ssin) for i in range(5)]
    for k in range(KV):
        qp = jnp.concatenate(
            [pair(tiles[(3 * k + g) // 2], (3 * k + g) % 2) for g in range(3)], axis=0
        )
        qt_ref[k] = doubled(qp * 0.125)

    in_one = lanes((1, 384)) < 192
    bias = diag_bias()
    zero128 = jnp.zeros((128, 128), BF)
    runs = []
    for k in range(KV):
        keys = diag_keys(kv[x, z, c, k, 0])
        sd = mm_t(jnp.concatenate([zero128, keys], axis=1), qt_ref[k]) + bias
        sd_scr[k] = sd
        lo = jnp.max(sd[:64].reshape(8, 8, 384), axis=0)
        hi = jnp.max(sd[64:].reshape(8, 8, 384), axis=0)
        runs.append((jnp.full((8, 384), NEG, F32), lo, hi))
    dlane = lanes((128, 128))
    drow = lax.broadcasted_iota(jnp.int32, (128, 128), 0)
    dind = jnp.where(
        ((dlane == 65) & (drow < 64)) | ((dlane == 66) & (drow >= 64)), 1.0, 0.0
    ).astype(BF)
    first = lanes((256, 128)) < HD

    def scores(k):
        def step(pairi, carry):
            one, lo, hi = carry
            for ci in (2 * pairi, 2 * pairi + 1):
                keys = chunk_of(kv, ci, k, 0)
                s = mm_t(jnp.concatenate([keys, keys * mask_ref[ci]], axis=1), qt_ref[k])
                s_scr[k, ci] = s
                for i in range(4):
                    top = jnp.max(s[64 * i : 64 * i + 64].reshape(8, 8, 384), axis=0)
                    slot = 4 * ci + i
                    one = jnp.maximum(one, top)
                    lo = jnp.maximum(lo, top + scal[0, slot])
                    hi = jnp.maximum(hi, top + scal[1, slot])
            return one, lo, hi

        got = lax.fori_loop(0, 4, step, runs[k])
        one, lo, hi = [jnp.max(r, axis=0, keepdims=True) for r in got]
        top = jnp.where(in_one, one, hi)
        top = jnp.maximum(top, pltpu.roll(top, 192, 1))
        return jnp.where(in_one, top, lo), top

    def values(k, row_a, row_b):
        sd = sd_scr[k]
        p = jnp.concatenate([jnp.exp(sd[:64] - row_a), jnp.exp(sd[64:] - row_b)], axis=0)
        vals = jnp.concatenate([dind, diag_keys(kv[x, z, c, k, 1])], axis=1)
        acc_scr[k] = tmm(vals, p.astype(BF))

        def step(pairi, carry):
            total = acc_scr[k]
            for ci in (2 * pairi, 2 * pairi + 1):
                s = s_scr[k, ci]
                parts = []
                for i in range(4):
                    base, extra = slot_row(scal, 4 * ci + i, row_a, row_b)
                    parts.append(jnp.exp(s[64 * i : 64 * i + 64] - (base + extra)))
                p = jnp.concatenate(parts, axis=0).astype(BF)
                v = chunk_of(kv, ci, k, 1)
                vals = jnp.concatenate(
                    [jnp.where(first, v, ind_ref[ci]), v * mask_ref[ci]], axis=1
                )
                total = total + tmm(vals, p)
            acc_scr[k] = total
            return carry

        lax.fori_loop(0, 4, step, 0)

    for k in range(KV):
        tick(spread[k])
    tick(later)
    row_a, row_b = [], []
    run_all([spread[0]])
    for k in range(KV):
        if k + 1 < KV:
            tick(spread[k + 1])
        tick(later)
        a, b = scores(k)
        row_a.append(a)
        row_b.append(b)
        if k + 1 < KV:
            run_all([spread[k + 1]])
        values(k, a, b)

    pairs = []
    for k in range(KV):
        acc = acc_scr[k]
        rolled = pltpu.roll(acc, 192, 1)
        hi = acc[0:64] + rolled[192:256]
        lo = rolled[128:192]
        tot_hi = acc[64:65] + rolled[66:67]
        tot_lo = rolled[65:66]
        lse_hi = row_b[k] + jnp.log(jnp.where(in_one, tot_hi, 1.0))
        lse_hi = jnp.where(in_one, lse_hi, pltpu.roll(lse_hi, 192, 1))
        lse_lo = pltpu.roll(row_a[k], 192, 1) + jnp.log(jnp.where(in_one, tot_lo, 1.0))
        lse_ref[k, 0:1] = jnp.where(in_one, lse_hi, pltpu.roll(lse_lo, 192, 1))
        lse_ref[k, 1:2] = lse_hi
        lse_ref[k, 2:8] = jnp.zeros((6, 384), F32)
        out_t = jnp.concatenate(
            [lo / jnp.where(in_one, tot_lo, 1.0), hi / jnp.where(in_one, tot_hi, 1.0)], axis=0
        )
        p = jnp.transpose(out_t)[:192]
        op_ref[k] = p
        pairs += [p[64 * g : 64 * g + 64] for g in range(3)]
    pairs.append(jnp.zeros((64, 128), F32))
    attn = jnp.concatenate(
        [unpair(pairs[2 * t], pairs[2 * t + 1]) for t in range(5)], axis=1
    ).astype(BF)
    attn_ref[...] = attn
    a = attn[:, :D]
    proj = jnp.concatenate([mm(a, w_attn(wa, 2)), mm(a, w_attn(wa, 3))], axis=1)
    mid = h + pltpu.roll(proj, D, 1)[:, :D]
    mid_ref[...] = mid
    n2 = (mid * inv_rms(mid) * gains[2 + layer : 3 + layer, :D]).astype(BF)
    need(0)
    for i in range(4):
        gate = mm(n2, w_mat(wm, 0, i))
        up = mm(n2, w_mat(wm, 1, i))
        inner = (gate * jax.nn.sigmoid(gate) * up).astype(BF)
        mid = mid + mm_t(inner, w_down(wm, i))
    next_ref[...] = mid


SAVED = (
    jax.ShapeDtypeStruct((128, D), F32),
    jax.ShapeDtypeStruct((128, D), F32),
    jax.ShapeDtypeStruct((128, 640), BF),
    jax.ShapeDtypeStruct((KV, 384, 256), BF),
    jax.ShapeDtypeStruct((NX, NZ, 2, KV, 2, 64, 128), BF),
    jax.ShapeDtypeStruct((KV, 8, 384), F32),
    jax.ShapeDtypeStruct((KV, 192, 128), F32),
)
FORWARD_SCRATCH = (
    ((4, 4, 144, 384), BF),
    ((4, 4, 4, 144, 384), BF),
    ((KV, 8, 256, 384), F32),
    ((KV, 128, 384), F32),
    ((KV, 256, 384), F32),
)
GATHERED = jax.ShapeDtypeStruct((NX, NZ, NY, 144, 384), BF)
ATTN_GATHERED = jax.ShapeDtypeStruct((4, NY, 144, 384), BF)


def specs():
    return (
        pl.BlockSpec(memory_space=pltpu.VMEM),
        pl.BlockSpec(memory_space=pl.ANY),
        pl.BlockSpec(memory_space=pltpu.SMEM),
    )


def sems(*counts):
    return [pltpu.SemaphoreType.DMA((n,)) for n in counts]


def params(cid):
    return pltpu.CompilerParams(
        collective_id=cid, has_side_effects=True, vmem_limit_bytes=VMEM_LIMIT
    )


def first_forward(h, win_a, win_b, gin, cos, ssin, mask, ind, scal):
    vm, anyw, sm = specs()
    return pl.pallas_call(
        first_forward_kernel,
        out_shape=SAVED + (ATTN_GATHERED, GATHERED, jax.ShapeDtypeStruct((16, 640), F32)),
        in_specs=[vm, anyw, anyw, vm, vm, vm, vm, vm, sm],
        out_specs=(vm,) * 7 + (anyw, anyw, vm),
        scratch_shapes=[pltpu.VMEM(*v) for v in FORWARD_SCRATCH]
        + [pltpu.VMEM((NY, 16, 256), BF)]
        + sems(SEMS, SEMS, 4),
        compiler_params=params(0),
        name="first_forward",
    )(h, win_a, win_b, gin, cos, ssin, mask, ind, scal)


def second_forward(h, w_b, win_m, gains, cos, ssin, mask, ind, scal):
    vm, anyw, sm = specs()
    return pl.pallas_call(
        second_forward_kernel,
        out_shape=SAVED + (GATHERED,),
        in_specs=[vm, anyw, anyw, vm, vm, vm, vm, vm, sm],
        out_specs=(vm,) * 7 + (anyw,),
        scratch_shapes=[pltpu.VMEM(*v) for v in FORWARD_SCRATCH] + sems(SEMS, SEMS, 3),
        compiler_params=params(1),
        name="second_forward",
    )(h, w_b, win_m, gains, cos, ssin, mask, ind, scal)


def transposed(v, wide):
    wide[:, :D] = v.astype(F32)
    return jnp.transpose(wide[...])[:D].astype(BF)


def first_backward_kernel(*refs):
    ins, attn_any, mlp_any = refs[:13], refs[13], refs[14]
    dh_ref, g_attn, gg_ref, summed = refs[15:19]
    work, rest = refs[19 : 19 + N_WORK], refs[19 + N_WORK :]
    gm, bufs, (send, recv, loc) = rest[0], rest[1:-3], rest[-3:]
    loads = load_weights(attn_any, mlp_any, work[0], work[1], loc)
    for k in (0, 1, 3, 2):
        loads[k].start()
    greet(True, True)
    wire = Wire(send, recv)
    gm[2] = jnp.zeros((4, 4, 144, 384), BF)
    batch = reduce_gen(wire, gm, summed, bufs, loc.at[4])
    backward_core(1, wire, batch, loads, ins, dh_ref, gm, g_attn, gg_ref, work)
    run_all([batch])
    wire.close()


def second_backward_kernel(*refs):
    ins, attn_any, mlp_any, ga1, gg1 = refs[:13], refs[13], refs[14], refs[15], refs[16]
    dh_ref, summed, summed_a, gains_out = refs[17:21]
    work, rest = refs[21 : 21 + N_WORK], refs[21 + N_WORK :]
    gm, ga, gg, steps, got = rest[:5]
    bufs, late = rest[5 : 5 + N_REDUCE], rest[5 + N_REDUCE : -3]
    send, recv, loc = rest[-3:]
    loads = load_weights(attn_any, mlp_any, work[0], work[1], loc)
    for k in (0, 1, 3, 2):
        loads[k].start()
    other = pltpu.make_async_copy(ga1, gm.at[2], loc.at[5])
    other.start()
    greet(True, True)
    wire = Wire(send, recv)
    batch = reduce_gen(wire, gm, summed, bufs, loc.at[4])
    other.wait()
    backward_core(0, wire, batch, loads, ins, dh_ref, gm, ga, gg, work)
    steps[0] = jnp.zeros((8, 640), F32)
    steps[0, 0:2, :D] = gg[0:2]
    steps[0, 2:4, :D] = gg1[0:2]
    run_all([attn_reduce_gen(wire, ga, summed_a, late), gains_gen(wire, steps, got), batch])
    gains_out[...] = steps[4]
    wire.close()


def backward_core(layer, wire, batch, loads, ins, dh_ref, gm, ga, gg_ref, work):
    (
        g_ref, h_ref, mid_ref, attn_ref, qt_ref, kv, lse_ref, op_ref, gains,
        cos_ref, sin_ref, mask_ref, scal,
    ) = ins
    wa, wm, dot_scr, dq_scr, pbuf, rcore, kv_one, kv_two, wide = work
    x, z, c = place()
    wide[...] = jnp.zeros((128, 640), F32)
    g = g_ref[...]
    mid = mid_ref[...]
    gain2 = gains[2 + layer : 3 + layer, :D]
    n2 = (mid * inv_rms(mid) * gain2).astype(BF)
    n2_t = transposed(n2, wide)
    branch = g.astype(BF)
    branch_t = transposed(branch, wide)
    d_n2 = jnp.zeros((128, D), F32)
    for k in (0, 1, 3):
        loads[k].wait()
    for i in range(4):
        gate_w, up_w, down_w = w_mat(wm, 0, i), w_mat(wm, 1, i), w_down(wm, i)
        gate = mm(n2, gate_w)
        up = mm(n2, up_w)
        sig = jax.nn.sigmoid(gate)
        act = gate * sig
        inner = (act * up).astype(BF)
        d_inner = mm(branch, down_w)
        d_gate = (d_inner * up * (sig + act * (1.0 - sig))).astype(BF)
        d_up = (d_inner * act).astype(BF)
        gm[0, i] = mm(n2_t, d_gate).astype(BF).reshape(4, 144, 384)
        gm[1, i] = mm(n2_t, d_up).astype(BF).reshape(4, 144, 384)
        gm[3, :, i] = mm(branch_t, inner).astype(BF).reshape(4, 144, 384)
        d_n2 = d_n2 + mm_t(d_gate, gate_w) + mm_t(d_up, up_w)
    tick(batch)
    d_hn, gg2 = norm_back(mid, gain2, d_n2)
    d_mid = g + d_hn
    gg_ref[1:2] = gg2
    gg_ref[2:8] = jnp.zeros((6, D), F32)
    loads[2].wait()
    wide[:, :D] = d_mid
    dm = jnp.concatenate([wide[...], jnp.zeros((128, 128), F32)], axis=1)
    dm = pltpu.roll(dm, 192, 1).astype(BF)
    d_attn = mm_t(dm[:, :384], w_attn(wa, 2)) + mm_t(dm[:, 384:], w_attn(wa, 3))
    wide[:, :D] = d_attn
    attn_t = jnp.transpose(attn_ref[...].astype(F32))[:D].astype(BF)
    g_out = mm(attn_t, dm)
    ga[3] = g_out[:, 384:].astype(BF).reshape(4, 144, 384)
    ga[2] = g_out[:, :384].astype(BF).reshape(4, 144, 384)
    da = wide[...].astype(BF).astype(F32)
    da_tiles = [tile(da, i) for i in range(5)]
    tick(batch)

    in_one = lanes((1, 384)) < 192
    pick_lo = jnp.where(
        lanes((16, 128)) < HD,
        jnp.where(lax.broadcasted_iota(jnp.int32, (16, 128), 0) == 0, 1.0, 0.0),
        jnp.where(lax.broadcasted_iota(jnp.int32, (16, 128), 0) == 1, 1.0, 0.0),
    ).astype(BF)
    delta_a, delta_b = [], []
    for k in range(KV):
        dp = jnp.concatenate(
            [pair(da_tiles[(3 * k + q) // 2], (3 * k + q) % 2) for q in range(3)], axis=0
        )
        dot_scr[k] = doubled(dp)
        prod = dp * op_ref[k]
        prod = jnp.concatenate([prod, prod], axis=0)
        coarse = prod.astype(BF)
        fine = (prod - coarse.astype(F32)).astype(BF)
        rows = mm_t(pick_lo, coarse) + mm_t(pick_lo, fine)
        lo, hi = rows[0:1], rows[1:2]
        delta_a.append(jnp.where(in_one, hi, lo))
        delta_b.append(hi)

    def back(k, keys2, vals2, subs, deltas, bias):
        s = mm_t(keys2, qt_ref[k])
        if bias is not None:
            s = s + bias
        dp = mm_t(vals2, dot_scr[k])
        probs, d_s = [], []
        for i, (sub, delta) in enumerate(zip(subs, deltas)):
            p = jnp.exp(s[64 * i : 64 * i + 64] - sub)
            probs.append(p.astype(BF))
            d_s.append((p * (dp[64 * i : 64 * i + 64] - delta)).astype(BF))
        probs = jnp.concatenate(probs, axis=0)
        d_s = jnp.concatenate(d_s, axis=0)
        return mm(d_s, qt_ref[k]), mm(probs, dot_scr[k]), tmm(keys2, d_s)

    bias = diag_bias()
    zero128 = jnp.zeros((128, 128), BF)
    first = lanes((64, 128)) < HD
    wide_first = lanes((256, 128)) < HD

    def head(k):
        own = []
        dk, dv, dq = back(
            k,
            jnp.concatenate([zero128, diag_keys(kv[x, z, c, k, 0])], axis=1),
            jnp.concatenate([zero128, diag_keys(kv[x, z, c, k, 1])], axis=1),
            [lse_ref[k, 0:1], lse_ref[k, 1:2]],
            [delta_a[k], delta_b[k]],
            bias,
        )
        for d in (dk, dv):
            own.append(jnp.where(first, d[:64, 128:], d[64:, 128:]))
        dq_scr[k] = dq

        def step(pairi, carry):
            total = dq_scr[k]
            for ci in (2 * pairi, 2 * pairi + 1):
                m = mask_ref[ci]
                keys, vals = chunk_of(kv, ci, k, 0), chunk_of(kv, ci, k, 1)
                subs, deltas = [], []
                for i in range(4):
                    base, extra = slot_row(scal, 4 * ci + i, lse_ref[k, 0:1], lse_ref[k, 1:2])
                    subs.append(base + extra)
                    deltas.append(slot_row(scal, 4 * ci + i, delta_a[k], delta_b[k])[0])
                dk, dv, dq = back(
                    k,
                    jnp.concatenate([keys, keys * m], axis=1),
                    jnp.concatenate([vals, vals * m], axis=1),
                    subs,
                    deltas,
                    None,
                )
                mf = m.astype(F32)
                for j, d in enumerate((dk, dv)):
                    both = jnp.where(wide_first, d[:, :128], 0.0) + mf * d[:, 128:]
                    both = both.astype(BF).reshape(2, 2, 64, 128)
                    pbuf[pairi, pl.ds(2 * (ci - 2 * pairi), 2), :, k, j] = both
                total = total + dq
            dq_scr[k] = total
            return carry

        lax.fori_loop(0, 2, step, 0)
        tick(batch)
        lax.fori_loop(2, 4, step, 0)
        for j in (0, 1):
            part = pbuf.at[x, z, c, k, j]
            part[...] = (part[...].astype(F32) + own[j]).astype(BF)

    def kv_reduce(k, h):
        me = halves(h)[1][0]

        def view(f, s):
            xi, zi = xz(h, f, s)
            return pbuf.at[xi, zi, c, k, h]

        def src(f):
            xi, zi = xz(h, f, ALL)
            return pbuf.at[xi, zi, 1 - c, k, h]

        def dst(f):
            xi, zi = xz(h, f, ALL)
            return rcore.at[xi, zi, k, h]

        ready_of = core_swap(wire, me, src, dst)
        return scatter_half(
            wire, h, view, (kv_one.at[k, h], kv_two.at[k, h]), ready_of(lambda f: view(f, ALL))
        )

    sums = []
    for k in range(KV):
        head(k)
        tick(batch)
        sums.append(lockstep([kv_reduce(k, j) for j in (0, 1)]))
        for gen in sums:
            tick(gen)

    h = h_ref[...]
    gain1 = gains[layer : layer + 1, :D]
    n1 = (h * inv_rms(h) * gain1).astype(BF)
    n1_t = transposed(n1, wide)
    cos, ssin = cos_ref[...], -sin_ref[...]
    pairs = []
    for k in range(KV):
        dq = dq_scr[k]
        rolled = pltpu.roll(dq, 192, 1)
        out_t = jnp.concatenate([rolled[128:192], dq[0:64] + rolled[192:256]], axis=0)
        p = jnp.transpose(out_t)[:192]
        pairs += [p[64 * q : 64 * q + 64] for q in range(3)]
    pairs.append(jnp.zeros((64, 128), F32))
    q_tiles = [
        (rope(unpair(pairs[2 * t], pairs[2 * t + 1]), cos, ssin) * 0.125).astype(BF)
        for t in range(5)
    ]
    q_tiles.append(jnp.zeros((128, 128), BF))
    d_n1 = jnp.zeros((128, D), F32)

    def attn_block(i, d):
        grad = mm(n1_t, d)
        if i == 2:
            grad = grad + ga[2].reshape(D, 384).astype(F32)
        ga[i] = grad.astype(BF).reshape(4, 144, 384)
        return mm_t(d, w_attn(wa, i))

    for i in (1, 2):
        d_n1 = d_n1 + attn_block(i, jnp.concatenate(q_tiles[3 * i - 3 : 3 * i], axis=1))
    tick(batch)
    run_all(sums)
    done = [[pbuf[x, z, c, k, j].astype(F32) for j in (0, 1)] for k in range(KV)]
    low = lanes((128, 128)) < HD
    t0 = rope(unpair(done[0][0], done[1][0]), cos, ssin)
    t1 = unpair(done[2][0], done[0][1])
    t1 = jnp.where(low, rope(t1, cos, ssin), t1)
    t2 = unpair(done[1][1], done[2][1])
    d_n1 = d_n1 + attn_block(0, jnp.concatenate([t0, t1, t2], axis=1).astype(BF))
    d_h, gg1 = norm_back(h, gain1, d_n1)
    gg_ref[0:1] = gg1
    dh_ref[...] = d_mid + d_h


BACKWARD_SCRATCH = (
    ((4, 4, 144, 384), BF),
    ((4, 4, 4, 144, 384), BF),
    ((KV, 384, 256), BF),
    ((KV, 256, 384), F32),
    ((NX, NZ, 2, KV, 2, 64, 128), BF),
    ((NX, NZ, KV, 2, 64, 128), BF),
    ((KV, 2, 3, 4, 64, 128), BF),
    ((KV, 2, 3, 64, 128), BF),
    ((128, 640), F32),
)
N_WORK = len(BACKWARD_SCRATCH)
SUMMED = jax.ShapeDtypeStruct((NX, NZ, 144, 384), BF)


def vmems(shapes):
    return [pltpu.VMEM(v, BF) for v in shapes]


def first_backward(ins):
    vm, anyw, sm = specs()
    return pl.pallas_call(
        first_backward_kernel,
        out_shape=(
            jax.ShapeDtypeStruct((128, D), F32), ATTN_GATHERED, jax.ShapeDtypeStruct((8, D), F32),
            SUMMED,
        ),
        in_specs=[vm] * 12 + [sm, anyw, anyw],
        out_specs=(vm,) * 4,
        scratch_shapes=[pltpu.VMEM(*v) for v in BACKWARD_SCRATCH]
        + [pltpu.VMEM((4, 4, 4, 144, 384), BF)] + vmems(REDUCE_SHAPES) + sems(SEMS, SEMS, 5),
        compiler_params=params(2),
        name="first_backward",
    )(*ins)


def second_backward(ins, ga1, gg1):
    vm, anyw, sm = specs()
    scratch = [pltpu.VMEM(*v) for v in BACKWARD_SCRATCH]
    scratch += [
        pltpu.VMEM((4, 4, 4, 144, 384), BF),
        pltpu.VMEM((4, 4, 144, 384), BF),
        pltpu.VMEM((8, D), F32),
        pltpu.VMEM((5, 8, 640), F32),
        pltpu.VMEM((10, 8, 640), F32),
    ]
    scratch += vmems(REDUCE_SHAPES) + vmems(ATTN_REDUCE_SHAPES)
    return pl.pallas_call(
        second_backward_kernel,
        out_shape=(
            jax.ShapeDtypeStruct((128, D), F32), SUMMED,
            jax.ShapeDtypeStruct((4, 144, 384), BF), jax.ShapeDtypeStruct((8, 640), F32),
        ),
        in_specs=[vm] * 12 + [sm, anyw, anyw, anyw, vm],
        out_specs=(vm,) * 4,
        scratch_shapes=scratch + sems(SEMS, SEMS, 6),
        compiler_params=params(3),
        name="second_backward",
    )(*ins, ga1, gg1)


REDUCE_SHAPES = (
    ((4, 4, 4, 80, 384),) * 2
    + ((3, 4, 2, 80, 256), (3, 2, 80, 256)) * 2
    + ((3, 4, 4, 80, 128),)
    + ((3, 4, 48, 128), (3, 48, 128), (3, 4, 32, 128), (3, 32, 128))
    + ((3, 80, 256),)
)
N_REDUCE = len(REDUCE_SHAPES)


def reduce_gen(wire, src, out, bufs, sem):
    total, rcore = bufs[0], bufs[1]
    plane, ring, late, from_y = (bufs[2:4], bufs[4:6]), bufs[6], (bufs[7:9], bufs[9:11]), bufs[11]
    x, z, c = place()
    y = lax.axis_index("dp")
    mine = row_split()[0]
    theirs = pl.ds(multiple(64 - 64 * c, 16), 80)
    hi, lo = pl.ds(256, 128), pl.ds(0, 256)
    load = pltpu.make_async_copy(src.at[:, :, :, mine], total, sem)
    load.start()

    def plane_first(h):
        ys = pl.ds(2 * h, 2)

        def view(f, s):
            xi, zi = xz(h, f, s)
            return total.at[xi, zi, ys, :, lo]

        def give(f):
            xi, zi = xz(h, f, ALL)
            return src.at[xi, zi, ys, theirs, lo]

        def dst(f):
            xi, zi = xz(h, f, ALL)
            return rcore.at[xi, zi, ys, :, lo]

        ready_of = core_swap(wire, halves(h)[1][0], give, dst)
        return scatter_half(wire, h, view, plane[h], ready_of(lambda f: view(f, ALL)))

    def y_first():
        def at(i):
            return total.at[:, :, i, :, hi]

        ready_of = core_swap(
            wire, y, lambda i: src.at[:, :, i, theirs, hi], lambda i: rcore.at[:, :, i, :, hi]
        )

        def after():
            yield from ring_reduce(wire, y, on_y, at, ring, ready_of(at))

            def half(h):
                rows = pl.ds(48 * h, 48 - 16 * h)

                def view(f, s):
                    xi, zi = xz(h, f, s)
                    return total.at[xi, zi, y, rows, hi]

                return scatter_half(wire, h, view, late[h], lambda d: None)

            yield from lockstep([half(0), half(1)])

        return after()

    gens = [plane_first(0), plane_first(1), y_first()]
    yield
    load.wait()
    yield from lockstep(gens)
    piece = total.at[x, z]
    yield from ring_reduce(
        wire, y, on_y, lambda i: piece.at[i, :, lo], from_y, lambda d: None
    )
    out[x, z, mine] = total[x, z, y]

    def spread(h):
        rows = pl.ds(multiple((96 * c, 48 + 16 * c)[h], 16), 48 - 16 * h)

        def view(f, s):
            xi, zi = xz(h, f, s)
            return out.at[xi, zi, rows]

        def share(f, s, core):
            xi, zi = xz(h, f, s)
            begin = multiple((96 * core, 48 + 32 * core)[h], 16)
            return out.at[xi, zi, pl.ds(begin, 48 - 32 * h)]

        return gather_half(wire, h, view, share)

    yield from lockstep([spread(0), spread(1)])


ATTN_REDUCE_SHAPES = (
    ((4, 4, 80, 384),) * 2
    + ((3, 4, 80, 384),)
    + ((3, 48, 384), (3, 48, 384), (3, 32, 384), (3, 32, 384), (48, 384), (32, 384))
)


def attn_reduce_gen(wire, src, out, bufs):
    total, rcore, ring = bufs[:3]
    one, two, held = (bufs[3], bufs[5]), (bufs[4], bufs[6]), bufs[7:9]
    c = place()[2]
    y = lax.axis_index("dp")
    oth = {"ctx": other_core()}
    mine = row_split()[0]
    theirs = pl.ds(multiple(64 - 64 * c, 16), 80)
    total[...] = src[:, :, mine]

    def at(i):
        return total.at[:, i]

    ready_of = core_swap(wire, y, lambda i: src.at[:, i, theirs], lambda i: rcore.at[:, i])
    yield from ring_reduce(wire, y, on_y, at, ring, ready_of(at))

    def half(h):
        axes, (me, _) = halves(h)
        rows = pl.ds(48 * h, 48 - 16 * h)
        where = pl.ds(multiple(64 * c + 48 * h, 16), 48 - 16 * h)
        yield from ring_reduce(
            wire, me, lambda d: on_plane(axes[0], d), lambda i: total.at[i, y, rows], one[h],
            lambda d: None,
        )
        base = wire.take(3)
        for j, d in enumerate(DIRS):
            wire.go(total.at[me, y, rows], two[h].at[j], base + j, on_plane(axes[1], d))
        yield
        for j, d in enumerate(DIRS):
            wire.got(two[h].at[j], base + j, oth)
        sums = total[me, y, rows].astype(F32)
        for j in range(3):
            sums = sums + two[h][j].astype(F32)
        held[h][...] = sums.astype(BF)
        base = wire.take(3)
        out[me, where] = held[h][...]
        for j, d in enumerate(DIRS):
            wire.go(held[h], out.at[me, where], base + j, on_plane(axes[0], d))
        yield
        for j, d in enumerate(DIRS):
            wire.got(out.at[turn(me, -d), where], base + j, oth)

    yield from lockstep([half(0), half(1)])
    base = wire.take(1)

    def handed(core):
        return out.at[:, pl.ds(multiple(80 * core, 16), 64)]

    wire.go(handed(c), handed(c), base, oth)
    yield
    wire.got(handed(1 - c), base, oth)


def gains_gen(wire, steps, got):
    y = lax.axis_index("dp")
    base = wire.take(10)
    k = 0
    for stage in range(4):
        if stage < 2:
            there = [(d, {"ctx": neighbour(stage, d)}) for d in (1, -1, 2)]
        elif stage == 2:
            there = [(0, {"ctx": other_core()})]
        else:
            there = [(d, {"dp": turn(y, d)}) for d in (1, 2, 3)]
        for i, (d, dev) in enumerate(there):
            wire.go(steps.at[stage], got.at[k + i], base + k + i, dev)
        yield
        total = steps[stage]
        for i, (d, dev) in enumerate(there):
            wire.got(got.at[k + i], base + k + i, dev)
            total = total + got[k + i]
        steps[stage + 1] = total
        k += len(there)


def pack_weights(wq, wk, wv, wo, wg, wu, wd):
    def blocks(w):
        return w.reshape(LAYERS, 144, 4, 384).transpose(0, 2, 1, 3)

    attn = blocks(jnp.concatenate([wk, wv, wq, wo], axis=2))
    gate, up = blocks(wg), blocks(wu)
    down = wd.transpose(0, 2, 1).reshape(LAYERS, 4, 144, 384)
    return (
        attn[0],
        jnp.stack([gate[0], up[0], attn[1], down[0]]),
        jnp.stack([gate[1], up[1], up[1], down[1]]),
    )


def unpack_grads(early, late, attn0):
    attn = jnp.stack([attn0, late[2]]).astype(F32)

    def cols(v):
        return v.transpose(0, 2, 1, 3).reshape(LAYERS, 144, 1536)

    def both(i):
        return jnp.stack([late[i], early[i]]).astype(F32)

    attn = cols(attn)
    down = both(3).reshape(LAYERS, D, 384).transpose(0, 2, 1)
    return (
        attn[:, :, 384:960], attn[:, :, :192], attn[:, :, 192:384], attn[:, :, 960:],
        cols(both(0)), cols(both(1)), down,
    )


def body(
    tokens, out_grad, w_query, w_key, w_value, w_out, w_gate, w_up, w_down_, attn_gain, ffn_gain,
    block_pairs,
):
    me = lax.axis_index("ctx")
    y = lax.axis_index("dp")
    mine = block_pairs[me]
    offs = jnp.arange(64, dtype=jnp.int32)
    pos = jnp.concatenate([mine * 64 + offs, (63 - mine) * 64 + offs])
    freq = ROPE_BASE ** (-2.0 * jnp.arange(HD // 2, dtype=F32) / HD)
    ang = pos.astype(F32)[:, None] * freq[None, :]
    cos = jnp.cos(ang)
    sin = jnp.sin(ang)
    cos = jnp.concatenate([cos] * 4, axis=1)
    ssin = jnp.concatenate([-sin, sin, -sin, sin], axis=1)
    is_lo = block_pairs < mine
    is_hi = block_pairs > mine
    scal = jnp.stack([
        jnp.where(is_lo, 0.0, NEG), jnp.where(is_hi, 0.0, NEG),
        jnp.where(is_lo, 1.0, 0.0), jnp.where(is_lo | is_hi, 0.0, BIG),
    ]).astype(F32)
    lane = jnp.arange(128)[None, :]
    lo_col = jnp.repeat(is_lo, 64)[:, None]
    hi_col = jnp.repeat(is_hi, 64)[:, None]
    mask = jnp.where(lane < 64, lo_col, hi_col).astype(BF).reshape(8, 256, 128)
    ind = ((lane == 64) | ((lane == 65) & lo_col) | ((lane == 66) & hi_col)).astype(BF)
    ind = ind.reshape(8, 256, 128)

    win_a, win_b, win_m = pack_weights(w_query, w_key, w_value, w_out, w_gate, w_up, w_down_)
    gin = jnp.zeros((16, 256), BF)
    gin = gin.at[0:2, :144].set(attn_gain).at[2:4, :144].set(ffn_gain)
    h = tokens.astype(F32)
    common = (cos, ssin, mask, ind, scal)
    out0 = first_forward(h, win_a, win_b, gin, *common)
    saved0, (w_a, w_b, gains) = out0[:7], out0[7:]
    out1 = second_forward(saved0[0], w_b, win_m, gains, *common)
    saved1, w_m = out1[:7], out1[7]
    result = saved1[0].astype(BF)
    g = out_grad.astype(F32)
    tail = (gains, cos, ssin, mask, scal)
    g, ga1, gg1, early = first_backward((g, saved0[0]) + saved1[1:] + tail + (w_b[2], w_m))
    g, late, attn0, gg = second_backward((g, h) + saved0[1:] + tail + (w_a, w_b), ga1, gg1)
    grads = unpack_grads(early, late, attn0)
    gg = lax.dynamic_slice(gg, (0, y * 144), (4, 144))
    return (result, g) + grads + (gg[0::2], gg[1::2])


def solution(mesh):
    row = P(("dp", "ctx"), None)
    mat = P(None, "dp", None)
    vec = P(None, "dp")
    return jax.shard_map(
        body,
        mesh=mesh,
        in_specs=(row, row) + (mat,) * 7 + (vec, vec, P()),
        out_specs=(row, row) + (mat,) * 7 + (vec, vec),
        check_vma=False,
    )
```

```python
import functools

import jax
import jax.numpy as jnp
from jax import lax
from jax.experimental import pallas as pl
from jax.experimental.pallas import tpu as pltpu
from jax.sharding import PartitionSpec as P

HEADS = 9
KV = 3
HD = 64
LAYERS = 2
D = 576
FF = 1536
NX = 4
NZ = 4
NY = 4
NORM_EPS = 1e-05
ROPE_BASE = 100000.0
NEG = -1e30
BIG = 1e30
MESH = pl.DeviceIdType.MESH
ALL = slice(None)
F32 = jnp.float32
BF = jnp.bfloat16
VMEM_LIMIT = 60 * 1024 * 1024
DIRS = (2, 1, -1)
SEMS = 352


def place():
    ctx = lax.axis_index("ctx")
    return lax.div(ctx, 8), lax.rem(lax.div(ctx, 2), 4), lax.rem(ctx, 2)


def ctx_of(x, z, c):
    return (x * NZ + z) * 2 + c


def turn(i, d):
    return lax.rem(i + (d + 4), 4)


def neighbour(axis, d):
    x, z, c = place()
    return ctx_of(turn(x, d), z, c) if axis == 0 else ctx_of(x, turn(z, d), c)


def other_core():
    x, z, c = place()
    return ctx_of(x, z, 1 - c)


def partners(y_too):
    devs = [{"ctx": neighbour(axis, d)} for axis in (0, 1) for d in (1, -1, 2)]
    devs.append({"ctx": other_core()})
    if y_too:
        y = lax.axis_index("dp")
        devs += [{"dp": turn(y, d)} for d in (1, -1, 2)]
    return devs


def signal_all(sem, devs):
    for dev in devs:
        pl.semaphore_signal(sem, inc=1, device_id=dev, device_id_type=MESH)


def greet():
    barrier = pltpu.get_barrier_semaphore()
    devs = partners(True)
    signal_all(barrier, devs)
    pl.semaphore_wait(barrier, len(devs))


class Wire:
    def __init__(self, send, recv, used=None):
        self.send, self.recv, self.open = send, recv, []
        self.used = [0] if used is None else used

    def branch(self):
        return Wire(self.send, self.recv, self.used)

    def take(self, n):
        self.used[0] += n
        assert self.used[0] <= SEMS
        return self.used[0] - n

    def desc(self, src, dst, k, dev):
        return pltpu.make_async_remote_copy(
            src_ref=src,
            dst_ref=dst,
            send_sem=self.send.at[k],
            recv_sem=self.recv.at[k],
            device_id=dev,
            device_id_type=MESH,
        )

    def go(self, src, dst, k, dev):
        copy = self.desc(src, dst, k, dev)
        copy.start()
        self.open.append(copy)

    def got(self, dst, k, dev):
        self.desc(dst, dst, k, dev).wait_recv()

    def close(self):
        for copy in self.open:
            copy.wait_send()
        self.open = []


def lockstep(gens):
    gens = list(gens)
    while gens:
        left = []
        for g in gens:
            try:
                next(g)
                left.append(g)
            except StopIteration:
                pass
        gens = left
        yield


def run_all(gens):
    for _ in lockstep(gens):
        pass


def tick(gen):
    try:
        next(gen)
    except StopIteration:
        pass


def halves(h):
    x, z, _ = place()
    return ((0, 1), (x, z)) if h == 0 else ((1, 0), (z, x))


def xz(h, first, second):
    return (first, second) if h == 0 else (second, first)


def on_plane(axis, d):
    return {"ctx": neighbour(axis, d)}


def on_y(d):
    return {"dp": turn(lax.axis_index("dp"), d)}


def gather_half(wire, h, view, share_view):
    c = place()[2]
    axes, (me1, me2) = halves(h)
    oth = {"ctx": other_core()}
    near, far, core = wire.take(3), wire.take(12), wire.take(4)
    firsts = [me1] + [turn(me1, -d) for d in DIRS]

    def along(n):
        block = view(firsts[n], me2)
        for j, d in enumerate(DIRS):
            wire.go(block, block, far + 3 * n + j, on_plane(axes[1], d))

    own = view(me1, me2)
    for j, d in enumerate(DIRS):
        wire.go(own, own, near + j, on_plane(axes[0], d))
    along(0)
    yield
    for j in (1, 2, 0):
        wire.got(view(firsts[j + 1], me2), near + j, oth)
        along(j + 1)
    mine = share_view(ALL, me2, c)
    wire.go(mine, mine, core + 3, oth)
    yield
    for j in (1, 2, 0):
        second = turn(me2, -DIRS[j])
        for n in range(4):
            wire.got(view(firsts[n], second), far + 3 * n + j, oth)
        part = share_view(ALL, second, c)
        wire.go(part, part, core + j, oth)
    yield
    for j in range(4):
        second = turn(me2, -DIRS[j]) if j < 3 else me2
        wire.got(share_view(ALL, second, 1 - c), core + j, oth)


def add_into(dst, *srcs):
    if len(dst.shape) > 2:

        def step(i, carry):
            add_into(dst.at[i], *[s.at[i] for s in srcs])
            return carry

        if len(dst.shape) == 3:
            for i in range(dst.shape[0]):
                step(i, 0)
        else:
            lax.fori_loop(0, dst.shape[0], step, 0)
        return
    total = dst[...].astype(F32)
    for s in srcs:
        total = total + s[...].astype(F32)
    dst[...] = total.astype(dst.dtype)


def core_swap(wire, me, src, dst):
    base = wire.take(4)
    order = DIRS + (0,)
    oth = {"ctx": other_core()}
    for k, d in enumerate(order):
        wire.go(src(turn(me, d)), dst(turn(me, d)), base + k, oth)

    def ready_of(view):
        def ready(d):
            f = turn(me, d)
            wire.got(dst(f), base + order.index(d), oth)
            add_into(view(f), dst(f))

        return ready

    return ready_of


def ring_reduce(wire, me, dev, at, buf, ready):
    base = wire.take(3)
    for j, d in enumerate(DIRS):
        ready(d)
        wire.go(at(turn(me, d)), buf.at[j], base + j, dev(d))
    ready(0)
    yield
    for j, d in enumerate(DIRS):
        wire.got(buf.at[j], base + j, dev(d))
    add_into(at(me), buf.at[0], buf.at[1], buf.at[2])


def scatter_half(wire, h, view, bufs, ready):
    axes, pos = halves(h)
    yield from ring_reduce(
        wire, pos[0], lambda d: on_plane(axes[0], d), lambda i: view(i, ALL), bufs[0], ready
    )
    yield from ring_reduce(
        wire, pos[1], lambda d: on_plane(axes[1], d), lambda i: view(pos[0], i), bufs[1],
        lambda d: None,
    )


def lanes(shape):
    return lax.broadcasted_iota(jnp.int32, shape, len(shape) - 1)


def mm(a, b):
    return lax.dot_general(a, b, (((1,), (0,)), ((), ())), preferred_element_type=F32)


def mm_t(a, b):
    return lax.dot_general(a, b, (((1,), (1,)), ((), ())), preferred_element_type=F32)


def tmm(a, b):
    return lax.dot_general(a, b, (((0,), (0,)), ((), ())), preferred_element_type=F32)


def inv_rms(v):
    return lax.rsqrt(jnp.mean(v * v, axis=-1, keepdims=True) + NORM_EPS)


def norm_back(v, g, d):
    r = inv_rms(v)
    dv = r * g * d - v * (r * r * r * jnp.mean(g * d * v, axis=-1, keepdims=True))
    return dv, jnp.sum(d * v * r, axis=0, keepdims=True)


def rope(t, cos, ssin):
    first = lax.rem(lanes(t.shape), HD) < HD // 2
    turned = jnp.where(first, pltpu.roll(t, 96, 1), pltpu.roll(t, 32, 1))
    return t * cos + turned * ssin


def pair(t, half):
    lo, hi = t[:64], t[64:]
    first = lanes((64, 128)) < HD
    if half == 0:
        return jnp.where(first, lo, pltpu.roll(hi, HD, 1))
    return jnp.where(first, pltpu.roll(lo, HD, 1), hi)


def unpair(a, b):
    first = lanes((64, 128)) < HD
    lo = jnp.where(first, a, pltpu.roll(b, HD, 1))
    hi = jnp.where(first, pltpu.roll(a, HD, 1), b)
    return jnp.concatenate([lo, hi], axis=0)


def tile(v, i):
    return v[:, 128 * i : 128 * i + 128]


def doubled(p):
    first = lanes((192, 128)) < HD
    one = jnp.where(first, pltpu.roll(p, HD, 1), 0.0)
    zero = jnp.zeros((192, 128), F32)
    return jnp.concatenate(
        [jnp.concatenate([one, zero], axis=1), jnp.concatenate([zero, p], axis=1)], axis=0
    ).astype(BF)


def slot_row(scal, c, row_a, row_b):
    pick = jnp.full((1, 384), scal[2, c], F32) > 0.5
    own = jnp.full((1, 384), scal[3, c], F32)
    extra = jnp.where(lanes((1, 384)) >= 192, own, 0.0)
    return jnp.where(pick, row_a, row_b), extra


def rel(i):
    return turn(i - lax.axis_index("dp"), 4)


def w_mat(wv, kind, i):
    return jnp.concatenate([wv[kind, i, rel(j)] for j in range(NY)], axis=0)


def w_attn(wa, i):
    return jnp.concatenate([wa[i, rel(j)] for j in range(NY)], axis=0)


def w_down(wv, i):
    return wv[3, :, rel(i)].reshape(D, 384)


def load_mlp(src, wm, sems):
    return [pltpu.make_async_copy(src.at[k], wm.at[k], sems.at[k]) for k in (0, 1, 3)]


def multiple(v, n):
    return pl.multiple_of(v, n)


def kv_gather(wire, kv, k):
    c = place()[2]

    def gen(h):
        def view(first, second):
            xi, zi = xz(h, first, second)
            return kv.at[xi, zi, c, k, h]

        def share(first, second, core):
            xi, zi = xz(h, first, second)
            return kv.at[xi, zi, core, k, h]

        return gather_half(wire, h, view, share)

    return lockstep([gen(h) for h in (0, 1)])


def chunk_of(buf, ci, k, j):
    return buf[ci // 2, pl.ds(2 * (ci % 2), 2), :, k, j].reshape(256, 128)


def diag_keys(k):
    first = lanes((64, 128)) < HD
    zero = jnp.zeros((64, 128), k.dtype)
    both = jnp.concatenate([jnp.where(first, k, zero), jnp.where(first, zero, k)], axis=0)
    return both


def diag_bias():
    shape = (128, 384)
    key = lax.rem(lax.broadcasted_iota(jnp.int32, shape, 0), 64)
    q = lanes(shape)
    visible = (q >= 192) & (key <= lax.rem(q, 64))
    return jnp.where(visible, 0.0, NEG)


def row_split():
    c = place()[2]
    mine = pl.ds(multiple(64 * c, 16), 80)
    return mine, lambda core: pl.ds(multiple(80 * core, 16), 64)


def over_y(wire, src, view):
    mine, handed = row_split()
    c = place()[2]
    oth = {"ctx": other_core()}
    near, core = wire.take(3), wire.take(3)
    for j, d in enumerate(DIRS):
        wire.go(src(mine), view((4 - d) % 4, mine), near + j, on_y(d))
    yield
    for j in (1, 2, 0):
        k = (4 - DIRS[j]) % 4
        wire.got(view(k, mine), near + j, oth)
        part = view(k, handed(c))
        wire.go(part, part, core + j, oth)
    yield
    for j in range(3):
        wire.got(view((4 - DIRS[j]) % 4, handed(1 - c)), core + j, oth)


def attn_weights_gen(wire, win, wa, first, count):
    blocks = pl.ds(first, count)
    return over_y(
        wire, lambda rows: win.at[blocks, rows], lambda k, rows: wa.at[blocks, k, rows]
    )


def weights_around(wire, win, w):
    hi = pl.ds(256, 128)
    return over_y(
        wire, lambda rows: win.at[:, :, rows, hi], lambda k, rows: w.at[:, :, k, rows, hi]
    )


def weights_over(wire, win, w):
    x, z, _ = place()
    mine, handed = row_split()
    lo = pl.ds(0, 256)
    near = wire.take(3)
    for j, d in enumerate(DIRS):
        wire.go(win.at[x, z, mine, lo], w.at[x, z, (4 - d) % 4, mine, lo], near + j, on_y(d))
    yield
    for j, d in enumerate(DIRS):
        wire.got(w.at[x, z, (4 - d) % 4, mine, lo], near + j, on_y(d))

    def half(h):
        cols = pl.ds(128 * h, 128)

        def view(first, second):
            xi, zi = xz(h, first, second)
            return w.at[xi, zi, pl.ds(1, 3), mine, cols]

        def share(first, second, core):
            xi, zi = xz(h, first, second)
            return w.at[xi, zi, pl.ds(1, 3), handed(core), cols]

        return gather_half(wire, h, view, share)

    yield from lockstep([half(0), half(1)])


def gains_exchange(wire, gin, landing):
    base = wire.take(3)
    for j, d in enumerate(DIRS):
        wire.go(gin, landing.at[(4 - d) % 4], base + j, on_y(d))
    yield
    for j, d in enumerate(DIRS):
        wire.got(landing.at[(4 - d) % 4], base + j, on_y(d))


def gains_rows(gin, landing):
    total = jnp.zeros((16, 640), F32)
    landing[0] = gin[...]
    for j in range(NY):
        part = landing[rel(j)].astype(F32)
        part = jnp.concatenate([part, jnp.zeros((16, 384), F32)], axis=1)
        total = total + (pltpu.roll(part, 144 * j, 1) if j else part)
    return total


def forward_kernel(*refs):
    h_ref, win_a, win_b, win_m, gin = refs[:5]
    shared = refs[5:10]
    result = refs[10]
    saved0, saved1 = refs[11:17], refs[17:23]
    h1_ref, a_out, b_out, m_out, gains = refs[23:28]
    wa, wb, wm, s_scr, sd_scr, acc_scr, landing, send, recv, loc = refs[28:]
    own = [
        pltpu.make_async_copy(win_a, wa.at[:, 0], loc.at[0]),
        pltpu.make_async_copy(win_b, wb.at[:, :, 0], loc.at[1]),
        pltpu.make_async_copy(win_m, wm.at[:, :, 0], loc.at[2]),
    ]
    keep = [
        pltpu.make_async_copy(wa, a_out, loc.at[3]),
        pltpu.make_async_copy(wb, b_out, loc.at[4]),
        pltpu.make_async_copy(wm, m_out, loc.at[5]),
    ]
    for copy in own:
        copy.start()
    greet()
    wire = Wire(send, recv)
    early = attn_weights_gen(wire, win_a, wa, 0, 3)
    tick(early)
    slots = weights_over(wire, win_b, wb)
    tick(slots)
    last = attn_weights_gen(wire, win_a, wa, 3, 1)
    tick(last)
    run_all([early, gains_exchange(wire, gin, landing)])
    around = weights_around(wire, win_b, wb)
    tick(around)
    own[0].wait()
    gains[...] = gains_rows(gin, landing)
    slots1, around1 = weights_over(wire, win_m, wm), weights_around(wire, win_m, wm)
    work = (s_scr, sd_scr, acc_scr)

    def need_first():
        run_all([slots, around])
        own[1].wait()
        keep[0].start()
        keep[1].start()
        tick(slots1)
        tick(around1)

    def need_second():
        run_all([slots1, around1])
        own[2].wait()
        keep[2].start()

    h1 = forward_core(
        0, wire, lambda: tick(slots), lambda: run_all([last]), need_first, h_ref[...], gains, shared,
        saved0, wa, wb, work,
    )
    h1_ref[...] = h1
    h2 = forward_core(
        1, wire, lambda: tick(slots1), lambda: None, need_second, h1, gains, shared, saved1,
        wb.at[2], wm, work,
    )
    result[...] = h2.astype(BF)
    for copy in keep:
        copy.wait()
    wire.close()


def forward_core(layer, wire, later, need_out, need, h, gains, shared, saved, wa, wm, work):
    cos_ref, sin_ref, mask_ref, ind_ref, scal = shared
    mid_ref, attn_ref, qt_ref, kv, lse_ref, op_ref = saved
    s_scr, sd_scr, acc_scr = work
    x, z, c = place()
    x, z, c = place()
    n1 = (h * inv_rms(h) * gains[layer : layer + 1, :D]).astype(BF)
    cos, ssin = cos_ref[...], sin_ref[...]
    low = lanes((128, 128)) < HD
    kv_part = mm(n1, w_attn(wa, 0))
    t0, t1, t2 = [tile(kv_part, i) for i in range(3)]
    t0 = rope(t0, cos, ssin)
    t1 = jnp.where(low, rope(t1, cos, ssin), t1)
    k_pairs = [pair(t0, 0), pair(t0, 1), pair(t1, 0)]
    v_pairs = [pair(t1, 1), pair(t2, 0), pair(t2, 1)]
    spread = []
    for k in range(KV):
        kv[x, z, c, k, 0] = k_pairs[k].astype(BF)
        kv[x, z, c, k, 1] = v_pairs[k].astype(BF)
        spread.append(kv_gather(wire, kv, k))
        tick(spread[k])
    q_part = [mm(n1, w_attn(wa, i)) for i in (1, 2)]
    tiles = [rope(tile(q_part[i // 3], i % 3), cos, ssin) for i in range(5)]
    for k in range(KV):
        qp = jnp.concatenate(
            [pair(tiles[(3 * k + g) // 2], (3 * k + g) % 2) for g in range(3)], axis=0
        )
        qt_ref[k] = doubled(qp * 0.125)

    in_one = lanes((1, 384)) < 192
    bias = diag_bias()
    zero128 = jnp.zeros((128, 128), BF)
    runs = []
    for k in range(KV):
        keys = diag_keys(kv[x, z, c, k, 0])
        sd = mm_t(jnp.concatenate([zero128, keys], axis=1), qt_ref[k]) + bias
        sd_scr[k] = sd
        lo = jnp.max(sd[:64].reshape(8, 8, 384), axis=0)
        hi = jnp.max(sd[64:].reshape(8, 8, 384), axis=0)
        runs.append((jnp.full((8, 384), NEG, F32), lo, hi))
    dlane = lanes((128, 128))
    drow = lax.broadcasted_iota(jnp.int32, (128, 128), 0)
    dind = jnp.where(
        ((dlane == 65) & (drow < 64)) | ((dlane == 66) & (drow >= 64)), 1.0, 0.0
    ).astype(BF)
    first = lanes((256, 128)) < HD

    def scores(k):
        def step(pairi, carry):
            one, lo, hi = carry
            for ci in (2 * pairi, 2 * pairi + 1):
                keys = chunk_of(kv, ci, k, 0)
                s = mm_t(jnp.concatenate([keys, keys * mask_ref[ci]], axis=1), qt_ref[k])
                s_scr[ci] = s
                for i in range(4):
                    top = jnp.max(s[64 * i : 64 * i + 64].reshape(8, 8, 384), axis=0)
                    slot = 4 * ci + i
                    one = jnp.maximum(one, top)
                    lo = jnp.maximum(lo, top + scal[0, slot])
                    hi = jnp.maximum(hi, top + scal[1, slot])
            return one, lo, hi

        got = lax.fori_loop(0, 4, step, runs[k])
        one, lo, hi = [jnp.max(r, axis=0, keepdims=True) for r in got]
        top = jnp.where(in_one, one, hi)
        top = jnp.maximum(top, pltpu.roll(top, 192, 1))
        return jnp.where(in_one, top, lo), top

    def values(k, row_a, row_b):
        sd = sd_scr[k]
        p = jnp.concatenate([jnp.exp(sd[:64] - row_a), jnp.exp(sd[64:] - row_b)], axis=0)
        vals = jnp.concatenate([dind, diag_keys(kv[x, z, c, k, 1])], axis=1)
        acc_scr[k] = tmm(vals, p.astype(BF))

        def step(pairi, carry):
            total = acc_scr[k]
            for ci in (2 * pairi, 2 * pairi + 1):
                s = s_scr[ci]
                parts = []
                for i in range(4):
                    base, extra = slot_row(scal, 4 * ci + i, row_a, row_b)
                    parts.append(jnp.exp(s[64 * i : 64 * i + 64] - (base + extra)))
                p = jnp.concatenate(parts, axis=0).astype(BF)
                v = chunk_of(kv, ci, k, 1)
                vals = jnp.concatenate(
                    [jnp.where(first, v, ind_ref[ci]), v * mask_ref[ci]], axis=1
                )
                total = total + tmm(vals, p)
            acc_scr[k] = total
            return carry

        lax.fori_loop(0, 4, step, 0)

    for k in range(KV):
        tick(spread[k])
    later()
    row_a, row_b = [], []
    run_all([spread[0]])
    later()
    for k in range(KV):
        if k + 1 < KV:
            tick(spread[k + 1])
        a, b = scores(k)
        row_a.append(a)
        row_b.append(b)
        if k + 1 < KV:
            run_all([spread[k + 1]])
        values(k, a, b)

    pairs = []
    for k in range(KV):
        acc = acc_scr[k]
        rolled = pltpu.roll(acc, 192, 1)
        hi = acc[0:64] + rolled[192:256]
        lo = rolled[128:192]
        tot_hi = acc[64:65] + rolled[66:67]
        tot_lo = rolled[65:66]
        lse_hi = row_b[k] + jnp.log(jnp.where(in_one, tot_hi, 1.0))
        lse_hi = jnp.where(in_one, lse_hi, pltpu.roll(lse_hi, 192, 1))
        lse_lo = pltpu.roll(row_a[k], 192, 1) + jnp.log(jnp.where(in_one, tot_lo, 1.0))
        lse_ref[k, 0:1] = jnp.where(in_one, lse_hi, pltpu.roll(lse_lo, 192, 1))
        lse_ref[k, 1:2] = lse_hi
        lse_ref[k, 2:8] = jnp.zeros((6, 384), F32)
        out_t = jnp.concatenate(
            [lo / jnp.where(in_one, tot_lo, 1.0), hi / jnp.where(in_one, tot_hi, 1.0)], axis=0
        )
        p = jnp.transpose(out_t)[:192]
        op_ref[k] = p
        pairs += [p[64 * g : 64 * g + 64] for g in range(3)]
    pairs.append(jnp.zeros((64, 128), F32))
    attn = jnp.concatenate(
        [unpair(pairs[2 * t], pairs[2 * t + 1]) for t in range(5)], axis=1
    ).astype(BF)
    attn_ref[...] = attn
    a = attn[:, :D]
    need_out()
    proj = jnp.concatenate([mm(a, w_attn(wa, 2)), mm(a, w_attn(wa, 3))], axis=1)
    mid = h + pltpu.roll(proj, D, 1)[:, :D]
    mid_ref[...] = mid
    n2 = (mid * inv_rms(mid) * gains[2 + layer : 3 + layer, :D]).astype(BF)
    need()
    for i in range(4):
        gate = mm(n2, w_mat(wm, 0, i))
        up = mm(n2, w_mat(wm, 1, i))
        inner = (gate * jax.nn.sigmoid(gate) * up).astype(BF)
        mid = mid + mm_t(inner, w_down(wm, i))
    return mid


SAVED = (
    jax.ShapeDtypeStruct((128, D), F32),
    jax.ShapeDtypeStruct((128, 640), BF),
    jax.ShapeDtypeStruct((KV, 384, 256), BF),
    jax.ShapeDtypeStruct((NX, NZ, 2, KV, 2, 64, 128), BF),
    jax.ShapeDtypeStruct((KV, 8, 384), F32),
    jax.ShapeDtypeStruct((KV, 192, 128), F32),
)
FORWARD_SCRATCH = (
    ((4, 4, 144, 384), BF),
    ((4, 4, 4, 144, 384), BF),
    ((4, 4, 4, 144, 384), BF),
    ((8, 256, 384), F32),
    ((KV, 128, 384), F32),
    ((KV, 256, 384), F32),
    ((NY, 16, 256), BF),
)
GATHERED = jax.ShapeDtypeStruct((NX, NZ, NY, 144, 384), BF)
ATTN_GATHERED = jax.ShapeDtypeStruct((4, NY, 144, 384), BF)


def specs():
    return (
        pl.BlockSpec(memory_space=pltpu.VMEM),
        pl.BlockSpec(memory_space=pl.ANY),
        pl.BlockSpec(memory_space=pltpu.SMEM),
    )


def sems(*counts):
    return [pltpu.SemaphoreType.DMA((n,)) for n in counts]


def params(cid):
    return pltpu.CompilerParams(
        collective_id=cid, has_side_effects=True, vmem_limit_bytes=VMEM_LIMIT
    )


def forward(h, win_a, win_b, win_m, gin, cos, ssin, mask, ind, scal):
    vm, anyw, sm = specs()
    return pl.pallas_call(
        forward_kernel,
        out_shape=(jax.ShapeDtypeStruct((128, D), BF),) + SAVED * 2
        + (jax.ShapeDtypeStruct((128, D), F32), ATTN_GATHERED, GATHERED, GATHERED,
           jax.ShapeDtypeStruct((16, 640), F32)),
        in_specs=[vm, anyw, anyw, anyw, vm, vm, vm, vm, vm, sm],
        out_specs=(vm,) * 14 + (anyw, anyw, anyw, vm),
        scratch_shapes=[pltpu.VMEM(*v) for v in FORWARD_SCRATCH] + sems(SEMS, SEMS, 6),
        compiler_params=params(0),
        name="forward",
    )(h, win_a, win_b, win_m, gin, cos, ssin, mask, ind, scal)


def transposed(v, wide):
    wide[:, :D] = v.astype(F32)
    return jnp.transpose(wide[...])[:D].astype(BF)


def backward_kernel(*refs):
    g_ref, gains, cos_ref, sin_ref, mask_ref, scal = refs[:6]
    saved0, saved1 = refs[6:13], refs[13:20]
    a_any, b_any, m_any = refs[20:23]
    dh_ref, summed1, summed0, summed_a, gains_out = refs[23:28]
    rest = refs[28:]
    work, rest = rest[:N_WORK], rest[N_WORK:]
    wa0, wa1, kv, gm, ga0, ga1, gg0, gg1, steps, got = rest[:10]
    bufs, late = rest[10 : 10 + N_REDUCE], rest[10 + N_REDUCE : -5]
    kv_free, batch_free, send, recv, loc = rest[-5:]
    shared = (gains, cos_ref, sin_ref, mask_ref, scal)
    wm = work[0]
    attn_loads = [
        pltpu.make_async_copy(b_any.at[2], wa1, loc.at[4]),
        pltpu.make_async_copy(a_any, wa0, loc.at[5]),
    ]
    mlp1, mlp0 = load_mlp(m_any, wm, loc), load_mlp(b_any, wm, loc)
    kv1 = pltpu.make_async_copy(saved1[3], kv, loc.at[6])
    kv0 = pltpu.make_async_copy(saved0[3], kv, loc.at[6])
    for copy in mlp1 + [attn_loads[0], kv1, attn_loads[1]]:
        copy.start()
    greet()
    wire = Wire(send, recv)
    back = wire.branch()
    gm[2] = jnp.zeros((4, 4, 144, 384), BF)
    first = reduce_gen(back, gm, summed1, bufs, loc.at[7])
    second = reduce_gen(back, gm, summed0, bufs, loc.at[8])

    def after_mlp1():
        tick(first)
        for copy in mlp0:
            copy.start()

    def step1(point, i):
        if point in ("attn", "heads", "sums"):
            tick(first)

    def ready1():
        attn_loads[0].wait()

    def after_heads1():
        kv0.start()

    for copy in mlp1:
        copy.wait()
    g1 = backward_core(
        1, wire, step1, after_mlp1, ready1, kv1.wait, lambda k: None, after_heads1,
        g_ref[...], saved1[:3] + saved1[4:], kv, shared, wa1, gm, ga1, gg1, work,
    )
    signal_all(kv_free, partners(False))
    wire.close()
    back.close()
    for copy in mlp0:
        copy.wait()

    def after_mlp0():
        gm[2] = ga1[...]

    def step0(point, i):
        if point == "mlp" and i in (0, 2):
            tick(first)
        if point == "attn":
            run_all([first])
            back.close()
            signal_all(batch_free, partners(True))
            pl.semaphore_wait(batch_free, len(partners(True)))
            tick(second)
        if (point == "head" and i == 0) or point in ("heads", "sums"):
            tick(second)

    def before_reduce(k):
        if k == 0:
            pl.semaphore_wait(kv_free, len(partners(False)))

    g0 = backward_core(
        0, wire, step0, after_mlp0, attn_loads[1].wait, kv0.wait, before_reduce, lambda: None,
        g1, saved0[:3] + saved0[4:], kv, shared, wa0, gm, ga0, gg0, work,
    )
    dh_ref[...] = g0
    steps[0] = jnp.zeros((8, 640), F32)
    steps[0, 0:2, :D] = gg0[0:2]
    steps[0, 2:4, :D] = gg1[0:2]
    run_all([attn_reduce_gen(wire, ga0, summed_a, late), gains_gen(wire, steps, got), second])
    gains_out[...] = steps[4]
    wire.close()
    back.close()


def backward_core(
    layer, wire, step_batch, after_mlp, need_attn, need_kv, before_reduce, after_heads,
    g, saved, kv, shared, wa, gm, ga, gg_ref, work,
):
    h_ref, mid_ref, attn_ref, qt_ref, lse_ref, op_ref = saved
    gains, cos_ref, sin_ref, mask_ref, scal = shared
    wm, dot_scr, dq_scr, pbuf, rcore, kv_one, kv_two, wide = work
    x, z, c = place()
    wide[...] = jnp.zeros((128, 640), F32)
    mid = mid_ref[...]
    gain2 = gains[2 + layer : 3 + layer, :D]
    n2 = (mid * inv_rms(mid) * gain2).astype(BF)
    n2_t = transposed(n2, wide)
    branch = g.astype(BF)
    branch_t = transposed(branch, wide)
    d_n2 = jnp.zeros((128, D), F32)
    for i in range(4):
        gate_w, up_w, down_w = w_mat(wm, 0, i), w_mat(wm, 1, i), w_down(wm, i)
        gate = mm(n2, gate_w)
        up = mm(n2, up_w)
        sig = jax.nn.sigmoid(gate)
        act = gate * sig
        inner = (act * up).astype(BF)
        d_inner = mm(branch, down_w)
        d_gate = (d_inner * up * (sig + act * (1.0 - sig))).astype(BF)
        d_up = (d_inner * act).astype(BF)
        gm[0, i] = mm(n2_t, d_gate).astype(BF).reshape(4, 144, 384)
        gm[1, i] = mm(n2_t, d_up).astype(BF).reshape(4, 144, 384)
        gm[3, :, i] = mm(branch_t, inner).astype(BF).reshape(4, 144, 384)
        d_n2 = d_n2 + mm_t(d_gate, gate_w) + mm_t(d_up, up_w)
        step_batch("mlp", i)
    after_mlp()
    d_hn, gg2 = norm_back(mid, gain2, d_n2)
    d_mid = g + d_hn
    gg_ref[1:2] = gg2
    gg_ref[2:8] = jnp.zeros((6, D), F32)
    need_attn()
    wide[:, :D] = d_mid
    dm = jnp.concatenate([wide[...], jnp.zeros((128, 128), F32)], axis=1)
    dm = pltpu.roll(dm, 192, 1).astype(BF)
    d_attn = mm_t(dm[:, :384], w_attn(wa, 2)) + mm_t(dm[:, 384:], w_attn(wa, 3))
    wide[:, :D] = d_attn
    attn_t = jnp.transpose(attn_ref[...].astype(F32))[:D].astype(BF)
    g_out = mm(attn_t, dm)
    ga[3] = g_out[:, 384:].astype(BF).reshape(4, 144, 384)
    ga[2] = g_out[:, :384].astype(BF).reshape(4, 144, 384)
    da = wide[...].astype(BF).astype(F32)
    da_tiles = [tile(da, i) for i in range(5)]
    step_batch("attn", 0)

    in_one = lanes((1, 384)) < 192
    pick_lo = jnp.where(
        lanes((16, 128)) < HD,
        jnp.where(lax.broadcasted_iota(jnp.int32, (16, 128), 0) == 0, 1.0, 0.0),
        jnp.where(lax.broadcasted_iota(jnp.int32, (16, 128), 0) == 1, 1.0, 0.0),
    ).astype(BF)
    delta_a, delta_b = [], []
    for k in range(KV):
        dp = jnp.concatenate(
            [pair(da_tiles[(3 * k + q) // 2], (3 * k + q) % 2) for q in range(3)], axis=0
        )
        dot_scr[k] = doubled(dp)
        prod = dp * op_ref[k]
        prod = jnp.concatenate([prod, prod], axis=0)
        coarse = prod.astype(BF)
        fine = (prod - coarse.astype(F32)).astype(BF)
        rows = mm_t(pick_lo, coarse) + mm_t(pick_lo, fine)
        lo, hi = rows[0:1], rows[1:2]
        delta_a.append(jnp.where(in_one, hi, lo))
        delta_b.append(hi)

    def back(k, keys2, vals2, subs, deltas, bias):
        s = mm_t(keys2, qt_ref[k])
        if bias is not None:
            s = s + bias
        dp = mm_t(vals2, dot_scr[k])
        probs, d_s = [], []
        for i, (sub, delta) in enumerate(zip(subs, deltas)):
            p = jnp.exp(s[64 * i : 64 * i + 64] - sub)
            probs.append(p.astype(BF))
            d_s.append((p * (dp[64 * i : 64 * i + 64] - delta)).astype(BF))
        probs = jnp.concatenate(probs, axis=0)
        d_s = jnp.concatenate(d_s, axis=0)
        return mm(d_s, qt_ref[k]), mm(probs, dot_scr[k]), tmm(keys2, d_s)

    need_kv()
    bias = diag_bias()
    zero128 = jnp.zeros((128, 128), BF)
    first = lanes((64, 128)) < HD
    wide_first = lanes((256, 128)) < HD

    def head(k):
        own = []
        dk, dv, dq = back(
            k,
            jnp.concatenate([zero128, diag_keys(kv[x, z, c, k, 0])], axis=1),
            jnp.concatenate([zero128, diag_keys(kv[x, z, c, k, 1])], axis=1),
            [lse_ref[k, 0:1], lse_ref[k, 1:2]],
            [delta_a[k], delta_b[k]],
            bias,
        )
        for d in (dk, dv):
            own.append(jnp.where(first, d[:64, 128:], d[64:, 128:]))
        dq_scr[k] = dq

        def step(pairi, carry):
            total = dq_scr[k]
            for ci in (2 * pairi, 2 * pairi + 1):
                m = mask_ref[ci]
                keys, vals = chunk_of(kv, ci, k, 0), chunk_of(kv, ci, k, 1)
                subs, deltas = [], []
                for i in range(4):
                    base, extra = slot_row(scal, 4 * ci + i, lse_ref[k, 0:1], lse_ref[k, 1:2])
                    subs.append(base + extra)
                    deltas.append(slot_row(scal, 4 * ci + i, delta_a[k], delta_b[k])[0])
                dk, dv, dq = back(
                    k,
                    jnp.concatenate([keys, keys * m], axis=1),
                    jnp.concatenate([vals, vals * m], axis=1),
                    subs,
                    deltas,
                    None,
                )
                mf = m.astype(F32)
                for j, d in enumerate((dk, dv)):
                    both = jnp.where(wide_first, d[:, :128], 0.0) + mf * d[:, 128:]
                    both = both.astype(BF).reshape(2, 2, 64, 128)
                    pbuf[pairi, pl.ds(2 * (ci - 2 * pairi), 2), :, k, j] = both
                total = total + dq
            dq_scr[k] = total
            return carry

        lax.fori_loop(0, 4, step, 0)
        for j in (0, 1):
            part = pbuf.at[x, z, c, k, j]
            part[...] = (part[...].astype(F32) + own[j]).astype(BF)

    def kv_reduce(k, h):
        me = halves(h)[1][0]

        def view(f, s):
            xi, zi = xz(h, f, s)
            return pbuf.at[xi, zi, c, k, h]

        def src(f):
            xi, zi = xz(h, f, ALL)
            return pbuf.at[xi, zi, 1 - c, k, h]

        def dst(f):
            xi, zi = xz(h, f, ALL)
            return rcore.at[xi, zi, k, h]

        ready_of = core_swap(wire, me, src, dst)
        return scatter_half(
            wire, h, view, (kv_one.at[k, h], kv_two.at[k, h]), ready_of(lambda f: view(f, ALL))
        )

    sums = []
    for k in range(KV):
        head(k)
        before_reduce(k)
        step_batch("head", k)
        sums.append(lockstep([kv_reduce(k, j) for j in (0, 1)]))
        for gen in sums:
            tick(gen)
    after_heads()
    step_batch("heads", 0)

    h = h_ref[...]
    gain1 = gains[layer : layer + 1, :D]
    n1 = (h * inv_rms(h) * gain1).astype(BF)
    n1_t = transposed(n1, wide)
    cos, ssin = cos_ref[...], -sin_ref[...]
    pairs = []
    for k in range(KV):
        dq = dq_scr[k]
        rolled = pltpu.roll(dq, 192, 1)
        out_t = jnp.concatenate([rolled[128:192], dq[0:64] + rolled[192:256]], axis=0)
        p = jnp.transpose(out_t)[:192]
        pairs += [p[64 * q : 64 * q + 64] for q in range(3)]
    pairs.append(jnp.zeros((64, 128), F32))
    q_tiles = [
        (rope(unpair(pairs[2 * t], pairs[2 * t + 1]), cos, ssin) * 0.125).astype(BF)
        for t in range(5)
    ]
    q_tiles.append(jnp.zeros((128, 128), BF))
    d_n1 = jnp.zeros((128, D), F32)

    def attn_block(i, d):
        grad = mm(n1_t, d)
        if i == 2:
            grad = grad + ga[2].reshape(D, 384).astype(F32)
        ga[i] = grad.astype(BF).reshape(4, 144, 384)
        return mm_t(d, w_attn(wa, i))

    for i in (1, 2):
        d_n1 = d_n1 + attn_block(i, jnp.concatenate(q_tiles[3 * i - 3 : 3 * i], axis=1))
    run_all(sums)
    step_batch("sums", 0)
    done = [[pbuf[x, z, c, k, j].astype(F32) for j in (0, 1)] for k in range(KV)]
    low = lanes((128, 128)) < HD
    t0 = rope(unpair(done[0][0], done[1][0]), cos, ssin)
    t1 = unpair(done[2][0], done[0][1])
    t1 = jnp.where(low, rope(t1, cos, ssin), t1)
    t2 = unpair(done[1][1], done[2][1])
    d_n1 = d_n1 + attn_block(0, jnp.concatenate([t0, t1, t2], axis=1).astype(BF))
    d_h, gg1 = norm_back(h, gain1, d_n1)
    gg_ref[0:1] = gg1
    return d_mid + d_h


BACKWARD_SCRATCH = (
    ((4, 4, 4, 144, 384), BF),
    ((KV, 384, 256), BF),
    ((KV, 256, 384), F32),
    ((NX, NZ, 2, KV, 2, 64, 128), BF),
    ((NX, NZ, KV, 2, 64, 128), BF),
    ((KV, 2, 3, 4, 64, 128), BF),
    ((KV, 2, 3, 64, 128), BF),
    ((128, 640), F32),
)
N_WORK = len(BACKWARD_SCRATCH)
SUMMED = jax.ShapeDtypeStruct((NX, NZ, 144, 384), BF)


def vmems(shapes):
    return [pltpu.VMEM(v, BF) for v in shapes]


def backward(g, gains, cos, ssin, mask, scal, saved0, saved1, w_a, w_b, w_m):
    vm, anyw, sm = specs()
    scratch = [pltpu.VMEM(*v) for v in BACKWARD_SCRATCH]
    scratch += vmems([(4, 4, 144, 384)] * 2)
    scratch += vmems([(NX, NZ, 2, KV, 2, 64, 128), (4, 4, 4, 144, 384)])
    scratch += vmems([(4, 4, 144, 384)] * 2)
    scratch += [pltpu.VMEM((8, D), F32)] * 2
    scratch += [pltpu.VMEM((5, 8, 640), F32), pltpu.VMEM((10, 8, 640), F32)]
    scratch += vmems(REDUCE_SHAPES) + vmems(ATTN_REDUCE_SHAPES)
    scratch += [pltpu.SemaphoreType.REGULAR] * 2
    kept = [vm, vm, vm, anyw, vm, vm, vm]
    order = lambda v: (v[0], v[1], v[2], v[4], v[3], v[5], v[6])
    return pl.pallas_call(
        backward_kernel,
        out_shape=(
            jax.ShapeDtypeStruct((128, D), F32), SUMMED, SUMMED,
            jax.ShapeDtypeStruct((4, 144, 384), BF), jax.ShapeDtypeStruct((8, 640), F32),
        ),
        in_specs=[vm] * 5 + [sm] + kept + kept + [anyw] * 3,
        out_specs=(vm,) * 5,
        scratch_shapes=scratch + sems(SEMS, SEMS, 9),
        compiler_params=params(1),
        name="backward",
    )(g, gains, cos, ssin, mask, scal, *order(saved0), *order(saved1), w_a, w_b, w_m)


REDUCE_SHAPES = (
    ((4, 4, 4, 80, 384),) * 2
    + ((3, 4, 2, 80, 256), (3, 2, 80, 256)) * 2
    + ((3, 4, 4, 80, 128),)
    + ((3, 4, 48, 128), (3, 48, 128), (3, 4, 32, 128), (3, 32, 128))
    + ((3, 80, 256),)
)
N_REDUCE = len(REDUCE_SHAPES)


def reduce_gen(wire, src, out, bufs, sem):
    total, rcore = bufs[0], bufs[1]
    plane, ring, late, from_y = (bufs[2:4], bufs[4:6]), bufs[6], (bufs[7:9], bufs[9:11]), bufs[11]
    x, z, c = place()
    y = lax.axis_index("dp")
    mine = row_split()[0]
    theirs = pl.ds(multiple(64 - 64 * c, 16), 80)
    hi, lo = pl.ds(256, 128), pl.ds(0, 256)
    load = pltpu.make_async_copy(src.at[:, :, :, mine], total, sem)
    load.start()

    def plane_first(h):
        ys = pl.ds(2 * h, 2)

        def view(f, s):
            xi, zi = xz(h, f, s)
            return total.at[xi, zi, ys, :, lo]

        def give(f):
            xi, zi = xz(h, f, ALL)
            return src.at[xi, zi, ys, theirs, lo]

        def dst(f):
            xi, zi = xz(h, f, ALL)
            return rcore.at[xi, zi, ys, :, lo]

        ready_of = core_swap(wire, halves(h)[1][0], give, dst)
        return scatter_half(wire, h, view, plane[h], ready_of(lambda f: view(f, ALL)))

    def y_first():
        def at(i):
            return total.at[:, :, i, :, hi]

        ready_of = core_swap(
            wire, y, lambda i: src.at[:, :, i, theirs, hi], lambda i: rcore.at[:, :, i, :, hi]
        )

        def after():
            yield from ring_reduce(wire, y, on_y, at, ring, ready_of(at))

            def half(h):
                rows = pl.ds(48 * h, 48 - 16 * h)

                def view(f, s):
                    xi, zi = xz(h, f, s)
                    return total.at[xi, zi, y, rows, hi]

                return scatter_half(wire, h, view, late[h], lambda d: None)

            yield from lockstep([half(0), half(1)])

        return after()

    gens = [plane_first(0), plane_first(1), y_first()]
    yield
    load.wait()

    def plane_then_y():
        yield from lockstep(gens[:2])
        yield from ring_reduce(
            wire, y, on_y, lambda i: total.at[x, z, i, :, lo], from_y, lambda d: None
        )

    yield from lockstep([plane_then_y(), gens[2]])
    out[x, z, mine] = total[x, z, y]

    def spread(h):
        rows = pl.ds(multiple((96 * c, 48 + 16 * c)[h], 16), 48 - 16 * h)

        def view(f, s):
            xi, zi = xz(h, f, s)
            return out.at[xi, zi, rows]

        def share(f, s, core):
            xi, zi = xz(h, f, s)
            begin = multiple((96 * core, 48 + 32 * core)[h], 16)
            return out.at[xi, zi, pl.ds(begin, 48 - 32 * h)]

        return gather_half(wire, h, view, share)

    yield from lockstep([spread(0), spread(1)])


ATTN_REDUCE_SHAPES = (
    ((4, 4, 80, 384),) * 2
    + ((3, 4, 80, 384),)
    + ((3, 48, 384), (3, 48, 384), (3, 32, 384), (3, 32, 384), (48, 384), (32, 384))
)


def attn_reduce_gen(wire, src, out, bufs):
    total, rcore, ring = bufs[:3]
    one, two, held = (bufs[3], bufs[5]), (bufs[4], bufs[6]), bufs[7:9]
    c = place()[2]
    y = lax.axis_index("dp")
    oth = {"ctx": other_core()}
    mine = row_split()[0]
    theirs = pl.ds(multiple(64 - 64 * c, 16), 80)
    total[...] = src[:, :, mine]

    def at(i):
        return total.at[:, i]

    ready_of = core_swap(wire, y, lambda i: src.at[:, i, theirs], lambda i: rcore.at[:, i])
    yield from ring_reduce(wire, y, on_y, at, ring, ready_of(at))

    def half(h):
        axes, (me, _) = halves(h)
        rows = pl.ds(48 * h, 48 - 16 * h)
        where = pl.ds(multiple(64 * c + 48 * h, 16), 48 - 16 * h)
        yield from ring_reduce(
            wire, me, lambda d: on_plane(axes[0], d), lambda i: total.at[i, y, rows], one[h],
            lambda d: None,
        )
        base = wire.take(3)
        for j, d in enumerate(DIRS):
            wire.go(total.at[me, y, rows], two[h].at[j], base + j, on_plane(axes[1], d))
        yield
        for j, d in enumerate(DIRS):
            wire.got(two[h].at[j], base + j, oth)
        sums = total[me, y, rows].astype(F32)
        for j in range(3):
            sums = sums + two[h][j].astype(F32)
        held[h][...] = sums.astype(BF)
        base = wire.take(3)
        out[me, where] = held[h][...]
        for j, d in enumerate(DIRS):
            wire.go(held[h], out.at[me, where], base + j, on_plane(axes[0], d))
        yield
        for j, d in enumerate(DIRS):
            wire.got(out.at[turn(me, -d), where], base + j, oth)

    yield from lockstep([half(0), half(1)])
    base = wire.take(1)

    def handed(core):
        return out.at[:, pl.ds(multiple(80 * core, 16), 64)]

    wire.go(handed(c), handed(c), base, oth)
    yield
    wire.got(handed(1 - c), base, oth)


def gains_gen(wire, steps, got):
    y = lax.axis_index("dp")
    base = wire.take(10)
    k = 0
    for stage in range(4):
        if stage < 2:
            there = [(d, {"ctx": neighbour(stage, d)}) for d in (1, -1, 2)]
        elif stage == 2:
            there = [(0, {"ctx": other_core()})]
        else:
            there = [(d, {"dp": turn(y, d)}) for d in (1, 2, 3)]
        for i, (d, dev) in enumerate(there):
            wire.go(steps.at[stage], got.at[k + i], base + k + i, dev)
        yield
        total = steps[stage]
        for i, (d, dev) in enumerate(there):
            wire.got(got.at[k + i], base + k + i, dev)
            total = total + got[k + i]
        steps[stage + 1] = total
        k += len(there)


def pack_weights(wq, wk, wv, wo, wg, wu, wd):
    def blocks(w):
        return w.reshape(LAYERS, 144, 4, 384).transpose(0, 2, 1, 3)

    attn = blocks(jnp.concatenate([wk, wv, wq, wo], axis=2))
    gate, up = blocks(wg), blocks(wu)
    down = wd.transpose(0, 2, 1).reshape(LAYERS, 4, 144, 384)
    return (
        attn[0],
        jnp.stack([gate[0], up[0], attn[1], down[0]]),
        jnp.stack([gate[1], up[1], up[1], down[1]]),
    )


def unpack_grads(early, late, attn0):
    attn = jnp.stack([attn0, late[2]]).astype(F32)

    def cols(v):
        return v.transpose(0, 2, 1, 3).reshape(LAYERS, 144, 1536)

    def both(i):
        return jnp.stack([late[i], early[i]]).astype(F32)

    attn = cols(attn)
    down = both(3).reshape(LAYERS, D, 384).transpose(0, 2, 1)
    return (
        attn[:, :, 384:960], attn[:, :, :192], attn[:, :, 192:384], attn[:, :, 960:],
        cols(both(0)), cols(both(1)), down,
    )


def body(
    tokens, out_grad, w_query, w_key, w_value, w_out, w_gate, w_up, w_down_, attn_gain, ffn_gain,
    block_pairs,
):
    me = lax.axis_index("ctx")
    y = lax.axis_index("dp")
    mine = block_pairs[me]
    offs = jnp.arange(64, dtype=jnp.int32)
    pos = jnp.concatenate([mine * 64 + offs, (63 - mine) * 64 + offs])
    freq = ROPE_BASE ** (-2.0 * jnp.arange(HD // 2, dtype=F32) / HD)
    ang = pos.astype(F32)[:, None] * freq[None, :]
    cos = jnp.cos(ang)
    sin = jnp.sin(ang)
    cos = jnp.concatenate([cos] * 4, axis=1)
    ssin = jnp.concatenate([-sin, sin, -sin, sin], axis=1)
    is_lo = block_pairs < mine
    is_hi = block_pairs > mine
    scal = jnp.stack([
        jnp.where(is_lo, 0.0, NEG), jnp.where(is_hi, 0.0, NEG),
        jnp.where(is_lo, 1.0, 0.0), jnp.where(is_lo | is_hi, 0.0, BIG),
    ]).astype(F32)
    lane = jnp.arange(128)[None, :]
    lo_col = jnp.repeat(is_lo, 64)[:, None]
    hi_col = jnp.repeat(is_hi, 64)[:, None]
    mask = jnp.where(lane < 64, lo_col, hi_col).astype(BF).reshape(8, 256, 128)
    ind = ((lane == 64) | ((lane == 65) & lo_col) | ((lane == 66) & hi_col)).astype(BF)
    ind = ind.reshape(8, 256, 128)

    win_a, win_b, win_m = pack_weights(w_query, w_key, w_value, w_out, w_gate, w_up, w_down_)
    gin = jnp.zeros((16, 256), BF)
    gin = gin.at[0:2, :144].set(attn_gain).at[2:4, :144].set(ffn_gain)
    h = tokens.astype(F32)
    common = (cos, ssin, mask, ind, scal)
    out = forward(h, win_a, win_b, win_m, gin, *common)
    result, saved0, saved1, h1, w_a, w_b, w_m, gains = (
        out[0], out[1:7], out[7:13], out[13], out[14], out[15], out[16], out[17]
    )
    g, early, late, attn0, gg = backward(
        out_grad.astype(F32), gains, cos, ssin, mask, scal, (h,) + saved0, (h1,) + saved1,
        w_a, w_b, w_m,
    )
    grads = unpack_grads(early, late, attn0)
    gg = lax.dynamic_slice(gg, (0, y * 144), (4, 144))
    return (result, g) + grads + (gg[0::2], gg[1::2])


def solution(mesh):
    row = P(("dp", "ctx"), None)
    mat = P(None, "dp", None)
    vec = P(None, "dp")
    return jax.shard_map(
        body,
        mesh=mesh,
        in_specs=(row, row) + (mat,) * 7 + (vec, vec, P()),
        out_specs=(row, row) + (mat,) * 7 + (vec, vec),
        check_vma=False,
    )
```

```python
import functools

import jax
import jax.numpy as jnp
from jax import lax
from jax.experimental import pallas as pl
from jax.experimental.pallas import tpu as pltpu
from jax.sharding import PartitionSpec as P

HEADS = 9
KV = 3
HD = 64
LAYERS = 2
D = 576
FF = 1536
NX = 4
NZ = 4
NY = 4
NORM_EPS = 1e-05
ROPE_BASE = 100000.0
NEG = -1e30
BIG = 1e30
MESH = pl.DeviceIdType.MESH
ALL = slice(None)
F32 = jnp.float32
BF = jnp.bfloat16
VMEM_LIMIT = 62 * 1024 * 1024
DIRS = (2, 1, -1)
SEMS = 352


def place():
    ctx = lax.axis_index("ctx")
    return lax.div(ctx, 8), lax.rem(lax.div(ctx, 2), 4), lax.rem(ctx, 2)


def ctx_of(x, z, c):
    return (x * NZ + z) * 2 + c


def turn(i, d):
    return lax.rem(i + (d + 4), 4)


def neighbour(axis, d):
    x, z, c = place()
    return ctx_of(turn(x, d), z, c) if axis == 0 else ctx_of(x, turn(z, d), c)


def other_core():
    x, z, c = place()
    return ctx_of(x, z, 1 - c)


def partners(y_too):
    devs = [{"ctx": neighbour(axis, d)} for axis in (0, 1) for d in (1, -1, 2)]
    devs.append({"ctx": other_core()})
    if y_too:
        y = lax.axis_index("dp")
        devs += [{"dp": turn(y, d)} for d in (1, -1, 2)]
    return devs


def signal_all(sem, devs):
    for dev in devs:
        pl.semaphore_signal(sem, inc=1, device_id=dev, device_id_type=MESH)


def greet():
    barrier = pltpu.get_barrier_semaphore()
    devs = partners(True)
    signal_all(barrier, devs)
    pl.semaphore_wait(barrier, len(devs))


class Wire:
    def __init__(self, send, recv, used=None):
        self.send, self.recv, self.open = send, recv, []
        self.used = [0] if used is None else used

    def branch(self):
        return Wire(self.send, self.recv, self.used)

    def take(self, n):
        self.used[0] += n
        assert self.used[0] <= SEMS
        return self.used[0] - n

    def desc(self, src, dst, k, dev):
        return pltpu.make_async_remote_copy(
            src_ref=src,
            dst_ref=dst,
            send_sem=self.send.at[k],
            recv_sem=self.recv.at[k],
            device_id=dev,
            device_id_type=MESH,
        )

    def go(self, src, dst, k, dev):
        copy = self.desc(src, dst, k, dev)
        copy.start()
        self.open.append(copy)

    def got(self, dst, k, dev):
        self.desc(dst, dst, k, dev).wait_recv()

    def close(self):
        for copy in self.open:
            copy.wait_send()
        self.open = []


def lockstep(gens):
    gens = list(gens)
    while gens:
        left = []
        for g in gens:
            try:
                next(g)
                left.append(g)
            except StopIteration:
                pass
        gens = left
        yield


def run_all(gens):
    for _ in lockstep(gens):
        pass


def tick(gen):
    try:
        next(gen)
    except StopIteration:
        pass


def halves(h):
    x, z, _ = place()
    return ((0, 1), (x, z)) if h == 0 else ((1, 0), (z, x))


def xz(h, first, second):
    return (first, second) if h == 0 else (second, first)


def on_plane(axis, d):
    return {"ctx": neighbour(axis, d)}


def on_y(d):
    return {"dp": turn(lax.axis_index("dp"), d)}


def gather_half(wire, h, view, share_view):
    c = place()[2]
    axes, (me1, me2) = halves(h)
    oth = {"ctx": other_core()}
    near, far, core = wire.take(3), wire.take(12), wire.take(4)
    firsts = [me1] + [turn(me1, -d) for d in DIRS]

    def along(n):
        block = view(firsts[n], me2)
        for j, d in enumerate(DIRS):
            wire.go(block, block, far + 3 * n + j, on_plane(axes[1], d))

    own = view(me1, me2)
    for j, d in enumerate(DIRS):
        wire.go(own, own, near + j, on_plane(axes[0], d))
    along(0)
    yield
    for j in (1, 2, 0):
        wire.got(view(firsts[j + 1], me2), near + j, oth)
        along(j + 1)
    mine = share_view(ALL, me2, c)
    wire.go(mine, mine, core + 3, oth)
    yield
    for j in (1, 2, 0):
        second = turn(me2, -DIRS[j])
        for n in range(4):
            wire.got(view(firsts[n], second), far + 3 * n + j, oth)
        part = share_view(ALL, second, c)
        wire.go(part, part, core + j, oth)
    yield
    for j in range(4):
        second = turn(me2, -DIRS[j]) if j < 3 else me2
        wire.got(share_view(ALL, second, 1 - c), core + j, oth)


def add_into(dst, *srcs):
    if len(dst.shape) > 2:

        def step(i, carry):
            add_into(dst.at[i], *[s.at[i] for s in srcs])
            return carry

        if len(dst.shape) == 3:
            for i in range(dst.shape[0]):
                step(i, 0)
        else:
            lax.fori_loop(0, dst.shape[0], step, 0)
        return
    total = dst[...].astype(F32)
    for s in srcs:
        total = total + s[...].astype(F32)
    dst[...] = total.astype(dst.dtype)


def core_swap(wire, me, src, dst):
    base = wire.take(4)
    order = DIRS + (0,)
    oth = {"ctx": other_core()}
    for k, d in enumerate(order):
        wire.go(src(turn(me, d)), dst(turn(me, d)), base + k, oth)

    def ready_of(total, term):
        def ready(d):
            f = turn(me, d)
            wire.got(dst(f), base + order.index(d), oth)
            add_into(total(f), term(f))

        return ready

    return ready_of


def ring_reduce(wire, me, dev, at, buf, ready):
    base = wire.take(3)
    for j, d in enumerate(DIRS):
        ready(d)
        wire.go(at(turn(me, d)), buf.at[j], base + j, dev(d))
    ready(0)
    yield
    for j, d in enumerate(DIRS):
        wire.got(buf.at[j], base + j, dev(d))
    add_into(at(me), buf.at[0], buf.at[1], buf.at[2])


def scatter_half(wire, h, view, bufs, ready):
    axes, pos = halves(h)
    yield from ring_reduce(
        wire, pos[0], lambda d: on_plane(axes[0], d), lambda i: view(i, ALL), bufs[0], ready
    )
    yield from ring_reduce(
        wire, pos[1], lambda d: on_plane(axes[1], d), lambda i: view(pos[0], i), bufs[1],
        lambda d: None,
    )


def lanes(shape):
    return lax.broadcasted_iota(jnp.int32, shape, len(shape) - 1)


def mm(a, b):
    return lax.dot_general(a, b, (((1,), (0,)), ((), ())), preferred_element_type=F32)


def mm_t(a, b):
    return lax.dot_general(a, b, (((1,), (1,)), ((), ())), preferred_element_type=F32)


def tmm(a, b):
    return lax.dot_general(a, b, (((0,), (0,)), ((), ())), preferred_element_type=F32)


def inv_rms(v):
    return lax.rsqrt(jnp.mean(v * v, axis=-1, keepdims=True) + NORM_EPS)


def norm_back(v, g, d):
    r = inv_rms(v)
    dv = r * g * d - v * (r * r * r * jnp.mean(g * d * v, axis=-1, keepdims=True))
    return dv, jnp.sum(d * v * r, axis=0, keepdims=True)


def rope(t, cos, ssin):
    first = lax.rem(lanes(t.shape), HD) < HD // 2
    turned = jnp.where(first, pltpu.roll(t, 96, 1), pltpu.roll(t, 32, 1))
    return t * cos + turned * ssin


def pair(t, half):
    lo, hi = t[:64], t[64:]
    first = lanes((64, 128)) < HD
    if half == 0:
        return jnp.where(first, lo, pltpu.roll(hi, HD, 1))
    return jnp.where(first, pltpu.roll(lo, HD, 1), hi)


def unpair(a, b):
    first = lanes((64, 128)) < HD
    lo = jnp.where(first, a, pltpu.roll(b, HD, 1))
    hi = jnp.where(first, pltpu.roll(a, HD, 1), b)
    return jnp.concatenate([lo, hi], axis=0)


def tile(v, i):
    return v[:, 128 * i : 128 * i + 128]


def doubled(p):
    first = lanes((192, 128)) < HD
    one = jnp.where(first, pltpu.roll(p, HD, 1), 0.0)
    zero = jnp.zeros((192, 128), F32)
    return jnp.concatenate(
        [jnp.concatenate([one, zero], axis=1), jnp.concatenate([zero, p], axis=1)], axis=0
    ).astype(BF)


def slot_row(scal, c, row_a, row_b):
    pick = jnp.full((1, 384), scal[2, c], F32) > 0.5
    own = jnp.full((1, 384), scal[3, c], F32)
    extra = jnp.where(lanes((1, 384)) >= 192, own, 0.0)
    return jnp.where(pick, row_a, row_b), extra


def rel(i):
    return turn(i - lax.axis_index("dp"), 4)


def w_mat(wv, kind, i):
    return jnp.concatenate([wv[kind, i, rel(j)] for j in range(NY)], axis=0)


def w_attn(wa, i):
    return jnp.concatenate([wa[i, rel(j)] for j in range(NY)], axis=0)


def w_down(wv, i):
    return wv[3, :, rel(i)].reshape(D, 384)


def load_mlp(src, wm, sems):
    return [pltpu.make_async_copy(src.at[k], wm.at[k], sems.at[k]) for k in (0, 1, 3)]


def multiple(v, n):
    return pl.multiple_of(v, n)


def kv_gather(wire, kv, k):
    c = place()[2]

    def gen(h):
        def view(first, second):
            xi, zi = xz(h, first, second)
            return kv.at[xi, zi, c, k, h]

        def share(first, second, core):
            xi, zi = xz(h, first, second)
            return kv.at[xi, zi, core, k, h]

        return gather_half(wire, h, view, share)

    return lockstep([gen(h) for h in (0, 1)])


def chunk_of(buf, ci, k, j):
    return buf[ci // 2, pl.ds(2 * (ci % 2), 2), :, k, j].reshape(256, 128)


def diag_keys(k):
    first = lanes((64, 128)) < HD
    zero = jnp.zeros((64, 128), k.dtype)
    both = jnp.concatenate([jnp.where(first, k, zero), jnp.where(first, zero, k)], axis=0)
    return both


def diag_bias():
    shape = (128, 384)
    key = lax.rem(lax.broadcasted_iota(jnp.int32, shape, 0), 64)
    q = lanes(shape)
    visible = (q >= 192) & (key <= lax.rem(q, 64))
    return jnp.where(visible, 0.0, NEG)


def row_split():
    c = place()[2]
    mine = pl.ds(multiple(64 * c, 16), 80)
    return mine, lambda core: pl.ds(multiple(80 * core, 16), 64)


def over_y(wire, src, view):
    mine, handed = row_split()
    c = place()[2]
    oth = {"ctx": other_core()}
    near, core = wire.take(3), wire.take(3)
    for j, d in enumerate(DIRS):
        wire.go(src(mine), view((4 - d) % 4, mine), near + j, on_y(d))
    yield
    for j in (1, 2, 0):
        k = (4 - DIRS[j]) % 4
        wire.got(view(k, mine), near + j, oth)
        part = view(k, handed(c))
        wire.go(part, part, core + j, oth)
    yield
    for j in range(3):
        wire.got(view((4 - DIRS[j]) % 4, handed(1 - c)), core + j, oth)


def attn_weights_gen(wire, win, wa, first, count):
    blocks = pl.ds(first, count)
    return over_y(
        wire, lambda rows: win.at[blocks, rows], lambda k, rows: wa.at[blocks, k, rows]
    )


def weights_around(wire, win, w):
    hi = pl.ds(128, 256)
    return over_y(
        wire, lambda rows: win.at[:, :, rows, hi], lambda k, rows: w.at[:, :, k, rows, hi]
    )


def weights_over(wire, win, w):
    x, z, _ = place()
    mine = row_split()[0]
    lo = pl.ds(0, 128)
    near = wire.take(3)
    for j, d in enumerate(DIRS):
        wire.go(win.at[x, z, mine, lo], w.at[x, z, (4 - d) % 4, mine, lo], near + j, on_y(d))
    yield
    for j, d in enumerate(DIRS):
        wire.got(w.at[x, z, (4 - d) % 4, mine, lo], near + j, on_y(d))

    def half(h):
        c = place()[2]
        rows = pl.ds(multiple((96 * c, 48 + 16 * c)[h], 16), 48 - 16 * h)

        def view(first, second):
            xi, zi = xz(h, first, second)
            return w.at[xi, zi, pl.ds(1, 3), rows, lo]

        def share(first, second, core):
            xi, zi = xz(h, first, second)
            begin = multiple((96 * core, 48 + 32 * core)[h], 16)
            return w.at[xi, zi, pl.ds(1, 3), pl.ds(begin, 48 - 32 * h), lo]

        return gather_half(wire, h, view, share)

    yield from lockstep([half(0), half(1)])


def gains_exchange(wire, gin, landing):
    base = wire.take(3)
    for j, d in enumerate(DIRS):
        wire.go(gin, landing.at[(4 - d) % 4], base + j, on_y(d))
    yield
    for j, d in enumerate(DIRS):
        wire.got(landing.at[(4 - d) % 4], base + j, on_y(d))


def gains_rows(gin, landing):
    total = jnp.zeros((16, 640), F32)
    landing[0] = gin[...]
    for j in range(NY):
        part = landing[rel(j)].astype(F32)
        part = jnp.concatenate([part, jnp.zeros((16, 384), F32)], axis=1)
        total = total + (pltpu.roll(part, 144 * j, 1) if j else part)
    return total


def forward_kernel(*refs):
    h_ref, win_a, win_b, win_m, gin = refs[:5]
    shared = refs[5:10]
    result = refs[10]
    saved0, saved1 = refs[11:17], refs[17:23]
    h1_ref, a_out, b_out, m_out, gains = refs[23:28]
    wa, wb, wm, s_scr, sd_scr, acc_scr, landing, send, recv, loc = refs[28:]
    own = [
        pltpu.make_async_copy(win_a, wa.at[:, 0], loc.at[0]),
        pltpu.make_async_copy(win_b, wb.at[:, :, 0], loc.at[1]),
        pltpu.make_async_copy(win_m, wm.at[:, :, 0], loc.at[2]),
    ]
    keep = [
        pltpu.make_async_copy(wa, a_out, loc.at[3]),
        pltpu.make_async_copy(wb, b_out, loc.at[4]),
        pltpu.make_async_copy(wm, m_out, loc.at[5]),
    ]
    for copy in own:
        copy.start()
    greet()
    wire = Wire(send, recv)
    early = attn_weights_gen(wire, win_a, wa, 0, 3)
    tick(early)
    slots = weights_over(wire, win_b, wb)
    tick(slots)
    last = attn_weights_gen(wire, win_a, wa, 3, 1)
    tick(last)
    run_all([early, gains_exchange(wire, gin, landing)])
    around = weights_around(wire, win_b, wb)
    tick(around)
    own[0].wait()
    gains[...] = gains_rows(gin, landing)
    slots1, around1 = weights_over(wire, win_m, wm), weights_around(wire, win_m, wm)
    work = (s_scr, sd_scr, acc_scr)

    def need_first():
        run_all([slots, around])
        own[1].wait()
        keep[0].start()
        keep[1].start()
        tick(slots1)
        tick(around1)

    def need_second():
        run_all([slots1, around1])
        own[2].wait()
        keep[2].start()

    h1 = forward_core(
        0, wire, lambda: tick(slots), lambda: run_all([last]), need_first, h_ref[...], gains, shared,
        saved0, wa, wb, work,
    )
    h1_ref[...] = h1
    h2 = forward_core(
        1, wire, lambda: tick(slots1), lambda: None, need_second, h1, gains, shared, saved1,
        wb.at[2], wm, work,
    )
    result[...] = h2.astype(BF)
    for copy in keep:
        copy.wait()
    wire.close()


def forward_core(layer, wire, later, need_out, need, h, gains, shared, saved, wa, wm, work):
    cos_ref, sin_ref, mask_ref, ind_ref, scal = shared
    mid_ref, attn_ref, qt_ref, kv, lse_ref, op_ref = saved
    s_scr, sd_scr, acc_scr = work
    x, z, c = place()
    x, z, c = place()
    n1 = (h * inv_rms(h) * gains[layer : layer + 1, :D]).astype(BF)
    cos, ssin = cos_ref[...], sin_ref[...]
    low = lanes((128, 128)) < HD
    kv_part = mm(n1, w_attn(wa, 0))
    t0, t1, t2 = [tile(kv_part, i) for i in range(3)]
    t0 = rope(t0, cos, ssin)
    t1 = jnp.where(low, rope(t1, cos, ssin), t1)
    k_pairs = [pair(t0, 0), pair(t0, 1), pair(t1, 0)]
    v_pairs = [pair(t1, 1), pair(t2, 0), pair(t2, 1)]
    spread = []
    for k in range(KV):
        kv[x, z, c, k, 0] = k_pairs[k].astype(BF)
        kv[x, z, c, k, 1] = v_pairs[k].astype(BF)
        spread.append(kv_gather(wire, kv, k))
        tick(spread[k])
    q_part = [mm(n1, w_attn(wa, i)) for i in (1, 2)]
    tiles = [rope(tile(q_part[i // 3], i % 3), cos, ssin) for i in range(5)]
    for k in range(KV):
        qp = jnp.concatenate(
            [pair(tiles[(3 * k + g) // 2], (3 * k + g) % 2) for g in range(3)], axis=0
        )
        qt_ref[k] = doubled(qp * 0.125)

    in_one = lanes((1, 384)) < 192
    bias = diag_bias()
    zero128 = jnp.zeros((128, 128), BF)
    runs = []
    for k in range(KV):
        keys = diag_keys(kv[x, z, c, k, 0])
        sd = mm_t(jnp.concatenate([zero128, keys], axis=1), qt_ref[k]) + bias
        sd_scr[k] = sd
        lo = jnp.max(sd[:64].reshape(8, 8, 384), axis=0)
        hi = jnp.max(sd[64:].reshape(8, 8, 384), axis=0)
        runs.append((jnp.full((8, 384), NEG, F32), lo, hi))
    dlane = lanes((128, 128))
    drow = lax.broadcasted_iota(jnp.int32, (128, 128), 0)
    dind = jnp.where(
        ((dlane == 65) & (drow < 64)) | ((dlane == 66) & (drow >= 64)), 1.0, 0.0
    ).astype(BF)
    first = lanes((256, 128)) < HD

    def scores(k):
        def step(pairi, carry):
            one, lo, hi = carry
            for ci in (2 * pairi, 2 * pairi + 1):
                keys = chunk_of(kv, ci, k, 0)
                s = mm_t(jnp.concatenate([keys, keys * mask_ref[ci]], axis=1), qt_ref[k])
                s_scr[ci] = s
                for i in range(4):
                    top = jnp.max(s[64 * i : 64 * i + 64].reshape(8, 8, 384), axis=0)
                    slot = 4 * ci + i
                    one = jnp.maximum(one, top)
                    lo = jnp.maximum(lo, top + scal[0, slot])
                    hi = jnp.maximum(hi, top + scal[1, slot])
            return one, lo, hi

        got = lax.fori_loop(0, 4, step, runs[k])
        one, lo, hi = [jnp.max(r, axis=0, keepdims=True) for r in got]
        top = jnp.where(in_one, one, hi)
        top = jnp.maximum(top, pltpu.roll(top, 192, 1))
        return jnp.where(in_one, top, lo), top

    def values(k, row_a, row_b):
        sd = sd_scr[k]
        p = jnp.concatenate([jnp.exp(sd[:64] - row_a), jnp.exp(sd[64:] - row_b)], axis=0)
        vals = jnp.concatenate([dind, diag_keys(kv[x, z, c, k, 1])], axis=1)
        acc_scr[k] = tmm(vals, p.astype(BF))

        def step(pairi, carry):
            total = acc_scr[k]
            for ci in (2 * pairi, 2 * pairi + 1):
                s = s_scr[ci]
                parts = []
                for i in range(4):
                    base, extra = slot_row(scal, 4 * ci + i, row_a, row_b)
                    parts.append(jnp.exp(s[64 * i : 64 * i + 64] - (base + extra)))
                p = jnp.concatenate(parts, axis=0).astype(BF)
                v = chunk_of(kv, ci, k, 1)
                vals = jnp.concatenate(
                    [jnp.where(first, v, ind_ref[ci]), v * mask_ref[ci]], axis=1
                )
                total = total + tmm(vals, p)
            acc_scr[k] = total
            return carry

        lax.fori_loop(0, 4, step, 0)

    for k in range(KV):
        tick(spread[k])
    later()
    row_a, row_b = [], []
    run_all([spread[0]])
    later()
    for k in range(KV):
        if k + 1 < KV:
            tick(spread[k + 1])
        a, b = scores(k)
        row_a.append(a)
        row_b.append(b)
        if k + 1 < KV:
            run_all([spread[k + 1]])
        values(k, a, b)

    pairs = []
    for k in range(KV):
        acc = acc_scr[k]
        rolled = pltpu.roll(acc, 192, 1)
        hi = acc[0:64] + rolled[192:256]
        lo = rolled[128:192]
        tot_hi = acc[64:65] + rolled[66:67]
        tot_lo = rolled[65:66]
        lse_hi = row_b[k] + jnp.log(jnp.where(in_one, tot_hi, 1.0))
        lse_hi = jnp.where(in_one, lse_hi, pltpu.roll(lse_hi, 192, 1))
        lse_lo = pltpu.roll(row_a[k], 192, 1) + jnp.log(jnp.where(in_one, tot_lo, 1.0))
        lse_ref[k, 0:1] = jnp.where(in_one, lse_hi, pltpu.roll(lse_lo, 192, 1))
        lse_ref[k, 1:2] = lse_hi
        lse_ref[k, 2:8] = jnp.zeros((6, 384), F32)
        out_t = jnp.concatenate(
            [lo / jnp.where(in_one, tot_lo, 1.0), hi / jnp.where(in_one, tot_hi, 1.0)], axis=0
        )
        p = jnp.transpose(out_t)[:192]
        op_ref[k] = p
        pairs += [p[64 * g : 64 * g + 64] for g in range(3)]
    pairs.append(jnp.zeros((64, 128), F32))
    attn = jnp.concatenate(
        [unpair(pairs[2 * t], pairs[2 * t + 1]) for t in range(5)], axis=1
    ).astype(BF)
    attn_ref[...] = attn
    a = attn[:, :D]
    need_out()
    proj = jnp.concatenate([mm(a, w_attn(wa, 2)), mm(a, w_attn(wa, 3))], axis=1)
    mid = h + pltpu.roll(proj, D, 1)[:, :D]
    mid_ref[...] = mid
    n2 = (mid * inv_rms(mid) * gains[2 + layer : 3 + layer, :D]).astype(BF)
    need()
    for i in range(4):
        gate = mm(n2, w_mat(wm, 0, i))
        up = mm(n2, w_mat(wm, 1, i))
        inner = (gate * jax.nn.sigmoid(gate) * up).astype(BF)
        mid = mid + mm_t(inner, w_down(wm, i))
    return mid


SAVED = (
    jax.ShapeDtypeStruct((128, D), F32),
    jax.ShapeDtypeStruct((128, 640), BF),
    jax.ShapeDtypeStruct((KV, 384, 256), BF),
    jax.ShapeDtypeStruct((NX, NZ, 2, KV, 2, 64, 128), BF),
    jax.ShapeDtypeStruct((KV, 8, 384), F32),
    jax.ShapeDtypeStruct((KV, 192, 128), F32),
)
FORWARD_SCRATCH = (
    ((4, 4, 144, 384), BF),
    ((4, 4, 4, 144, 384), BF),
    ((4, 4, 4, 144, 384), BF),
    ((8, 256, 384), F32),
    ((KV, 128, 384), F32),
    ((KV, 256, 384), F32),
    ((NY, 16, 256), BF),
)
GATHERED = jax.ShapeDtypeStruct((NX, NZ, NY, 144, 384), BF)
ATTN_GATHERED = jax.ShapeDtypeStruct((4, NY, 144, 384), BF)


def specs():
    return (
        pl.BlockSpec(memory_space=pltpu.VMEM),
        pl.BlockSpec(memory_space=pl.ANY),
        pl.BlockSpec(memory_space=pltpu.SMEM),
    )


def sems(*counts):
    return [pltpu.SemaphoreType.DMA((n,)) for n in counts]


def params(cid):
    return pltpu.CompilerParams(
        collective_id=cid, has_side_effects=True, vmem_limit_bytes=VMEM_LIMIT
    )


def forward(h, win_a, win_b, win_m, gin, cos, ssin, mask, ind, scal):
    vm, anyw, sm = specs()
    return pl.pallas_call(
        forward_kernel,
        out_shape=(jax.ShapeDtypeStruct((128, D), BF),) + SAVED * 2
        + (jax.ShapeDtypeStruct((128, D), F32), ATTN_GATHERED, GATHERED, GATHERED,
           jax.ShapeDtypeStruct((16, 640), F32)),
        in_specs=[vm, anyw, anyw, anyw, vm, vm, vm, vm, vm, sm],
        out_specs=(vm,) * 14 + (anyw, anyw, anyw, vm),
        scratch_shapes=[pltpu.VMEM(*v) for v in FORWARD_SCRATCH] + sems(SEMS, SEMS, 6),
        compiler_params=params(0),
        name="forward",
    )(h, win_a, win_b, win_m, gin, cos, ssin, mask, ind, scal)


def transposed(v, wide):
    wide[:, :D] = v.astype(F32)
    return jnp.transpose(wide[...])[:D].astype(BF)


def backward_kernel(*refs):
    g_ref, gains, cos_ref, sin_ref, mask_ref, scal = refs[:6]
    saved0, saved1 = refs[6:13], refs[13:20]
    a_any, b_any, m_any = refs[20:23]
    dh_ref, summed1, summed0, summed_a, gains_out = refs[23:28]
    rest = refs[28:]
    work, rest = rest[:N_WORK], rest[N_WORK:]
    wa0, wa1, kv, gm, ga0, ga1, gg0, gg1, steps, got = rest[:10]
    bufs1, bufs0 = rest[10 : 10 + N_REDUCE], rest[10 + N_REDUCE : 10 + 2 * N_REDUCE]
    late = rest[10 + 2 * N_REDUCE : -4]
    kv_free, send, recv, loc = rest[-4:]
    shared = (gains, cos_ref, sin_ref, mask_ref, scal)
    wm = work[0]
    attn_loads = [
        pltpu.make_async_copy(b_any.at[2], wa1, loc.at[4]),
        pltpu.make_async_copy(a_any, wa0, loc.at[5]),
    ]
    mlp1, mlp0 = load_mlp(m_any, wm, loc), load_mlp(b_any, wm, loc)
    kv1 = pltpu.make_async_copy(saved1[3], kv, loc.at[6])
    kv0 = pltpu.make_async_copy(saved0[3], kv, loc.at[6])
    for copy in mlp1 + [attn_loads[0], kv1, attn_loads[1]]:
        copy.start()
    greet()
    wire = Wire(send, recv)
    back = wire.branch()
    gm[2] = jnp.zeros((4, 4, 144, 384), BF)
    first = reduce_gen(back, gm, summed1, bufs1)
    second = reduce_gen(back, gm, summed0, bufs0)

    def after_mlp1():
        tick(first)
        for copy in mlp0:
            copy.start()

    def step1(point, i):
        if point == "head" and i == 0:
            tick(first)

    def ready1():
        attn_loads[0].wait()

    def after_heads1():
        kv0.start()

    for copy in mlp1:
        copy.wait()
    g1 = backward_core(
        1, wire, step1, after_mlp1, ready1, kv1.wait, lambda k: None, after_heads1,
        g_ref[...], saved1[:3] + saved1[4:], kv, shared, wa1, gm, ga1, gg1, work,
    )
    signal_all(kv_free, partners(False))
    wire.close()
    back.close()
    for copy in mlp0:
        copy.wait()

    def after_mlp0():
        gm[2] = ga1[...]
        tick(second)

    def step0(point, i):
        if (point == "mlp" and i == 3) or point == "attn" or (point == "head" and i < 2):
            tick(first)
        if point == "heads":
            run_all([first])
        if point == "head" and i == 0:
            tick(second)

    def before_reduce(k):
        if k == 0:
            pl.semaphore_wait(kv_free, len(partners(False)))

    g0 = backward_core(
        0, wire, step0, after_mlp0, attn_loads[1].wait, kv0.wait, before_reduce, lambda: None,
        g1, saved0[:3] + saved0[4:], kv, shared, wa0, gm, ga0, gg0, work,
    )
    dh_ref[...] = g0
    steps[0] = jnp.zeros((8, 640), F32)
    steps[0, 0:2, :D] = gg0[0:2]
    steps[0, 2:4, :D] = gg1[0:2]
    run_all([attn_reduce_gen(wire, ga0, summed_a, late), gains_gen(wire, steps, got), second])
    gains_out[...] = steps[4]
    wire.close()
    back.close()


def backward_core(
    layer, wire, step_batch, after_mlp, need_attn, need_kv, before_reduce, after_heads,
    g, saved, kv, shared, wa, gm, ga, gg_ref, work,
):
    h_ref, mid_ref, attn_ref, qt_ref, lse_ref, op_ref = saved
    gains, cos_ref, sin_ref, mask_ref, scal = shared
    wm, dot_scr, dq_scr, pbuf, rcore, kv_one, kv_two, wide = work
    x, z, c = place()
    wide[...] = jnp.zeros((128, 640), F32)
    mid = mid_ref[...]
    gain2 = gains[2 + layer : 3 + layer, :D]
    n2 = (mid * inv_rms(mid) * gain2).astype(BF)
    n2_t = transposed(n2, wide)
    branch = g.astype(BF)
    branch_t = transposed(branch, wide)
    d_n2 = jnp.zeros((128, D), F32)
    for i in range(4):
        gate_w, up_w, down_w = w_mat(wm, 0, i), w_mat(wm, 1, i), w_down(wm, i)
        gate = mm(n2, gate_w)
        up = mm(n2, up_w)
        sig = jax.nn.sigmoid(gate)
        act = gate * sig
        inner = (act * up).astype(BF)
        d_inner = mm(branch, down_w)
        d_gate = (d_inner * up * (sig + act * (1.0 - sig))).astype(BF)
        d_up = (d_inner * act).astype(BF)
        gm[0, i] = mm(n2_t, d_gate).astype(BF).reshape(4, 144, 384)
        gm[1, i] = mm(n2_t, d_up).astype(BF).reshape(4, 144, 384)
        gm[3, :, i] = mm(branch_t, inner).astype(BF).reshape(4, 144, 384)
        d_n2 = d_n2 + mm_t(d_gate, gate_w) + mm_t(d_up, up_w)
        step_batch("mlp", i)
    after_mlp()
    d_hn, gg2 = norm_back(mid, gain2, d_n2)
    d_mid = g + d_hn
    gg_ref[1:2] = gg2
    gg_ref[2:8] = jnp.zeros((6, D), F32)
    need_attn()
    wide[:, :D] = d_mid
    dm = jnp.concatenate([wide[...], jnp.zeros((128, 128), F32)], axis=1)
    dm = pltpu.roll(dm, 192, 1).astype(BF)
    d_attn = mm_t(dm[:, :384], w_attn(wa, 2)) + mm_t(dm[:, 384:], w_attn(wa, 3))
    wide[:, :D] = d_attn
    attn_t = jnp.transpose(attn_ref[...].astype(F32))[:D].astype(BF)
    g_out = mm(attn_t, dm)
    ga[3] = g_out[:, 384:].astype(BF).reshape(4, 144, 384)
    ga[2] = g_out[:, :384].astype(BF).reshape(4, 144, 384)
    da = wide[...].astype(BF).astype(F32)
    da_tiles = [tile(da, i) for i in range(5)]
    step_batch("attn", 0)

    in_one = lanes((1, 384)) < 192
    pick_lo = jnp.where(
        lanes((16, 128)) < HD,
        jnp.where(lax.broadcasted_iota(jnp.int32, (16, 128), 0) == 0, 1.0, 0.0),
        jnp.where(lax.broadcasted_iota(jnp.int32, (16, 128), 0) == 1, 1.0, 0.0),
    ).astype(BF)
    delta_a, delta_b = [], []
    for k in range(KV):
        dp = jnp.concatenate(
            [pair(da_tiles[(3 * k + q) // 2], (3 * k + q) % 2) for q in range(3)], axis=0
        )
        dot_scr[k] = doubled(dp)
        prod = dp * op_ref[k]
        prod = jnp.concatenate([prod, prod], axis=0)
        coarse = prod.astype(BF)
        fine = (prod - coarse.astype(F32)).astype(BF)
        rows = mm_t(pick_lo, coarse) + mm_t(pick_lo, fine)
        lo, hi = rows[0:1], rows[1:2]
        delta_a.append(jnp.where(in_one, hi, lo))
        delta_b.append(hi)

    def back(k, keys2, vals2, subs, deltas, bias):
        s = mm_t(keys2, qt_ref[k])
        if bias is not None:
            s = s + bias
        dp = mm_t(vals2, dot_scr[k])
        probs, d_s = [], []
        for i, (sub, delta) in enumerate(zip(subs, deltas)):
            p = jnp.exp(s[64 * i : 64 * i + 64] - sub)
            probs.append(p.astype(BF))
            d_s.append((p * (dp[64 * i : 64 * i + 64] - delta)).astype(BF))
        probs = jnp.concatenate(probs, axis=0)
        d_s = jnp.concatenate(d_s, axis=0)
        return mm(d_s, qt_ref[k]), mm(probs, dot_scr[k]), tmm(keys2, d_s)

    need_kv()
    bias = diag_bias()
    zero128 = jnp.zeros((128, 128), BF)
    first = lanes((64, 128)) < HD
    wide_first = lanes((256, 128)) < HD

    def head(k):
        own = []
        dk, dv, dq = back(
            k,
            jnp.concatenate([zero128, diag_keys(kv[x, z, c, k, 0])], axis=1),
            jnp.concatenate([zero128, diag_keys(kv[x, z, c, k, 1])], axis=1),
            [lse_ref[k, 0:1], lse_ref[k, 1:2]],
            [delta_a[k], delta_b[k]],
            bias,
        )
        for d in (dk, dv):
            own.append(jnp.where(first, d[:64, 128:], d[64:, 128:]))
        dq_scr[k] = dq

        def step(pairi, carry):
            total = dq_scr[k]
            for ci in (2 * pairi, 2 * pairi + 1):
                m = mask_ref[ci]
                keys, vals = chunk_of(kv, ci, k, 0), chunk_of(kv, ci, k, 1)
                subs, deltas = [], []
                for i in range(4):
                    base, extra = slot_row(scal, 4 * ci + i, lse_ref[k, 0:1], lse_ref[k, 1:2])
                    subs.append(base + extra)
                    deltas.append(slot_row(scal, 4 * ci + i, delta_a[k], delta_b[k])[0])
                dk, dv, dq = back(
                    k,
                    jnp.concatenate([keys, keys * m], axis=1),
                    jnp.concatenate([vals, vals * m], axis=1),
                    subs,
                    deltas,
                    None,
                )
                mf = m.astype(F32)
                for j, d in enumerate((dk, dv)):
                    both = jnp.where(wide_first, d[:, :128], 0.0) + mf * d[:, 128:]
                    both = both.astype(BF).reshape(2, 2, 64, 128)
                    pbuf[pairi, pl.ds(2 * (ci - 2 * pairi), 2), :, k, j] = both
                total = total + dq
            dq_scr[k] = total
            return carry

        lax.fori_loop(0, 4, step, 0)
        for j in (0, 1):
            part = pbuf.at[x, z, c, k, j]
            part[...] = (part[...].astype(F32) + own[j]).astype(BF)

    def kv_reduce(k, h):
        me = halves(h)[1][0]

        def view(f, s):
            xi, zi = xz(h, f, s)
            return pbuf.at[xi, zi, c, k, h]

        def src(f):
            xi, zi = xz(h, f, ALL)
            return pbuf.at[xi, zi, 1 - c, k, h]

        def dst(f):
            xi, zi = xz(h, f, ALL)
            return rcore.at[xi, zi, k, h]

        ready_of = core_swap(wire, me, src, dst)
        return scatter_half(
            wire, h, view, (kv_one.at[k, h], kv_two.at[k, h]),
            ready_of(lambda f: view(f, ALL), dst),
        )

    sums = []
    for k in range(KV):
        head(k)
        before_reduce(k)
        step_batch("head", k)
        sums.append(lockstep([kv_reduce(k, j) for j in (0, 1)]))
        for gen in sums:
            tick(gen)
    after_heads()
    step_batch("heads", 0)

    h = h_ref[...]
    gain1 = gains[layer : layer + 1, :D]
    n1 = (h * inv_rms(h) * gain1).astype(BF)
    n1_t = transposed(n1, wide)
    cos, ssin = cos_ref[...], -sin_ref[...]
    pairs = []
    for k in range(KV):
        dq = dq_scr[k]
        rolled = pltpu.roll(dq, 192, 1)
        out_t = jnp.concatenate([rolled[128:192], dq[0:64] + rolled[192:256]], axis=0)
        p = jnp.transpose(out_t)[:192]
        pairs += [p[64 * q : 64 * q + 64] for q in range(3)]
    pairs.append(jnp.zeros((64, 128), F32))
    q_tiles = [
        (rope(unpair(pairs[2 * t], pairs[2 * t + 1]), cos, ssin) * 0.125).astype(BF)
        for t in range(5)
    ]
    q_tiles.append(jnp.zeros((128, 128), BF))
    d_n1 = jnp.zeros((128, D), F32)

    def attn_block(i, d):
        grad = mm(n1_t, d)
        if i == 2:
            grad = grad + ga[2].reshape(D, 384).astype(F32)
        ga[i] = grad.astype(BF).reshape(4, 144, 384)
        return mm_t(d, w_attn(wa, i))

    for i in (1, 2):
        d_n1 = d_n1 + attn_block(i, jnp.concatenate(q_tiles[3 * i - 3 : 3 * i], axis=1))
    run_all(sums)
    step_batch("sums", 0)
    done = [[pbuf[x, z, c, k, j].astype(F32) for j in (0, 1)] for k in range(KV)]
    low = lanes((128, 128)) < HD
    t0 = rope(unpair(done[0][0], done[1][0]), cos, ssin)
    t1 = unpair(done[2][0], done[0][1])
    t1 = jnp.where(low, rope(t1, cos, ssin), t1)
    t2 = unpair(done[1][1], done[2][1])
    d_n1 = d_n1 + attn_block(0, jnp.concatenate([t0, t1, t2], axis=1).astype(BF))
    d_h, gg1 = norm_back(h, gain1, d_n1)
    gg_ref[0:1] = gg1
    return d_mid + d_h


BACKWARD_SCRATCH = (
    ((4, 4, 4, 144, 384), BF),
    ((KV, 384, 256), BF),
    ((KV, 256, 384), F32),
    ((NX, NZ, 2, KV, 2, 64, 128), BF),
    ((NX, NZ, KV, 2, 64, 128), BF),
    ((KV, 2, 3, 4, 64, 128), BF),
    ((KV, 2, 3, 64, 128), BF),
    ((128, 640), F32),
)
N_WORK = len(BACKWARD_SCRATCH)
SUMMED = jax.ShapeDtypeStruct((NX, NZ, 144, 384), BF)


def vmems(shapes):
    return [pltpu.VMEM(v, BF) for v in shapes]


def backward(g, gains, cos, ssin, mask, scal, saved0, saved1, w_a, w_b, w_m):
    vm, anyw, sm = specs()
    scratch = [pltpu.VMEM(*v) for v in BACKWARD_SCRATCH]
    scratch += vmems([(4, 4, 144, 384)] * 2)
    scratch += vmems([(NX, NZ, 2, KV, 2, 64, 128), (4, 4, 4, 144, 384)])
    scratch += vmems([(4, 4, 144, 384)] * 2)
    scratch += [pltpu.VMEM((8, D), F32)] * 2
    scratch += [pltpu.VMEM((5, 8, 640), F32), pltpu.VMEM((10, 8, 640), F32)]
    scratch += vmems(REDUCE_SHAPES * 2) + vmems(ATTN_REDUCE_SHAPES)
    scratch += [pltpu.SemaphoreType.REGULAR]
    kept = [vm, vm, vm, anyw, vm, vm, vm]
    order = lambda v: (v[0], v[1], v[2], v[4], v[3], v[5], v[6])
    return pl.pallas_call(
        backward_kernel,
        out_shape=(
            jax.ShapeDtypeStruct((128, D), F32), SUMMED, SUMMED,
            jax.ShapeDtypeStruct((4, 144, 384), BF), jax.ShapeDtypeStruct((8, 640), F32),
        ),
        in_specs=[vm] * 5 + [sm] + kept + kept + [anyw] * 3,
        out_specs=(vm,) * 5,
        scratch_shapes=scratch + sems(SEMS, SEMS, 9),
        compiler_params=params(1),
        name="backward",
    )(g, gains, cos, ssin, mask, scal, *order(saved0), *order(saved1), w_a, w_b, w_m)


REDUCE_SHAPES = (
    ((4, 4, 4, 80, 384),)
    + ((3, 4, 2, 80, 128), (3, 2, 80, 128)) * 2
    + ((3, 4, 4, 80, 256),)
    + ((3, 4, 48, 256), (3, 48, 256), (3, 4, 32, 256), (3, 32, 256))
    + ((3, 80, 128),)
)
N_REDUCE = len(REDUCE_SHAPES)


def reduce_gen(wire, src, out, bufs):
    total = bufs[0]
    plane, ring, late, from_y = (bufs[1:3], bufs[3:5]), bufs[5], (bufs[6:8], bufs[8:10]), bufs[10]
    x, z, c = place()
    y = lax.axis_index("dp")
    mine = row_split()[0]
    theirs = pl.ds(multiple(64 - 64 * c, 16), 80)
    hi, lo = pl.ds(128, 256), pl.ds(0, 128)

    def plane_first(h):
        ys = pl.ds(2 * h, 2)

        def view(f, s):
            xi, zi = xz(h, f, s)
            return total.at[xi, zi, ys, :, lo]

        def give(f, rows=theirs):
            xi, zi = xz(h, f, ALL)
            return src.at[xi, zi, ys, rows, lo]

        def dst(f):
            return view(f, ALL)

        ready_of = core_swap(wire, halves(h)[1][0], give, dst)
        return scatter_half(wire, h, view, plane[h], ready_of(dst, lambda f: give(f, mine)))

    def y_first():
        def at(i):
            return total.at[:, :, i, :, hi]

        ready_of = core_swap(wire, y, lambda i: src.at[:, :, i, theirs, hi], at)
        ready = ready_of(at, lambda i: src.at[:, :, i, mine, hi])

        def after():
            yield from ring_reduce(wire, y, on_y, at, ring, ready)

            def half(h):
                rows = pl.ds(48 * h, 48 - 16 * h)

                def view(f, s):
                    xi, zi = xz(h, f, s)
                    return total.at[xi, zi, y, rows, hi]

                return scatter_half(wire, h, view, late[h], lambda d: None)

            yield from lockstep([half(0), half(1)])

        return after()

    gens = [plane_first(0), plane_first(1), y_first()]
    yield

    def plane_then_y():
        yield from lockstep(gens[:2])
        yield from ring_reduce(
            wire, y, on_y, lambda i: total.at[x, z, i, :, lo], from_y, lambda d: None
        )

    yield from lockstep([plane_then_y(), gens[2]])
    out[x, z, mine] = total[x, z, y]

    def spread(h):
        rows = pl.ds(multiple((96 * c, 48 + 16 * c)[h], 16), 48 - 16 * h)

        def view(f, s):
            xi, zi = xz(h, f, s)
            return out.at[xi, zi, rows]

        def share(f, s, core):
            xi, zi = xz(h, f, s)
            begin = multiple((96 * core, 48 + 32 * core)[h], 16)
            return out.at[xi, zi, pl.ds(begin, 48 - 32 * h)]

        return gather_half(wire, h, view, share)

    yield from lockstep([spread(0), spread(1)])


ATTN_REDUCE_SHAPES = (
    ((4, 4, 80, 384),)
    + ((3, 4, 80, 384),)
    + ((3, 48, 384), (3, 48, 384), (3, 32, 384), (3, 32, 384), (48, 384), (32, 384))
)


def attn_reduce_gen(wire, src, out, bufs):
    total, ring = bufs[:2]
    one, two, held = (bufs[2], bufs[4]), (bufs[3], bufs[5]), bufs[6:8]
    c = place()[2]
    y = lax.axis_index("dp")
    oth = {"ctx": other_core()}
    mine = row_split()[0]
    theirs = pl.ds(multiple(64 - 64 * c, 16), 80)

    def at(i):
        return total.at[:, i]

    ready_of = core_swap(wire, y, lambda i: src.at[:, i, theirs], at)
    ready = ready_of(at, lambda i: src.at[:, i, mine])
    yield from ring_reduce(wire, y, on_y, at, ring, ready)

    def half(h):
        axes, (me, _) = halves(h)
        rows = pl.ds(48 * h, 48 - 16 * h)
        where = pl.ds(multiple(64 * c + 48 * h, 16), 48 - 16 * h)
        yield from ring_reduce(
            wire, me, lambda d: on_plane(axes[0], d), lambda i: total.at[i, y, rows], one[h],
            lambda d: None,
        )
        base = wire.take(3)
        for j, d in enumerate(DIRS):
            wire.go(total.at[me, y, rows], two[h].at[j], base + j, on_plane(axes[1], d))
        yield
        for j, d in enumerate(DIRS):
            wire.got(two[h].at[j], base + j, oth)
        sums = total[me, y, rows].astype(F32)
        for j in range(3):
            sums = sums + two[h][j].astype(F32)
        held[h][...] = sums.astype(BF)
        base = wire.take(3)
        out[me, where] = held[h][...]
        for j, d in enumerate(DIRS):
            wire.go(held[h], out.at[me, where], base + j, on_plane(axes[0], d))
        yield
        for j, d in enumerate(DIRS):
            wire.got(out.at[turn(me, -d), where], base + j, oth)

    yield from lockstep([half(0), half(1)])
    base = wire.take(1)

    def handed(core):
        return out.at[:, pl.ds(multiple(80 * core, 16), 64)]

    wire.go(handed(c), handed(c), base, oth)
    yield
    wire.got(handed(1 - c), base, oth)


def gains_gen(wire, steps, got):
    y = lax.axis_index("dp")
    base = wire.take(10)
    k = 0
    for stage in range(4):
        if stage < 2:
            there = [(d, {"ctx": neighbour(stage, d)}) for d in (1, -1, 2)]
        elif stage == 2:
            there = [(0, {"ctx": other_core()})]
        else:
            there = [(d, {"dp": turn(y, d)}) for d in (1, 2, 3)]
        for i, (d, dev) in enumerate(there):
            wire.go(steps.at[stage], got.at[k + i], base + k + i, dev)
        yield
        total = steps[stage]
        for i, (d, dev) in enumerate(there):
            wire.got(got.at[k + i], base + k + i, dev)
            total = total + got[k + i]
        steps[stage + 1] = total
        k += len(there)


def pack_weights(wq, wk, wv, wo, wg, wu, wd):
    def blocks(w):
        return w.reshape(LAYERS, 144, 4, 384).transpose(0, 2, 1, 3)

    attn = blocks(jnp.concatenate([wk, wv, wq, wo], axis=2))
    gate, up = blocks(wg), blocks(wu)
    down = wd.transpose(0, 2, 1).reshape(LAYERS, 4, 144, 384)
    return (
        attn[0],
        jnp.stack([gate[0], up[0], attn[1], down[0]]),
        jnp.stack([gate[1], up[1], up[1], down[1]]),
    )


def unpack_grads(early, late, attn0):
    attn = jnp.stack([attn0, late[2]]).astype(F32)

    def cols(v):
        return v.transpose(0, 2, 1, 3).reshape(LAYERS, 144, 1536)

    def both(i):
        return jnp.stack([late[i], early[i]]).astype(F32)

    attn = cols(attn)
    down = both(3).reshape(LAYERS, D, 384).transpose(0, 2, 1)
    return (
        attn[:, :, 384:960], attn[:, :, :192], attn[:, :, 192:384], attn[:, :, 960:],
        cols(both(0)), cols(both(1)), down,
    )


def body(
    tokens, out_grad, w_query, w_key, w_value, w_out, w_gate, w_up, w_down_, attn_gain, ffn_gain,
    block_pairs,
):
    me = lax.axis_index("ctx")
    y = lax.axis_index("dp")
    mine = block_pairs[me]
    offs = jnp.arange(64, dtype=jnp.int32)
    pos = jnp.concatenate([mine * 64 + offs, (63 - mine) * 64 + offs])
    freq = ROPE_BASE ** (-2.0 * jnp.arange(HD // 2, dtype=F32) / HD)
    ang = pos.astype(F32)[:, None] * freq[None, :]
    cos = jnp.cos(ang)
    sin = jnp.sin(ang)
    cos = jnp.concatenate([cos] * 4, axis=1)
    ssin = jnp.concatenate([-sin, sin, -sin, sin], axis=1)
    is_lo = block_pairs < mine
    is_hi = block_pairs > mine
    scal = jnp.stack([
        jnp.where(is_lo, 0.0, NEG), jnp.where(is_hi, 0.0, NEG),
        jnp.where(is_lo, 1.0, 0.0), jnp.where(is_lo | is_hi, 0.0, BIG),
    ]).astype(F32)
    lane = jnp.arange(128)[None, :]
    lo_col = jnp.repeat(is_lo, 64)[:, None]
    hi_col = jnp.repeat(is_hi, 64)[:, None]
    mask = jnp.where(lane < 64, lo_col, hi_col).astype(BF).reshape(8, 256, 128)
    ind = ((lane == 64) | ((lane == 65) & lo_col) | ((lane == 66) & hi_col)).astype(BF)
    ind = ind.reshape(8, 256, 128)

    win_a, win_b, win_m = pack_weights(w_query, w_key, w_value, w_out, w_gate, w_up, w_down_)
    gin = jnp.zeros((16, 256), BF)
    gin = gin.at[0:2, :144].set(attn_gain).at[2:4, :144].set(ffn_gain)
    h = tokens.astype(F32)
    common = (cos, ssin, mask, ind, scal)
    out = forward(h, win_a, win_b, win_m, gin, *common)
    result, saved0, saved1, h1, w_a, w_b, w_m, gains = (
        out[0], out[1:7], out[7:13], out[13], out[14], out[15], out[16], out[17]
    )
    g, early, late, attn0, gg = backward(
        out_grad.astype(F32), gains, cos, ssin, mask, scal, (h,) + saved0, (h1,) + saved1,
        w_a, w_b, w_m,
    )
    grads = unpack_grads(early, late, attn0)
    gg = lax.dynamic_slice(gg, (0, y * 144), (4, 144))
    return (result, g) + grads + (gg[0::2], gg[1::2])


def solution(mesh):
    row = P(("dp", "ctx"), None)
    mat = P(None, "dp", None)
    vec = P(None, "dp")
    return jax.shard_map(
        body,
        mesh=mesh,
        in_specs=(row, row) + (mat,) * 7 + (vec, vec, P()),
        out_specs=(row, row) + (mat,) * 7 + (vec, vec),
        check_vma=False,
    )
```
